32 devices in a mesh: dp: 8 (over y, x, core), seq: 4 (over z).
Axes of the slice: x: 2, y: 2, z: 4, core: 2. Of those that a mesh axis runs over, the one named last changes fastest.
Arguments:
- inputs: bfloat16 [8, 1024, 1024], P('dp', 'seq'), may hold values from -6 to 6
- noise_buckets: int32 [8], P('dp'), may hold values from 0 to 255
- first_gain: bfloat16 [2, 1024], P(None, 'dp'), may hold values from 0.5 to 1.5
- first_shift: bfloat16 [2, 1024], P(None, 'dp'), may hold values from -1 to 1
- attention_in: bfloat16 [2, 1024, 3072], P(None, 'dp'), may hold values from -0.1875 to 0.1875
- attention_out: bfloat16 [2, 1024, 1024], P(None, 'dp'), may hold values from -1.5 to 1.5
- attention_bias: bfloat16 [2, 1024], P(None, 'dp'), may hold values from -1 to 1
- second_gain: bfloat16 [2, 1024], P(None, 'dp'), may hold values from 0.5 to 1.5
- second_shift: bfloat16 [2, 1024], P(None, 'dp'), may hold values from -1 to 1
- expand_weight: bfloat16 [2, 1024, 4096], P(None, 'dp'), may hold values from -0.1875 to 0.1875
- expand_bias: bfloat16 [2, 4096], P(None, 'dp'), may hold values from -1 to 1
- reduce_weight: bfloat16 [2, 4096, 1024], P(None, 'dp'), may hold values from -0.09375 to 0.09375
- reduce_bias: bfloat16 [2, 1024], P(None, 'dp'), may hold values from -1 to 1
- time_table: bfloat16 [2, 256, 1024], P(None, 'dp'), may hold values from -1.5 to 1.5
- cotangent: bfloat16 [8, 1024, 1024], P('dp', 'seq'), may hold values from -6 to 6
Outputs:
- outputs: bfloat16 [8, 1024, 1024], P('dp', 'seq')
- input_grad: float32 [8, 1024, 1024], P('dp', 'seq')
- first_gain_grad: float32 [2, 1024], P(None, ('dp', 'seq'))
- first_shift_grad: float32 [2, 1024], P(None, ('dp', 'seq'))
- attention_in_grad: float32 [2, 1024, 3072], P(None, ('dp', 'seq'))
- attention_out_grad: float32 [2, 1024, 1024], P(None, ('dp', 'seq'))
- attention_bias_grad: float32 [2, 1024], P(None, ('dp', 'seq'))
- second_gain_grad: float32 [2, 1024], P(None, ('dp', 'seq'))
- second_shift_grad: float32 [2, 1024], P(None, ('dp', 'seq'))
- expand_weight_grad: float32 [2, 1024, 4096], P(None, ('dp', 'seq'))
- expand_bias_grad: float32 [2, 4096], P(None, ('dp', 'seq'))
- reduce_weight_grad: float32 [2, 4096, 1024], P(None, ('dp', 'seq'))
- reduce_bias_grad: float32 [2, 1024], P(None, ('dp', 'seq'))
- time_table_grad: float32 [2, 256, 1024], P(None, ('dp', 'seq'))
The draws below stay inside these ranges and needn't reach their ends.
All inputs are finite; a program needn't handle non-finite values.
Results may differ from the reference program's by a relative error of at most 0.024.
Values may be sent and summed in bfloat16 or wider, within the bound.
No kernel may reach another device: no remote copies, remote signals or barrier semaphores. Data moves between devices by JAX's collectives and lax.ppermute only.
A program may use at most 384 MiB of HBM per device.

```python
import math
import jax
import jax.numpy as jnp
from jax import lax

D = 1024
HEAD = 64
FF = 4096
BUCKETS = 256
LAYERS = 2
SEQ_LEN = 1024
SEQS = 8


def touch_ends(drawn, stream_key, smallest, top_value):
    shape = drawn.shape
    spot = [jax.random.randint(jax.random.fold_in(stream_key, axis), (), 0, shape[axis]) for axis in range(len(shape))]
    drawn = drawn.at[tuple(spot)].set(smallest)
    longest = shape.index(max(shape))
    spot[longest] = (spot[longest] + 1) % shape[longest]
    return drawn.at[tuple(spot)].set(top_value)


def levels(rng, extent, shards, smallest, largest):
    def one(position, shards_of):
        draws = jax.random.uniform(jax.random.fold_in(jax.random.fold_in(rng, 6), position), (shards_of,), jnp.float32, smallest / len(shards), largest / len(shards))
        return jnp.repeat(jnp.exp(draws), extent[position] // shards_of).reshape((-1,) + (1,) * (len(extent) - position - 1))

    factor_of = one(*shards[0])
    for cut in shards[1:]:
        factor_of = factor_of * one(*cut)
    return factor_of


def centred(rng, shape, scale, most, cuts=(), kind=jnp.bfloat16):
    values = scale * jax.random.normal(rng, shape, jnp.float32)
    if cuts:
        values = values * levels(rng, shape, cuts, -0.22, 0.18)
    return jnp.clip(values, -most, most).astype(kind)


def setup_inputs(seed: int = 0) -> dict:
    keys = jax.random.split(jax.random.key(seed), 16)
    return {
        "inputs": centred(keys[0], (SEQS, SEQ_LEN, D), 1.0, 6.0, ((0, 8), (1, 4))),
        "noise_buckets": touch_ends(jax.random.randint(keys[1], (SEQS,), 0, BUCKETS), jax.random.fold_in(keys[1], 1), 0, BUCKETS - 1).astype(jnp.int32),
        "first_gain": jnp.clip(1.0 + 0.1 * jax.random.normal(keys[2], (LAYERS, D), jnp.float32), 0.5, 1.5).astype(jnp.bfloat16),
        "first_shift": centred(keys[3], (LAYERS, D), 0.2, 1.0, ((1, 8),)),
        "attention_in": centred(keys[4], (LAYERS, D, 3 * D), D ** -0.5, 0.1875, ((1, 8),)),
        "attention_out": centred(keys[5], (LAYERS, D, D), (D * 16 // SEQ_LEN) ** -0.5, 1.5, ((1, 8),)),
        "attention_bias": centred(keys[6], (LAYERS, D), 0.2, 1.0, ((1, 8),)),
        "second_gain": jnp.clip(1.0 + 0.1 * jax.random.normal(keys[7], (LAYERS, D), jnp.float32), 0.5, 1.5).astype(jnp.bfloat16),
        "second_shift": centred(keys[8], (LAYERS, D), 0.2, 1.0, ((1, 8),)),
        "expand_weight": centred(keys[9], (LAYERS, D, FF), D ** -0.5, 0.1875, ((1, 8),)),
        "expand_bias": centred(keys[10], (LAYERS, FF), 0.2, 1.0, ((1, 8),)),
        "reduce_weight": centred(keys[11], (LAYERS, FF, D), FF ** -0.5, 0.09375, ((1, 8),)),
        "reduce_bias": centred(keys[12], (LAYERS, D), 0.2, 1.0, ((1, 8),)),
        "time_table": centred(keys[13], (LAYERS, BUCKETS, D), 0.3, 1.5, ((1, 8),)),
        "cotangent": centred(keys[14], (SEQS, SEQ_LEN, D), 1.0, 6.0, ((0, 8), (1, 4))),
    }


@jax.custom_vjp
def low(v):
    return lax.optimization_barrier(v.astype(jnp.bfloat16)).astype(jnp.float32)

@jax.custom_vjp
def low_back(v):
    return v

def low_keep(v):
    return (low(v), None)

def low_pass(kept, grad):
    return (grad,)

def back_keep(v):
    return (v, None)

def back_low(kept, grad):
    return (low(grad),)
low.defvjp(low_keep, low_pass)
low_back.defvjp(back_keep, back_low)
highest = lax.Precision.HIGHEST
epsilon = 1e-05

def modulated_norm(activations, norm_gain, norm_shift, scaling):
    center = activations - lax.optimization_barrier(jnp.mean(activations, axis=-1, keepdims=True))
    spread = lax.optimization_barrier(jnp.mean(center * center, axis=-1, keepdims=True))
    return (center * lax.rsqrt(spread + epsilon) * norm_gain + norm_shift) * (1.0 + scaling)

def block_forward(stream, weights, selector):
    first_gain, first_shift, attention_in, attention_out, attention_bias, second_gain, second_shift, expand_weight, expand_bias, reduce_weight, reduce_bias, time_table = weights
    length = stream.shape[0]
    head_count = D // HEAD
    scaling = jnp.dot(selector, time_table, precision=highest)
    normed = low(modulated_norm(stream, first_gain, first_shift, scaling))
    project = low(low_back(jnp.dot(normed, attention_in, precision=highest)))
    queries = project[:, :D].reshape(length, head_count, HEAD)
    key_rows = project[:, D:2 * D].reshape(length, head_count, HEAD)
    values = project[:, 2 * D:].reshape(length, head_count, HEAD)
    scores = low_back(jnp.einsum('qhd,khd->hqk', queries, key_rows, precision=highest) * (1.0 / math.sqrt(HEAD)))
    shifted = jnp.exp(scores - lax.optimization_barrier(jnp.max(scores, axis=-1, keepdims=True)))
    attention = low(shifted / lax.optimization_barrier(jnp.sum(shifted, axis=-1, keepdims=True)))
    mixture = jnp.einsum('hqk,khd->qhd', attention, values, precision=highest).reshape(length, D)
    mixture = low(low_back(mixture))
    middle = stream + low_back(jnp.dot(mixture, attention_out, precision=highest)) + attention_bias
    second = low(modulated_norm(middle, second_gain, second_shift, scaling))
    hidden = low_back(jnp.dot(second, expand_weight, precision=highest)) + expand_bias
    active = low(jax.nn.gelu(hidden))
    return middle + low_back(jnp.dot(active, reduce_weight, precision=highest)) + reduce_bias

def reference(inputs, noise_buckets, first_gain, first_shift, attention_in, attention_out, attention_bias, second_gain, second_shift, expand_weight, expand_bias, reduce_weight, reduce_bias, time_table, cotangent):
    params = tuple((argument.astype(jnp.float32) for argument in (first_gain, first_shift, attention_in, attention_out, attention_bias, second_gain, second_shift, expand_weight, expand_bias, reduce_weight, reduce_bias, time_table)))

    def forward(stream, weights, selector):
        for layer_index in range(LAYERS):
            stream = block_forward(stream, tuple((tensor[layer_index] for tensor in weights)), selector)
        return stream

    def per_sequence(totals, sequence_item):
        sequence, bucket, incoming = sequence_item
        selector = (jnp.arange(BUCKETS, dtype=jnp.int32) == bucket).astype(jnp.float32)
        output, pullback = jax.vjp(lambda stream, weights: forward(stream, weights, selector), sequence.astype(jnp.float32), params)
        stream_grad, weight_grads = pullback(incoming.astype(jnp.float32))
        totals = jax.tree.map(lambda summed, addend: summed + addend, totals, weight_grads)
        return (totals, (output.astype(jnp.bfloat16), stream_grad))
    starting = tuple((jnp.zeros_like(tensor) for tensor in params))
    totals, (outputs, input_grad) = lax.scan(per_sequence, starting, (inputs, noise_buckets, cotangent))
    return (outputs, input_grad, totals[0], totals[1], totals[2], totals[3], totals[4], totals[5], totals[6], totals[7], totals[8], totals[9], totals[10], totals[11])
```

```python
import functools
import math

import jax
import jax.numpy as jnp
from jax import lax
from jax.experimental import pallas as pl
from jax.experimental.pallas import tpu as pltpu
from jax.sharding import PartitionSpec as P

HEAD = 64
BUCKETS = 256
SMALL = 8
WIDE = 1024

epsilon = 1e-05
bf16 = jnp.bfloat16
f32 = jnp.float32


def modulated_norm(activations, norm_gain, norm_shift, scaling):
    center = activations - jnp.mean(activations, axis=-1, keepdims=True)
    spread = jnp.mean(center * center, axis=-1, keepdims=True)
    return (center * lax.rsqrt(spread + epsilon) * norm_gain + norm_shift) * (1.0 + scaling)


def swap(array, bit):
    count = lax.axis_size("dp")
    return lax.ppermute(array, "dp", [(i, i ^ bit) for i in range(count)])


def swap_seq(array, bit):
    count = lax.axis_size("seq")
    return lax.ppermute(array, "seq", [(i, i ^ bit) for i in range(count)])


def after(array, *earlier):
    return lax.optimization_barrier((array,) + earlier)[0]


def layout_moves(back):
    moves = []
    for index in range(lax.axis_size("dp")):
        core, pair = index % 2, index - index % 2
        for plane in range(4):
            source = index * 4 + plane
            target = (pair + plane % 2) * 4 + 2 * core + plane // 2
            moves.append((target, source) if back else (source, target))
    return moves


def gather_rows(shard, route):
    if lax.axis_size("dp") != SMALL:
        return lax.all_gather(shard, "dp", axis=0, tiled=True)
    along_x = swap(shard, 2)
    along_y = swap(shard, 4)
    across = swap(along_x, 4) if route == 0 else swap(along_y, 2)
    mine = [shard, along_x, along_y, across]
    parts = []
    for part in mine:
        parts += [part, swap(part, 1)]
    return parts


def order_of(parts):
    me = lax.axis_index("dp")
    return [me ^ bit for bit in range(parts)]


def scatter_dense(left, right, orders):
    count, planes = lax.axis_size("dp"), lax.axis_size("seq")
    rows, columns = left.shape[1], right.shape[1]
    if count != SMALL:
        whole = jnp.einsum("tr,tc->rc", left, right, preferred_element_type=f32)
        return lax.psum_scatter(whole, ("dp", "seq"), scatter_dimension=0, tiled=True)
    me, plane = lax.axis_index("dp"), lax.axis_index("seq")
    block = rows // count
    width = columns // len(orders)

    def pick(masks):
        return jnp.concatenate(
            [lax.dynamic_slice_in_dim(left, (me ^ mask) * block, block, 1) for mask in masks], axis=1
        )

    def product(a, b):
        return jnp.einsum("tr,tc->rc", a, b, preferred_element_type=f32)

    pieces = []
    for position, (first, second) in enumerate(orders):
        part = right[:, position * width : (position + 1) * width]
        masks = [first | second, first, second, 0]
        arrived = swap(product(pick([mask | 1 for mask in masks]), part).astype(bf16), 1)
        half = 2 * block
        leaving = (product(pick(masks[:2]), part) + arrived[:half].astype(f32)).astype(bf16)
        staying = (product(pick(masks[2:]), part) + arrived[half:].astype(f32)).astype(bf16)
        arrived = swap(leaving, first)
        leaving = (staying[:block].astype(f32) + arrived[:block].astype(f32)).astype(bf16)
        staying = (staying[block:].astype(f32) + arrived[block:].astype(f32)).astype(bf16)
        arrived = swap(leaving, second)
        pieces.append((staying, arrived))
    total = jnp.concatenate([(a.astype(f32) + b.astype(f32)).astype(bf16) for a, b in pieces], axis=1)
    return scatter_planes(total, plane, planes)


def scatter_planes(total, plane, planes):
    rows, columns = total.shape
    low, high = plane & 1, plane >> 1
    cut = total.reshape(2, 2, rows // planes, columns)
    arrived = swap_seq(lax.dynamic_index_in_dim(cut, 1 - low, 1, keepdims=False), 1)
    kept = lax.dynamic_index_in_dim(cut, low, 1, keepdims=False)
    joined = kept.astype(f32) + arrived.astype(f32)
    arrived = swap_seq(lax.dynamic_index_in_dim(joined, 1 - high, 0, keepdims=False).astype(bf16), 2)
    return lax.dynamic_index_in_dim(joined, high, 0, keepdims=False) + arrived.astype(f32)


def scatter_small(array):
    count, planes = lax.axis_size("dp"), lax.axis_size("seq")
    if count != SMALL:
        return lax.psum_scatter(array, ("dp", "seq"), scatter_dimension=0, tiled=True)[0]
    me, plane = lax.axis_index("dp"), lax.axis_index("seq")
    columns = array.shape[1]
    shape = [count, planes]
    current = array.reshape(shape[0], shape[1], columns)
    for axis, index, send in ((0, me, swap), (1, plane, swap_seq)):
        bit = 1
        while current.shape[axis] > 1:
            pairs = current.shape[axis] // 2
            view = jnp.moveaxis(current, axis, 0).reshape(pairs, 2, -1, columns)
            mine = (index // bit) % 2
            leaving = lax.dynamic_index_in_dim(view, 1 - mine, 1, keepdims=False)
            staying = lax.dynamic_index_in_dim(view, mine, 1, keepdims=False)
            current = jnp.moveaxis((staying + send(leaving, bit)).reshape(pairs, -1, columns), 0, axis)
            bit *= 2
    return current.reshape(columns)


def gather_small(array, axes):
    if lax.axis_size("dp") != SMALL:
        stacked = lax.all_gather(array, axes, axis=0, tiled=False)
        stacked = stacked.reshape((-1,) + array.shape)
        places = jnp.arange(stacked.shape[0])
        if "seq" in axes:
            planes = lax.axis_size("seq")
            return stacked, places // planes, places % planes
        return stacked, places, None
    current = array[None]
    me = lax.axis_index("dp")
    for bit in (1, 2, 4):
        current = jnp.concatenate([current, swap(current, bit)], axis=0)
    sources = me ^ jnp.arange(SMALL)
    if "seq" not in axes:
        return current, sources, None
    plane = lax.axis_index("seq")
    for bit in (1, 2):
        current = jnp.concatenate([current, swap_seq(current, bit)], axis=0)
    places = jnp.arange(SMALL * 4)
    return current, me ^ (places % SMALL), plane ^ (places // SMALL)


VMEM_LIMIT = 56 * 1024 * 1024


def forward_kernel(count, depth, place, a_ref, *refs):
    weights, out, ordered = refs[:count], refs[count], refs[count + 1]

    @pl.when(pl.program_id(0) == 0)
    def _():
        for part in range(count):
            start = pl.multiple_of((place[0] ^ part) * depth, 128)
            ordered[:, part * depth : (part + 1) * depth] = a_ref[:, pl.ds(start, depth)]

    whole = jnp.concatenate([weight[...] for weight in weights], axis=0)
    out[...] = jnp.dot(ordered[...], whole, preferred_element_type=f32).astype(out.dtype)


def times(a, parts, out_type):
    if not isinstance(parts, list):
        return jnp.dot(a, parts, preferred_element_type=f32).astype(out_type)
    tokens, inner = a.shape
    depth, columns = parts[0].shape
    tile = min(512, columns)
    count = len(parts)
    place = lax.axis_index("dp").astype(jnp.int32).reshape(1)
    return pl.pallas_call(
        functools.partial(forward_kernel, count, depth),
        out_shape=jax.ShapeDtypeStruct((tokens, columns), out_type),
        grid_spec=pltpu.PrefetchScalarGridSpec(
            num_scalar_prefetch=1,
            grid=(columns // tile,),
            in_specs=[pl.BlockSpec((tokens, inner), lambda i, s: (0, 0))]
            + [pl.BlockSpec((depth, tile), lambda i, s: (0, i))] * count,
            out_specs=pl.BlockSpec((tokens, tile), lambda i, s: (0, i)),
            scratch_shapes=[pltpu.VMEM((tokens, inner), bf16)],
        ),
        compiler_params=pltpu.CompilerParams(vmem_limit_bytes=VMEM_LIMIT),
        cost_estimate=pl.CostEstimate(
            flops=2 * tokens * inner * columns,
            bytes_accessed=2 * inner * columns + 6 * tokens * (inner + columns),
            transcendentals=0,
        ),
    )(place, a, *parts)


def backward_kernel(count, depth, rows, place, a_ref, *refs):
    weights, out, total = refs[:count], refs[count], refs[count + 1]
    step, steps = pl.program_id(0), pl.num_programs(0)
    whole = jnp.concatenate([weight[...] for weight in weights], axis=0)
    product = lax.dot_general(
        a_ref[...], whole, (((1,), (1,)), ((), ())), preferred_element_type=f32
    )
    if rows == depth:

        @pl.when(step == 0)
        def _():
            total[...] = product

        @pl.when(step > 0)
        def _():
            total[...] += product

        @pl.when(step == steps - 1)
        def _():
            for part in range(count):
                start = pl.multiple_of((place[0] ^ part) * depth, 128)
                out[:, pl.ds(start, depth)] = total[:, part * depth : (part + 1) * depth].astype(
                    out.dtype
                )

    else:
        for part in range(count):
            start = pl.multiple_of((place[0] ^ part) * depth + step * rows, 128)
            out[:, pl.ds(start, rows)] = product[:, part * rows : (part + 1) * rows].astype(out.dtype)


def times_transposed(a, parts, out_type):
    if not isinstance(parts, list):
        return lax.dot_general(
            a, parts, (((1,), (1,)), ((), ())), preferred_element_type=f32
        ).astype(out_type)
    tokens, inner = a.shape
    depth = parts[0].shape[0]
    count = len(parts)
    place = lax.axis_index("dp").astype(jnp.int32).reshape(1)
    if depth > 128:
        rows, tile = 128, inner
        grid = depth // rows
        a_spec = pl.BlockSpec((tokens, inner), lambda i, s: (0, 0))
        w_spec = pl.BlockSpec((rows, inner), lambda i, s: (i, 0))
    else:
        rows, tile = depth, min(512, inner)
        grid = inner // tile
        a_spec = pl.BlockSpec((tokens, tile), lambda i, s: (0, i))
        w_spec = pl.BlockSpec((rows, tile), lambda i, s: (0, i))
    return pl.pallas_call(
        functools.partial(backward_kernel, count, depth, rows),
        out_shape=jax.ShapeDtypeStruct((tokens, count * depth), out_type),
        grid_spec=pltpu.PrefetchScalarGridSpec(
            num_scalar_prefetch=1,
            grid=(grid,),
            in_specs=[a_spec] + [w_spec] * count,
            out_specs=pl.BlockSpec((tokens, count * depth), lambda i, s: (0, 0)),
            scratch_shapes=[pltpu.VMEM((tokens, count * rows), f32)],
        ),
        compiler_params=pltpu.CompilerParams(vmem_limit_bytes=VMEM_LIMIT),
        cost_estimate=pl.CostEstimate(
            flops=2 * tokens * inner * count * depth,
            bytes_accessed=2 * inner * count * depth + 6 * tokens * (inner + count * depth),
            transcendentals=0,
        ),
    )(place, a, *parts)


def spread_keys(own):
    far = swap_seq(own, 1)
    return [own, swap(own, 1), far, swap(far, 1)]


def heads_of(rows):
    return rows.reshape(rows.shape[0], rows.shape[1] // HEAD, HEAD)


def attend(queries, chunks):
    model_width = queries.shape[1]
    whole = jnp.concatenate(chunks, axis=0)
    key_heads, value_heads = heads_of(whole[:, :model_width]), heads_of(whole[:, model_width:])
    scores = jnp.einsum("qhd,khd->hqk", heads_of(queries), key_heads, preferred_element_type=f32)
    scores = scores * (1.0 / math.sqrt(HEAD))
    exponent = jnp.exp(scores - jnp.max(scores, axis=-1, keepdims=True))
    probs = exponent / jnp.sum(exponent, axis=-1, keepdims=True)
    probs_low = probs.astype(bf16)
    mixture = jnp.einsum("hqk,khd->qhd", probs_low, value_heads, preferred_element_type=f32)
    return mixture.reshape(queries.shape).astype(bf16), (probs, probs_low)


def attend_back(queries, chunks, kept, mixture, mixture_grad):
    probs, probs_low = kept
    model_width = queries.shape[1]
    factor = 1.0 / math.sqrt(HEAD)
    whole = jnp.concatenate(chunks, axis=0)
    key_heads, value_heads = heads_of(whole[:, :model_width]), heads_of(whole[:, model_width:])
    grad_heads = heads_of(mixture_grad)
    prob_grad = jnp.einsum("qhd,khd->hqk", grad_heads, value_heads, preferred_element_type=f32)
    along = jnp.sum(probs * prob_grad, axis=-1, keepdims=True)
    score_grad = (probs * (prob_grad - along)).astype(bf16)
    query_grad = jnp.einsum("hqk,khd->qhd", score_grad, key_heads, preferred_element_type=f32)
    query_grad = (query_grad * factor).astype(bf16).reshape(queries.shape)
    key_part = jnp.einsum("hqk,qhd->khd", score_grad, heads_of(queries), preferred_element_type=f32)
    value_part = jnp.einsum("hqk,qhd->khd", probs_low, grad_heads, preferred_element_type=f32)
    parts = jnp.concatenate(
        [
            (key_part * factor).reshape(whole.shape[0], model_width),
            value_part.reshape(whole.shape[0], model_width),
        ],
        axis=1,
    ).astype(bf16)
    return query_grad, parts


def join_key_grads(parts):
    local = parts.shape[0] // 4
    cut = [parts[i * local : (i + 1) * local] for i in range(4)]
    far = cut[2].astype(f32) + swap(cut[3], 1).astype(f32)
    far = swap_seq(far.astype(bf16), 1)
    near = cut[0].astype(f32) + swap(cut[1], 1).astype(f32)
    return (near + far.astype(f32)).astype(bf16)


def layer_forward(stream, weights, vectors):
    w_query, w_keys, w_out, w_expand, w_reduce = weights
    first_gain, first_shift, attention_bias, second_gain, second_shift, reduce_bias, expand_bias, scaling = vectors
    normed = modulated_norm(stream, first_gain, first_shift, scaling).astype(bf16)
    chunks = spread_keys(times(normed, w_keys, bf16))
    queries = times(normed, w_query, bf16)
    mixture, kept = attend(queries, chunks)
    middle = stream + (times(mixture, w_out, f32) + attention_bias)
    second = modulated_norm(middle, second_gain, second_shift, scaling).astype(bf16)
    hidden = times(second, w_expand, f32) + expand_bias
    active = jax.nn.gelu(hidden).astype(bf16)
    result = middle + (times(active, w_reduce, f32) + reduce_bias)
    return result, (stream, normed, queries, chunks, kept, mixture, middle, second, hidden, active)


def layer_backward(saved, weights, vectors, grad_out):
    w_query, w_keys, w_out, w_expand, w_reduce = weights
    first_gain, first_shift, attention_bias, second_gain, second_shift, reduce_bias, expand_bias, scaling = vectors
    stream, normed, queries, chunks, kept, mixture, middle, second, hidden, active = saved
    both = ((2, 4), (4, 2))
    grad_low = grad_out.astype(bf16)
    reduce_bias_grad = jnp.sum(grad_out, axis=0)
    reduce_weight_grad = scatter_dense(active, grad_low, both)
    active_grad = times_transposed(grad_low, w_reduce, f32)
    hidden_grad = jax.vjp(jax.nn.gelu, hidden)[1](active_grad)[0]
    expand_bias_grad = jnp.sum(hidden_grad, axis=0)
    hidden_low = hidden_grad.astype(bf16)
    second_grad = times_transposed(hidden_low, w_expand, f32)
    expand_weight_grad = scatter_dense(second, hidden_low, both)
    _, second_back = jax.vjp(modulated_norm, middle, second_gain, second_shift, scaling)
    middle_part, second_gain_grad, second_shift_grad, second_scaling_grad = second_back(second_grad)
    middle_grad = grad_out + middle_part
    attention_bias_grad = jnp.sum(middle_grad, axis=0)
    middle_low = middle_grad.astype(bf16)
    mixture_grad = times_transposed(middle_low, w_out, bf16)
    attention_out_grad = scatter_dense(mixture, middle_low, both)
    query_grad, parts = attend_back(queries, chunks, kept, mixture, mixture_grad)
    key_grad = join_key_grads(parts)
    normed_grad = times_transposed(query_grad, w_query, f32) + times_transposed(key_grad, w_keys, f32)
    project_grad = jnp.concatenate([query_grad, key_grad], axis=1)
    attention_in_grad = scatter_dense(normed, project_grad, both)
    _, first_back = jax.vjp(modulated_norm, stream, first_gain, first_shift, scaling)
    stream_part, first_gain_grad, first_shift_grad, first_scaling_grad = first_back(normed_grad)
    stream_grad = middle_grad + stream_part
    small = (
        first_gain_grad,
        first_shift_grad,
        attention_bias_grad,
        second_gain_grad,
        second_shift_grad,
        reduce_bias_grad,
        expand_bias_grad,
    )
    dense = (attention_in_grad, attention_out_grad, expand_weight_grad, reduce_weight_grad)
    return stream_grad, dense, small, (first_scaling_grad + second_scaling_grad)[0]


def pack_small(vectors, rows):
    flat = jnp.concatenate([vector.reshape(-1) for vector in vectors])
    length = -(-flat.shape[0] // WIDE) * WIDE
    return jnp.pad(flat, (0, length - flat.shape[0])).reshape(-1, WIDE)


def on_device(
    inputs,
    noise_buckets,
    first_gain,
    first_shift,
    attention_in,
    attention_out,
    attention_bias,
    second_gain,
    second_shift,
    expand_weight,
    expand_bias,
    reduce_weight,
    reduce_bias,
    time_table,
    cotangent,
):
    layers = first_gain.shape[0]
    count, planes = lax.axis_size("dp"), lax.axis_size("seq")
    me, plane = lax.axis_index("dp"), lax.axis_index("seq")
    model_width = inputs.shape[-1]
    table_rows = time_table.shape[1]

    stream = lax.ppermute(inputs[0], ("dp", "seq"), layout_moves(False)).astype(f32)

    sequence = (me // 2) * 2 + plane // 2
    packs = []
    for layer in range(layers):
        rows = [
            time_table[layer],
            pack_small(
                [
                    member[layer]
                    for member in (
                        first_gain,
                        first_shift,
                        attention_bias,
                        second_gain,
                        second_shift,
                        reduce_bias,
                        expand_bias,
                    )
                ],
                WIDE,
            ),
            jnp.broadcast_to(noise_buckets.astype(bf16)[:, None], (1, model_width)),
        ]
        packs.append(jnp.concatenate(rows, axis=0))

    def unpack(pack):
        stacked, sources, _ = gather_small(pack, ("dp",))
        slot = me ^ jnp.arange(count) if count == SMALL else jnp.arange(count)
        per_pack = stacked.shape[1]
        flat = stacked.reshape(count * per_pack, model_width)

        def place(index):
            return (me ^ index) if count == SMALL else index

        buckets = jnp.stack(
            [lax.dynamic_index_in_dim(flat, place(index) * per_pack + per_pack - 1, 0, False)[0] for index in range(count)]
        ).astype(jnp.int32)
        bucket = lax.dynamic_index_in_dim(buckets, sequence, 0, False)
        row = place(bucket // table_rows) * per_pack + bucket % table_rows
        scaling = lax.dynamic_slice_in_dim(flat, row, 1, 0).astype(f32)
        vectors = jnp.stack(
            [
                lax.dynamic_slice_in_dim(
                    flat, place(index) * per_pack + table_rows, per_pack - 1 - table_rows, 0
                ).reshape(-1)
                for index in range(count)
            ]
        ).astype(f32)
        share = model_width // count
        members = [vectors[:, i * share : (i + 1) * share].reshape(1, -1) for i in range(6)]
        members.append(vectors[:, 6 * share : 6 * share + expand_bias.shape[1]].reshape(1, -1))
        return tuple(members) + (scaling,), buckets

    keys_at = model_width
    shards = []
    for layer in range(layers):
        shards += [
            attention_in[layer][:, keys_at:],
            attention_in[layer][:, :keys_at],
            attention_out[layer],
            expand_weight[layer],
            reduce_weight[layer],
        ]
    gathered = []
    for position, shard in enumerate(shards):
        if count == SMALL and position >= 2:
            shard = after(shard, gathered[position - 2][2], gathered[position - 2][4])
        gathered.append(gather_rows(shard, position % 2))

    all_vectors, buckets = [], None
    for layer in range(layers):
        vectors, buckets = unpack(packs[layer])
        all_vectors.append(vectors)

    saved, all_weights = [], []
    for layer in range(layers):
        w_keys, w_query, w_out, w_expand, w_reduce = gathered[5 * layer : 5 * layer + 5]
        weights = (w_query, w_keys, w_out, w_expand, w_reduce)
        all_weights.append(weights)
        stream, kept = layer_forward(stream, weights, all_vectors[layer])
        saved.append(kept)
    back_moves = layout_moves(True)
    outputs = lax.ppermute(stream.astype(bf16), ("dp", "seq"), back_moves)[None]

    grad_flow = lax.ppermute(cotangent[0], ("dp", "seq"), layout_moves(False)).astype(f32)
    dense, small, modulation = [None] * layers, [None] * layers, [None] * layers
    for layer in reversed(range(layers)):
        grad_flow, dense[layer], small[layer], modulation[layer] = layer_backward(
            saved[layer], all_weights[layer], all_vectors[layer], grad_flow
        )
    input_grad = lax.ppermute(grad_flow, ("dp", "seq"), back_moves)[None]

    devices = count * planes
    packed = jnp.concatenate(
        [member.reshape(devices, -1) for layer in range(layers) for member in small[layer]], axis=1
    )
    row = scatter_small(packed)
    small_out, start = [[] for _ in range(7)], 0
    for layer in range(layers):
        for member in range(7):
            width = small[layer][member].size // devices
            small_out[member].append(row[start : start + width])
            start += width
    small_out = [jnp.stack(member) for member in small_out]

    changes, from_dp, from_seq = gather_small(jnp.concatenate(modulation), ("dp", "seq"))
    owners = (from_dp // 2) * 2 + from_seq // 2
    source_buckets = jnp.sum(
        jnp.where(owners[:, None] == jnp.arange(count)[None, :], buckets[None, :], 0), axis=1
    )
    table_share = BUCKETS // devices
    first_row = (me * planes + plane) * table_share
    chosen = (source_buckets[None, :] == (first_row + jnp.arange(table_share))[:, None]).astype(f32)
    table_grad = jnp.dot(chosen, changes, precision=lax.Precision.HIGHEST)
    table_grad = jnp.stack(
        [table_grad[:, layer * model_width : (layer + 1) * model_width] for layer in range(layers)]
    )

    dense_out = [jnp.stack([dense[layer][member] for layer in range(layers)]) for member in range(4)]
    return (
        outputs,
        input_grad,
        small_out[0],
        small_out[1],
        dense_out[0],
        dense_out[1],
        small_out[2],
        small_out[3],
        small_out[4],
        dense_out[2],
        small_out[6],
        dense_out[3],
        small_out[5],
        table_grad,
    )


def solution(mesh):
    return jax.shard_map(
        on_device,
        mesh=mesh,
        in_specs=(
            P("dp", "seq", None),
            P("dp"),
            P(None, "dp"),
            P(None, "dp"),
            P(None, "dp", None),
            P(None, "dp", None),
            P(None, "dp"),
            P(None, "dp"),
            P(None, "dp"),
            P(None, "dp", None),
            P(None, "dp"),
            P(None, "dp", None),
            P(None, "dp"),
            P(None, "dp", None),
            P("dp", "seq", None),
        ),
        out_specs=(
            P("dp", "seq", None),
            P("dp", "seq", None),
            P(None, ("dp", "seq")),
            P(None, ("dp", "seq")),
            P(None, ("dp", "seq"), None),
            P(None, ("dp", "seq"), None),
            P(None, ("dp", "seq")),
            P(None, ("dp", "seq")),
            P(None, ("dp", "seq")),
            P(None, ("dp", "seq"), None),
            P(None, ("dp", "seq")),
            P(None, ("dp", "seq"), None),
            P(None, ("dp", "seq")),
            P(None, ("dp", "seq"), None),
        ),
        check_vma=False,
    )
```

```python
import functools
import math

import jax
import jax.numpy as jnp
from jax import lax
from jax.experimental import pallas as pl
from jax.experimental.pallas import tpu as pltpu
from jax.sharding import PartitionSpec as P

HEAD = 64
BUCKETS = 256
SMALL = 8
WIDE = 1024

epsilon = 1e-05
bf16 = jnp.bfloat16
f32 = jnp.float32


def modulated_norm(activations, norm_gain, norm_shift, scaling):
    center = activations - jnp.mean(activations, axis=-1, keepdims=True)
    spread = jnp.mean(center * center, axis=-1, keepdims=True)
    return (center * lax.rsqrt(spread + epsilon) * norm_gain + norm_shift) * (1.0 + scaling)


def swap(array, bit):
    count = lax.axis_size("dp")
    return lax.ppermute(array, "dp", [(i, i ^ bit) for i in range(count)])


def swap_seq(array, bit):
    count = lax.axis_size("seq")
    return lax.ppermute(array, "seq", [(i, i ^ bit) for i in range(count)])


def after(array, *earlier):
    return lax.optimization_barrier((array,) + earlier)[0]


def layout_moves(back):
    moves = []
    for index in range(lax.axis_size("dp")):
        core, pair = index % 2, index - index % 2
        for plane in range(4):
            source = index * 4 + plane
            target = (pair + plane % 2) * 4 + 2 * core + plane // 2
            moves.append((target, source) if back else (source, target))
    return moves


def gather_rows(shard, route):
    if lax.axis_size("dp") != SMALL:
        return lax.all_gather(shard, "dp", axis=0, tiled=True)
    along_x = swap(shard, 2)
    along_y = swap(shard, 4)
    across = swap(along_x, 4) if route == 0 else swap(along_y, 2)
    mine = [shard, along_x, along_y, across]
    parts = []
    for part in mine:
        parts += [part, swap(part, 1)]
    return parts


def order_of(parts):
    me = lax.axis_index("dp")
    return [me ^ bit for bit in range(parts)]


def scatter_dense(left, right, orders):
    count, planes = lax.axis_size("dp"), lax.axis_size("seq")
    rows, columns = left.shape[1], right.shape[1]
    if count != SMALL:
        whole = jnp.einsum("tr,tc->rc", left, right, preferred_element_type=f32)
        return lax.psum_scatter(whole, ("dp", "seq"), scatter_dimension=0, tiled=True)
    me, plane = lax.axis_index("dp"), lax.axis_index("seq")
    block = rows // count
    width = columns // len(orders)

    def pick(masks):
        return jnp.concatenate(
            [lax.dynamic_slice_in_dim(left, (me ^ mask) * block, block, 1) for mask in masks], axis=1
        )

    def product(a, b):
        return jnp.einsum("tr,tc->rc", a, b, preferred_element_type=f32)

    pieces = []
    for position, (first, second) in enumerate(orders):
        part = right[:, position * width : (position + 1) * width]
        masks = [first | second, first, second, 0]
        arrived = swap(product(pick([mask | 1 for mask in masks]), part).astype(bf16), 1)
        half = 2 * block
        leaving = (product(pick(masks[:2]), part) + arrived[:half].astype(f32)).astype(bf16)
        staying = (product(pick(masks[2:]), part) + arrived[half:].astype(f32)).astype(bf16)
        arrived = swap(leaving, first)
        leaving = (staying[:block].astype(f32) + arrived[:block].astype(f32)).astype(bf16)
        staying = (staying[block:].astype(f32) + arrived[block:].astype(f32)).astype(bf16)
        arrived = swap(leaving, second)
        pieces.append((staying, arrived))
    total = jnp.concatenate([(a.astype(f32) + b.astype(f32)).astype(bf16) for a, b in pieces], axis=1)
    return scatter_planes(total, plane, planes)


def scatter_planes(total, plane, planes):
    rows, columns = total.shape
    low, high = plane & 1, plane >> 1
    cut = total.reshape(2, 2, rows // planes, columns)
    arrived = swap_seq(lax.dynamic_index_in_dim(cut, 1 - low, 1, keepdims=False), 1)
    kept = lax.dynamic_index_in_dim(cut, low, 1, keepdims=False)
    joined = kept.astype(f32) + arrived.astype(f32)
    arrived = swap_seq(lax.dynamic_index_in_dim(joined, 1 - high, 0, keepdims=False).astype(bf16), 2)
    return lax.dynamic_index_in_dim(joined, high, 0, keepdims=False) + arrived.astype(f32)


def scatter_small(array):
    count, planes = lax.axis_size("dp"), lax.axis_size("seq")
    if count != SMALL:
        return lax.psum_scatter(array, ("dp", "seq"), scatter_dimension=0, tiled=True)[0]
    me, plane = lax.axis_index("dp"), lax.axis_index("seq")
    columns = array.shape[1]
    shape = [count, planes]
    current = array.reshape(shape[0], shape[1], columns)
    for axis, index, send in ((0, me, swap), (1, plane, swap_seq)):
        bit = 1
        while current.shape[axis] > 1:
            pairs = current.shape[axis] // 2
            view = jnp.moveaxis(current, axis, 0).reshape(pairs, 2, -1, columns)
            mine = (index // bit) % 2
            leaving = lax.dynamic_index_in_dim(view, 1 - mine, 1, keepdims=False)
            staying = lax.dynamic_index_in_dim(view, mine, 1, keepdims=False)
            current = jnp.moveaxis((staying + send(leaving, bit)).reshape(pairs, -1, columns), 0, axis)
            bit *= 2
    return current.reshape(columns)


def gather_small(array, axes):
    if lax.axis_size("dp") != SMALL:
        stacked = lax.all_gather(array, axes, axis=0, tiled=False)
        stacked = stacked.reshape((-1,) + array.shape)
        places = jnp.arange(stacked.shape[0])
        if "seq" in axes:
            planes = lax.axis_size("seq")
            return stacked, places // planes, places % planes
        return stacked, places, None
    current = array[None]
    me = lax.axis_index("dp")
    for bit in (1, 2, 4):
        current = jnp.concatenate([current, swap(current, bit)], axis=0)
    sources = me ^ jnp.arange(SMALL)
    if "seq" not in axes:
        return current, sources, None
    plane = lax.axis_index("seq")
    for bit in (1, 2):
        current = jnp.concatenate([current, swap_seq(current, bit)], axis=0)
    places = jnp.arange(SMALL * 4)
    return current, me ^ (places % SMALL), plane ^ (places // SMALL)


def times(a, weight, out_type):
    return jnp.dot(a, weight, preferred_element_type=f32).astype(out_type)


def times_transposed(a, weight, out_type):
    return lax.dot_general(a, weight, (((1,), (1,)), ((), ())), preferred_element_type=f32).astype(out_type)


def spread_keys(own):
    far = swap_seq(own, 1)
    return [own, swap(own, 1), far, swap(far, 1)]


def heads_of(rows):
    return rows.reshape(rows.shape[0], rows.shape[1] // HEAD, HEAD)


def attend(queries, chunks):
    model_width = queries.shape[1]
    whole = jnp.concatenate(chunks, axis=0)
    key_heads, value_heads = heads_of(whole[:, :model_width]), heads_of(whole[:, model_width:])
    scores = jnp.einsum("qhd,khd->hqk", heads_of(queries), key_heads, preferred_element_type=f32)
    scores = scores * (1.0 / math.sqrt(HEAD))
    exponent = jnp.exp(scores - jnp.max(scores, axis=-1, keepdims=True))
    probs = exponent / jnp.sum(exponent, axis=-1, keepdims=True)
    probs_low = probs.astype(bf16)
    mixture = jnp.einsum("hqk,khd->qhd", probs_low, value_heads, preferred_element_type=f32)
    return mixture.reshape(queries.shape).astype(bf16), (probs, probs_low)


def attend_back(queries, chunks, kept, mixture, mixture_grad):
    probs, probs_low = kept
    model_width = queries.shape[1]
    factor = 1.0 / math.sqrt(HEAD)
    whole = jnp.concatenate(chunks, axis=0)
    key_heads, value_heads = heads_of(whole[:, :model_width]), heads_of(whole[:, model_width:])
    grad_heads = heads_of(mixture_grad)
    prob_grad = jnp.einsum("qhd,khd->hqk", grad_heads, value_heads, preferred_element_type=f32)
    along = jnp.sum(probs * prob_grad, axis=-1, keepdims=True)
    score_grad = (probs * (prob_grad - along)).astype(bf16)
    query_grad = jnp.einsum("hqk,khd->qhd", score_grad, key_heads, preferred_element_type=f32)
    query_grad = (query_grad * factor).astype(bf16).reshape(queries.shape)
    key_part = jnp.einsum("hqk,qhd->khd", score_grad, heads_of(queries), preferred_element_type=f32)
    value_part = jnp.einsum("hqk,qhd->khd", probs_low, grad_heads, preferred_element_type=f32)
    parts = jnp.concatenate(
        [
            (key_part * factor).reshape(whole.shape[0], model_width),
            value_part.reshape(whole.shape[0], model_width),
        ],
        axis=1,
    ).astype(bf16)
    return query_grad, parts


def join_key_grads(parts):
    local = parts.shape[0] // 4
    cut = [parts[i * local : (i + 1) * local] for i in range(4)]
    far = cut[2].astype(f32) + swap(cut[3], 1).astype(f32)
    far = swap_seq(far.astype(bf16), 1)
    near = cut[0].astype(f32) + swap(cut[1], 1).astype(f32)
    return (near + far.astype(f32)).astype(bf16)


def layer_forward(stream, weights, vectors):
    w_query, w_keys, w_out, w_expand, w_reduce = weights
    first_gain, first_shift, attention_bias, second_gain, second_shift, reduce_bias, expand_bias, scaling = vectors
    normed = modulated_norm(stream, first_gain, first_shift, scaling).astype(bf16)
    chunks = spread_keys(times(normed, w_keys, bf16))
    queries = times(normed, w_query, bf16)
    mixture, kept = attend(queries, chunks)
    middle = stream + (times(mixture, w_out, f32) + attention_bias)
    second = modulated_norm(middle, second_gain, second_shift, scaling).astype(bf16)
    hidden = times(second, w_expand, f32) + expand_bias
    active = jax.nn.gelu(hidden).astype(bf16)
    result = middle + (times(active, w_reduce, f32) + reduce_bias)
    return result, (stream, normed, queries, chunks, kept, mixture, middle, second, hidden, active)


def layer_backward(saved, weights, vectors, grad_out):
    w_query, w_keys, w_out, w_expand, w_reduce = weights
    first_gain, first_shift, attention_bias, second_gain, second_shift, reduce_bias, expand_bias, scaling = vectors
    stream, normed, queries, chunks, kept, mixture, middle, second, hidden, active = saved
    both = ((2, 4), (4, 2))
    grad_low = grad_out.astype(bf16)
    reduce_bias_grad = jnp.sum(grad_out, axis=0)
    reduce_weight_grad = scatter_dense(active, grad_low, both)
    active_grad = times_transposed(grad_low, w_reduce, f32)
    hidden_grad = jax.vjp(jax.nn.gelu, hidden)[1](active_grad)[0]
    expand_bias_grad = jnp.sum(hidden_grad, axis=0)
    hidden_low = hidden_grad.astype(bf16)
    second_grad = times_transposed(hidden_low, w_expand, f32)
    expand_weight_grad = scatter_dense(second, hidden_low, both)
    _, second_back = jax.vjp(modulated_norm, middle, second_gain, second_shift, scaling)
    middle_part, second_gain_grad, second_shift_grad, second_scaling_grad = second_back(second_grad)
    middle_grad = grad_out + middle_part
    attention_bias_grad = jnp.sum(middle_grad, axis=0)
    middle_low = middle_grad.astype(bf16)
    mixture_grad = times_transposed(middle_low, w_out, bf16)
    attention_out_grad = scatter_dense(mixture, middle_low, both)
    query_grad, parts = attend_back(queries, chunks, kept, mixture, mixture_grad)
    key_grad = join_key_grads(parts)
    normed_grad = times_transposed(query_grad, w_query, f32) + times_transposed(key_grad, w_keys, f32)
    project_grad = jnp.concatenate([query_grad, key_grad], axis=1)
    attention_in_grad = scatter_dense(normed, project_grad, both)
    _, first_back = jax.vjp(modulated_norm, stream, first_gain, first_shift, scaling)
    stream_part, first_gain_grad, first_shift_grad, first_scaling_grad = first_back(normed_grad)
    stream_grad = middle_grad + stream_part
    small = (
        first_gain_grad,
        first_shift_grad,
        attention_bias_grad,
        second_gain_grad,
        second_shift_grad,
        reduce_bias_grad,
        expand_bias_grad,
    )
    dense = (attention_in_grad, attention_out_grad, expand_weight_grad, reduce_weight_grad)
    return stream_grad, dense, small, (first_scaling_grad + second_scaling_grad)[0]


def pack_small(vectors, rows):
    flat = jnp.concatenate([vector.reshape(-1) for vector in vectors])
    length = -(-flat.shape[0] // WIDE) * WIDE
    return jnp.pad(flat, (0, length - flat.shape[0])).reshape(-1, WIDE)


def table_rows_of(changes, from_dp, from_seq, buckets, layers, model_width):
    count, planes = lax.axis_size("dp"), lax.axis_size("seq")
    owners = (from_dp // 2) * 2 + from_seq // 2
    source_buckets = jnp.sum(
        jnp.where(owners[:, None] == jnp.arange(count)[None, :], buckets[None, :], 0), axis=1
    )
    return chosen_rows(changes, source_buckets, layers, model_width)


def chosen_rows(changes, source_buckets, layers, model_width):
    count, planes = lax.axis_size("dp"), lax.axis_size("seq")
    table_share = BUCKETS // (count * planes)
    first_row = (lax.axis_index("dp") * planes + lax.axis_index("seq")) * table_share
    chosen = (source_buckets[None, :] == (first_row + jnp.arange(table_share))[:, None]).astype(f32)
    table_grad = jnp.dot(chosen, changes, precision=lax.Precision.HIGHEST)
    return jnp.stack(
        [table_grad[:, layer * model_width : (layer + 1) * model_width] for layer in range(layers)]
    )


VMEM_LIMIT = 64_000 * 1024
TILE = 1024
BLOCK = 128
NT = (((1,), (1,)), ((), ()))
TN = (((0,), (0,)), ((), ()))


def whole_spec(array):
    zeros = (0,) * len(array.shape)
    return pl.BlockSpec(array.shape, lambda *_: zeros)


def run(body, grid, inputs, outputs, scratch=(), deps=(), aliases=(), cost=4):
    deps = tuple(aliases) + tuple(deps)
    arrays = [array for array, _ in inputs]
    specs = [spec if spec is not None else whole_spec(array) for array, spec in inputs]
    shapes = [jax.ShapeDtypeStruct(shape, kind) for shape, kind, _ in outputs]
    out_specs = [
        spec if spec is not None else whole_spec(shape) for shape, (_, _, spec) in zip(shapes, outputs)
    ]
    count, extra = len(arrays), len(deps)

    def kernel(place, *refs):
        body(place, refs[:count], refs[count + extra : count + extra + len(shapes)], refs[count + extra + len(shapes) :])

    place = jnp.stack([lax.axis_index("dp"), lax.axis_index("seq")]).astype(jnp.int32)
    return pl.pallas_call(
        kernel,
        out_shape=shapes,
        grid_spec=pltpu.PrefetchScalarGridSpec(
            num_scalar_prefetch=1,
            grid=(grid,),
            in_specs=specs + [pl.BlockSpec(memory_space=pl.ANY)] * extra,
            out_specs=out_specs,
            scratch_shapes=list(scratch),
        ),
        input_output_aliases={1 + count + i: i for i in range(len(aliases))},
        compiler_params=pltpu.CompilerParams(vmem_limit_bytes=VMEM_LIMIT),
        cost_estimate=pl.CostEstimate(flops=0, bytes_accessed=cost * 3_000_000, transcendentals=0),
    )(place, *arrays, *deps)


def pack_inputs(pack, tile_of):
    return [
        (array, pl.BlockSpec((rows, TILE), lambda i, s, r=row_block: (r, tile_of(i))))
        for array, row_block, rows in pack
    ]


def join(refs):
    return jnp.concatenate([ref[...] for ref in refs], axis=0)


def block_at(place, part, stride=BLOCK, offset=0):
    return pl.ds(pl.multiple_of((place[0] ^ part) * stride + offset, BLOCK), BLOCK)


def columns_in_order(place, ref, stride=BLOCK, offset=0):
    return jnp.concatenate(
        [ref[:, block_at(place, part, stride, offset)] for part in range(SMALL)], axis=1
    )


def normalise(v):
    center = v - jnp.mean(v, axis=-1, keepdims=True)
    inverse = lax.rsqrt(jnp.mean(center * center, axis=-1, keepdims=True) + epsilon)
    return center * inverse, inverse


def modulated(v, vec, gain_row):
    unit, _ = normalise(v)
    return (unit * vec[gain_row : gain_row + 1, :] + vec[gain_row + 1 : gain_row + 2, :]) * vec[6:7, :]


def modulated_back(v, vec, gain_row, grad):
    unit, inverse = normalise(v)
    gain, shift, scale = vec[gain_row : gain_row + 1, :], vec[gain_row + 1 : gain_row + 2, :], vec[6:7, :]
    scale_grad = jnp.sum(grad * (unit * gain + shift), axis=0, keepdims=True)
    inner = grad * scale
    gain_grad = jnp.sum(inner * unit, axis=0, keepdims=True)
    shift_grad = jnp.sum(inner, axis=0, keepdims=True)
    inner = inner * gain
    back = inverse * (
        inner
        - jnp.mean(inner, axis=-1, keepdims=True)
        - unit * jnp.mean(inner * unit, axis=-1, keepdims=True)
    )
    return back, gain_grad, shift_grad, scale_grad


ROOT = math.sqrt(2.0 / math.pi)
CUBIC = 0.044715


def first_norm(x, vec, deps=()):
    def body(place, ins, outs, _):
        outs[0][...] = modulated(ins[0][...].astype(f32), ins[1], 0).astype(bf16)

    return run(body, 1, [(x, None), (vec, None)], [(x.shape, bf16, None)], deps=deps)[0]


def project(a, pack, first_tile, tiles, deps=()):
    tokens, width = a.shape

    def body(place, ins, outs, scratch):
        @pl.when(pl.program_id(0) == 0)
        def _():
            scratch[0][...] = columns_in_order(place, ins[0])

        outs[0][...] = jnp.dot(scratch[0][...], join(ins[1:]), preferred_element_type=f32).astype(bf16)

    return run(
        body,
        tiles,
        [(a, None)] + pack_inputs(pack, lambda i: first_tile + i),
        [((tokens, tiles * TILE), bf16, pl.BlockSpec((tokens, TILE), lambda i, s: (0, i)))],
        [pltpu.VMEM((tokens, width), bf16)],
        deps=deps,
    )[0]


def key_specs(chunks):
    return [
        (chunk, pl.BlockSpec((chunk.shape[0], 4 * HEAD), lambda i, s: (0, i))) for chunk in chunks
    ]


def head_masks(rows):
    lane = lax.broadcasted_iota(jnp.int32, (rows, 2 * HEAD), 1)
    return lane < HEAD, lane >= HEAD


def attend_fast(queries, chunks, deps=()):
    tokens, width = queries.shape
    pairs = width // (2 * HEAD)

    def body(place, ins, outs, _):
        both = join(ins[1:5])
        keys, values = both[:, : 2 * HEAD], both[:, 2 * HEAD :]
        scaled = ins[0][...] * jnp.asarray(1.0 / math.sqrt(HEAD), bf16)
        halves, tops = [], []
        for head, mask in enumerate(head_masks(tokens)):
            query = jnp.where(mask, scaled, jnp.zeros_like(scaled))
            scores = lax.dot_general(keys, query, NT, preferred_element_type=f32)
            most = jnp.max(scores, axis=0, keepdims=True)
            exponent = jnp.exp(scores - most)
            total = jnp.sum(exponent, axis=0, keepdims=True)
            mixed = lax.dot_general(values, exponent.astype(bf16), TN, preferred_element_type=f32)
            halves.append(mixed[head * HEAD : (head + 1) * HEAD] / total)
            tops.append(most + jnp.log(total))
        outs[0][...] = jnp.concatenate(halves, axis=0).T.astype(bf16)
        outs[1][0, 0:1, :] = tops[0]
        outs[1][0, 1:2, :] = tops[1]

    return run(
        body,
        pairs,
        [(queries, pl.BlockSpec((tokens, 2 * HEAD), lambda i, s: (0, i)))] + key_specs(chunks),
        [
            (queries.shape, bf16, pl.BlockSpec((tokens, 2 * HEAD), lambda i, s: (0, i))),
            ((pairs, 8, tokens), f32, pl.BlockSpec((1, 8, tokens), lambda i, s: (i, 0, 0))),
        ],
        deps=deps,
        cost=15,
    )


def attend_fast_back(queries, chunks, kept, mixture_grad, tops, deps=()):
    tokens, width = queries.shape
    pairs = width // (2 * HEAD)

    def body(place, ins, outs, _):
        both = join(ins[1:5])
        keys, values = both[:, : 2 * HEAD], both[:, 2 * HEAD :]
        scaled = ins[0][...] * jnp.asarray(1.0 / math.sqrt(HEAD), bf16)
        grads = ins[6][...]
        masks = head_masks(tokens)
        select = jnp.concatenate([mask[0:1].astype(f32) for mask in masks] + [jnp.zeros((6, 2 * HEAD), f32)], axis=0)
        along = lax.dot_general(
            select,
            ins[5][...].astype(f32) * grads.astype(f32),
            NT,
            precision=lax.Precision.HIGHEST,
            preferred_element_type=f32,
        )
        key_grad = value_grad = None
        halves = []
        for head, mask in enumerate(masks):
            query = jnp.where(mask, scaled, jnp.zeros_like(scaled))
            grad = jnp.where(mask, grads, jnp.zeros_like(grads))
            scores = lax.dot_general(keys, query, NT, preferred_element_type=f32)
            probs = jnp.exp(scores - ins[7][0, head : head + 1, :])
            prob_grad = lax.dot_general(values, grad, NT, preferred_element_type=f32)
            score_grad = (probs * (prob_grad - along[head : head + 1, :])).astype(bf16)
            key_part = jnp.dot(score_grad, query, preferred_element_type=f32)
            value_part = jnp.dot(probs.astype(bf16), grad, preferred_element_type=f32)
            key_grad = key_part if head == 0 else key_grad + key_part
            value_grad = value_part if head == 0 else value_grad + value_part
            query_part = lax.dot_general(keys, score_grad, TN, preferred_element_type=f32)
            halves.append(query_part[head * HEAD : (head + 1) * HEAD])
        query_grad = jnp.concatenate(halves, axis=0) * (1.0 / math.sqrt(HEAD))
        outs[0][...] = query_grad.T.astype(bf16)
        for chunk in range(4):
            rows = slice(chunk * tokens, (chunk + 1) * tokens)
            outs[1 + chunk][:, : 2 * HEAD] = key_grad[rows].astype(bf16)
            outs[1 + chunk][:, 2 * HEAD :] = value_grad[rows].astype(bf16)

    pair_spec = pl.BlockSpec((tokens, 2 * HEAD), lambda i, s: (0, i))
    part = ((tokens, 2 * width), bf16, pl.BlockSpec((tokens, 4 * HEAD), lambda i, s: (0, i)))
    return run(
        body,
        pairs,
        [(queries, pair_spec)]
        + key_specs(chunks)
        + [
            (kept, pl.BlockSpec((tokens, 2 * HEAD), lambda i, s: (0, MIXTURE // (2 * HEAD) + i))),
            (mixture_grad, pair_spec),
            (tops, pl.BlockSpec((1, 8, tokens), lambda i, s: (i, 0, 0))),
        ],
        [(queries.shape, bf16, pair_spec)] + [part] * 4,
        deps=deps,
        cost=18,
    )


def window(step, tile):
    return pl.ds(pl.multiple_of((step - tile) * TILE, BLOCK), TILE)


ACTIVE, SECOND, MIXTURE, NORMED, KEPT = 0, 4 * TILE, 5 * TILE, 6 * TILE, 7 * TILE


def feed_forward(normed, mixture, packs, stream, vec, bias, next_vec, deps=()):
    tokens, width = mixture.shape
    columns = bias.shape[1]
    attention_pack, expand_pack, reduce_pack = packs
    one = len(attention_pack)

    def body(place, ins, outs, scratch):
        step = pl.program_id(0)
        mixture_ref, stream_ref, vec_ref, next_ref, bias_ref, normed_ref = ins[:6]
        middle_ref, kept_ref, slope_ref, result_ref, following_ref = outs
        ordered, total = scratch

        @pl.when(step == 0)
        def _():
            branch = jnp.dot(
                columns_in_order(place, mixture_ref), join(ins[6 : 6 + one]), preferred_element_type=f32
            )
            middle = stream_ref[...].astype(f32) + (branch + vec_ref[2:3, :])
            middle_ref[...] = middle
            kept_ref[:, SECOND:MIXTURE] = modulated(middle, vec_ref, 3).astype(bf16)
            kept_ref[:, MIXTURE:NORMED] = mixture_ref[...]
            kept_ref[:, NORMED:KEPT] = normed_ref[...]
            ordered[...] = columns_in_order(place, kept_ref, BLOCK, SECOND)

        @pl.when((step > 0) & (step < 5))
        def _():
            at = window(step, 1)
            hidden = jnp.dot(
                ordered[...], join(ins[6 + one : 6 + 2 * one]), preferred_element_type=f32
            ) + bias_ref[:, at]
            square = hidden * hidden
            bent = jnp.tanh(ROOT * hidden * (1.0 + CUBIC * square))
            half = 0.5 * (1.0 + bent)
            kept_ref[:, at] = (hidden * half).astype(bf16)
            slope = half + (0.5 * ROOT) * hidden * (1.0 - bent * bent) * (1.0 + (3.0 * CUBIC) * square)
            slope_ref[:, at] = slope.astype(bf16)

        @pl.when(step >= 5)
        def _():
            a = columns_in_order(place, kept_ref, 4 * BLOCK, (step - 5) * BLOCK)
            product = jnp.dot(a, join(ins[6 + 2 * one :]), preferred_element_type=f32)

            @pl.when(step == 5)
            def _():
                total[...] = product

            @pl.when(step > 5)
            def _():
                total[...] += product

            @pl.when(step == 8)
            def _():
                result = middle_ref[...] + (total[...] + vec_ref[5:6, :])
                result_ref[...] = result
                if next_vec is None:
                    following_ref[...] = result.astype(bf16)
                else:
                    following_ref[...] = modulated(result, next_ref, 0).astype(bf16)

    wide_shape = (tokens, columns)
    return run(
        body,
        9,
        [
            (mixture, None),
            (stream, None),
            (vec, None),
            (vec if next_vec is None else next_vec, None),
            (bias, None),
            (normed, None),
        ]
        + pack_inputs(attention_pack, lambda i: 3)
        + pack_inputs(expand_pack, lambda i: jnp.clip(i - 1, 0, 3))
        + pack_inputs(reduce_pack, lambda i: jnp.clip(i - 5, 0, 3)),
        [
            (mixture.shape, f32, None),
            ((tokens, KEPT), bf16, None),
            (wide_shape, bf16, None),
            (mixture.shape, f32, None),
            (mixture.shape, bf16, None),
        ],
        [pltpu.VMEM((tokens, width), bf16), pltpu.VMEM((tokens, width), f32)],
        deps=deps,
        cost=19,
    )


def feed_forward_back(grad, grad_low, slope, middle, packs, vec, deps=()):
    tokens, width = grad.shape
    columns = slope.shape[1]
    attention_pack, expand_pack, reduce_pack = packs
    one = len(attention_pack)

    def body(place, ins, outs, scratch):
        step = pl.program_id(0)
        grad_ref, grad_low_ref, slope_ref, middle_ref, vec_ref = ins[:5]
        hidden_refs, low_ref = outs[:2], outs[2]
        bias_ref, middle_grad_ref, sums_ref, mixture_ref = outs[3:]
        total, ordered = scratch

        @pl.when(step < 4)
        def _():
            product = lax.dot_general(
                grad_low_ref[...], join(ins[5 : 5 + one]), NT, preferred_element_type=f32
            )
            for part in range(SMALL):
                at = block_at(place, part, 4 * BLOCK, step * BLOCK)
                piece = product[:, part * BLOCK : (part + 1) * BLOCK] * slope_ref[:, at].astype(f32)
                bias_ref[:, at] = jnp.sum(piece, axis=0, keepdims=True)
                half = (place[0] ^ part) // 4
                within = pl.ds(pl.multiple_of(((place[0] ^ part) % 4) * 4 * BLOCK + step * BLOCK, BLOCK), BLOCK)
                for number in range(2):

                    @pl.when(half == number)
                    def _(number=number, piece=piece, within=within):
                        hidden_refs[number][:, within] = piece.astype(bf16)

        @pl.when((step >= 4) & (step < 8))
        def _():
            for number in range(4):

                @pl.when(step == 4 + number)
                def _(number=number):
                    start = (number % 2) * TILE
                    product = lax.dot_general(
                        hidden_refs[number // 2][:, start : start + TILE],
                        join(ins[5 + one : 5 + 2 * one]),
                        NT,
                        preferred_element_type=f32,
                    )
                    total[...] = product if number == 0 else total[...] + product

            @pl.when(step == 7)
            def _():
                for part in range(SMALL):
                    ordered[:, block_at(place, part)] = total[:, part * BLOCK : (part + 1) * BLOCK]
                back, gain_grad, shift_grad, scale_grad = modulated_back(
                    middle_ref[...], vec_ref, 3, ordered[...]
                )
                upstream = grad_ref[...].astype(f32)
                middle_grad = upstream + back
                middle_grad_ref[...] = middle_grad
                low_ref[...] = middle_grad.astype(bf16)
                sums_ref[0:1, :] = gain_grad
                sums_ref[1:2, :] = shift_grad
                sums_ref[2:3, :] = scale_grad
                sums_ref[3:4, :] = jnp.sum(middle_grad, axis=0, keepdims=True)
                sums_ref[4:5, :] = jnp.sum(upstream, axis=0, keepdims=True)

        @pl.when(step == 8)
        def _():
            product = lax.dot_general(
                low_ref[...], join(ins[5 + 2 * one :]), NT, preferred_element_type=f32
            ).astype(bf16)
            for part in range(SMALL):
                mixture_ref[:, block_at(place, part)] = product[:, part * BLOCK : (part + 1) * BLOCK]

    return run(
        body,
        9,
        [
            (grad, None),
            (grad_low[0], pl.BlockSpec((tokens, TILE), lambda i, s: (0, grad_low[1]))),
            (slope, None),
            (middle, None),
            (vec, None),
        ]
        + pack_inputs(reduce_pack, lambda i: jnp.minimum(i, 3))
        + pack_inputs(expand_pack, lambda i: jnp.clip(i - 4, 0, 3))
        + pack_inputs(attention_pack, lambda i: 3),
        [
            ((tokens, 2 * TILE), bf16, None),
            ((tokens, 2 * TILE), bf16, None),
            (grad.shape, bf16, None),
            ((1, columns), f32, None),
            (grad.shape, f32, None),
            ((8, width), f32, None),
            (grad.shape, bf16, None),
        ],
        [pltpu.VMEM((tokens, width), f32), pltpu.VMEM((tokens, width), f32)],
        deps=deps,
        cost=18,
    )


def first_back(query_grad, key_parts, pack, stream, middle_grad, vec, deps=()):
    tokens, width = stream.shape
    kept, arrived, far = key_parts

    def body(place, ins, outs, scratch):
        step = pl.program_id(0)
        weights = join(ins[7:])

        @pl.when(step == 0)
        def _():
            outs[1][:, :TILE] = ins[0][...]
            scratch[0][...] = lax.dot_general(ins[0][...], weights, NT, preferred_element_type=f32)

        @pl.when(step > 0)
        def _():
            total = ins[1][...].astype(f32) + ins[2][...].astype(f32) + ins[3][...].astype(f32)
            rounded = total.astype(bf16)
            outs[3][...] = rounded
            scratch[0][...] += lax.dot_general(rounded, weights, NT, preferred_element_type=f32)

        @pl.when(step == 2)
        def _():
            for part in range(SMALL):
                scratch[1][:, block_at(place, part)] = scratch[0][:, part * BLOCK : (part + 1) * BLOCK]
            back, gain_grad, shift_grad, scale_grad = modulated_back(
                ins[4][...].astype(f32), ins[6], 0, scratch[1][...]
            )
            result = ins[5][...] + back
            outs[0][...] = result
            outs[1][:, TILE:] = result.astype(bf16)
            outs[2][0:1, :] = gain_grad
            outs[2][1:2, :] = shift_grad
            outs[2][2:3, :] = scale_grad

    tile = pl.BlockSpec((tokens, TILE), lambda i, s: (0, jnp.maximum(i - 1, 0)))
    return run(
        body,
        3,
        [
            (query_grad, None),
            (kept, tile),
            (arrived, tile),
            (far, tile),
            (stream, None),
            (middle_grad, None),
            (vec, None),
        ]
        + pack_inputs(pack, lambda i: i),
        [
            (stream.shape, f32, None),
            ((tokens, 2 * TILE), bf16, None),
            ((8, width), f32, None),
            (far.shape, bf16, tile),
        ],
        [pltpu.VMEM((tokens, width), f32), pltpu.VMEM((tokens, width), f32)],
        deps=deps,
        cost=10,
    )


ORDERS = ((6, 2, 4, 0), (6, 4, 2, 0))


class Group:
    def __init__(self, arrays, left_of, right_of):
        self.left_of, self.right_of = left_of, right_of
        self.inputs = [(side, spec) for pair, spec in arrays for side in pair]

    def product(self, place, refs, tile):
        array, stride, offset = self.left_of[tile]
        left = [
            jnp.concatenate(
                [refs[2 * array + side][:, block_at(place, mask, stride, offset)] for mask in ORDERS[tile // 2]],
                axis=1,
            )
            for side in range(2)
        ]
        array = self.right_of[tile]
        return lax.dot_general(
            jnp.concatenate(left, axis=0), join(refs[2 * array : 2 * array + 2]), TN, preferred_element_type=f32
        )


def part_of(rows, first):
    at = first if callable(first) else (lambda i: first)
    return pl.BlockSpec((rows, TILE), lambda i, s: (0, at(i)))


def reduce_group(kept, lower, block):
    rows = kept[0].shape[0]
    return Group(
        [(kept, pl.BlockSpec((rows, 4 * TILE), lambda i, s: (0, 0))), (lower, part_of(rows, block))],
        [(0, 4 * BLOCK, u * BLOCK) for u in range(4)],
        [1] * 4,
    )


def expand_group(kept, back):
    rows = kept[0].shape[0]
    return Group(
        [
            (kept, part_of(rows, SECOND // TILE)),
            (back[0], part_of(rows, lambda i: jnp.minimum(i, 1))),
            (back[1], part_of(rows, lambda i: jnp.maximum(i - 2, 0))),
        ],
        [(0, BLOCK, 0)] * 4,
        [1, 1, 2, 2],
    )


def attention_group(kept, back, lower, key_grad):
    rows = kept[0].shape[0]
    return Group(
        [
            (kept, part_of(rows, NORMED // TILE)),
            (kept, part_of(rows, MIXTURE // TILE)),
            (lower, part_of(rows, 0)),
            (key_grad, part_of(rows, lambda i: jnp.clip(i - 1, 0, 1))),
            (back[2], part_of(rows, 0)),
        ],
        [(0, BLOCK, 0)] * 3 + [(1, BLOCK, 0)],
        [2, 3, 3, 4],
    )


def wide(value):
    return value.astype(f32)


def half_spec(rows, half):
    return pl.BlockSpec((rows, TILE), lambda i, s: (0, jnp.maximum(i - 2, 0) if half else jnp.minimum(i, 1)))


def both_spec(rows):
    return pl.BlockSpec((1, rows, TILE), lambda i, s: (i // 2, 0, i % 2))


class Reduction:
    def __init__(self, group, stacked=False):
        self.group, self.stacked = group, stacked


def advance(seconds=(), thirds=(), fourths=(), joint=(), deps=()):
    inputs, outputs, works = [], [], []
    quarter, eighth = (2 * BLOCK, 2 * TILE), (BLOCK, 2 * TILE)
    for one in seconds:
        group, base, out = one.group, len(inputs), len(outputs)
        inputs += group.inputs
        outputs += [
            (quarter, bf16, half_spec(2 * BLOCK, 0)),
            (quarter, bf16, half_spec(2 * BLOCK, 1)),
            ((2,) + quarter, bf16, both_spec(2 * BLOCK)),
        ]

        def product(place, ins, outs, tile, group=group, base=base, out=out):
            total = group.product(place, ins[base : base + len(group.inputs)], tile)
            outs[out + tile // 2][...] = total[: 2 * BLOCK].astype(bf16)
            outs[out + 2][0] = total[2 * BLOCK :].astype(bf16)

        works.append(product)
    for one in thirds:
        base, out = len(inputs), len(outputs)
        inputs += [
            (one.staying, both_spec(2 * BLOCK)),
            (one.from_x, half_spec(2 * BLOCK, 0)),
            (one.from_y, half_spec(2 * BLOCK, 1)),
        ]
        outputs += [
            (eighth, bf16, half_spec(BLOCK, 0)),
            (eighth, bf16, half_spec(BLOCK, 1)),
            ((2,) + eighth, bf16, both_spec(BLOCK)),
        ]

        def add(place, ins, outs, tile, base=base, out=out):
            total = (wide(ins[base][0]) + wide(ins[base + 1 + tile // 2][...])).astype(bf16)
            outs[out + tile // 2][...] = total[:BLOCK]
            outs[out + 2][0] = total[BLOCK:]

        works.append(add)
    for one in fourths:
        base, out = len(inputs), len(outputs)
        inputs += [
            (one.kept, both_spec(BLOCK)),
            (one.second_y, half_spec(BLOCK, 0)),
            (one.second_x, half_spec(BLOCK, 1)),
        ]
        shape = (4 * BLOCK, TILE) if one.stacked else (BLOCK, 4 * TILE)
        spec = pl.BlockSpec((BLOCK, TILE), lambda i, s, stacked=one.stacked: (i, 0) if stacked else (0, i))
        outputs.append((shape, bf16, spec))

        def finish(place, ins, outs, tile, base=base, out=out):
            outs[out][...] = (wide(ins[base][0]) + wide(ins[base + 1 + tile // 2][...])).astype(bf16)

        works.append(finish)

    if joint:
        base, out, share = len(inputs), len(outputs), BLOCK // 4
        for one in joint:
            inputs += [
                (one.kept, both_spec(BLOCK)),
                (one.second_y, half_spec(BLOCK, 0)),
                (one.second_x, half_spec(BLOCK, 1)),
            ]
        rows = len(joint) * BLOCK
        outputs.append(((rows, 4 * TILE), bf16, pl.BlockSpec((rows, TILE), lambda i, s: (0, i))))

        def interleave(place, ins, outs, tile):
            for number in range(len(joint)):
                at = base + 3 * number
                total = (wide(ins[at][0]) + wide(ins[at + 1 + tile // 2][...])).astype(bf16)
                for plane in range(4):
                    start = (plane * len(joint) + number) * share
                    outs[out][start : start + share, :] = total[plane * share : (plane + 1) * share]

        works.append(interleave)

    def body(place, ins, outs, _):
        for tile in range(4):

            @pl.when(pl.program_id(0) == tile)
            def _(tile=tile):
                for work in works:
                    work(place, ins, outs, tile)

    results = list(run(body, 4, inputs, outputs, deps=deps, cost=7 if seconds else 5))
    token = results[0]
    for one in seconds:
        along_x, along_y, one.staying = results[:3]
        results = results[3:]
        one.from_x, one.from_y = swap(along_x, 2), swap(along_y, 4)
    for one in thirds:
        along_y, along_x, one.kept = results[:3]
        results = results[3:]
        one.second_y, one.second_x = swap(along_y, 4), swap(along_x, 2)
    for one in fourths:
        one.share = lax.psum_scatter(results[0], "seq", scatter_dimension=0, tiled=True)
        results = results[1:]
    if joint:
        both = lax.psum_scatter(results[0], "seq", scatter_dimension=0, tiled=True)
        for number, one in enumerate(joint):
            one.share = both[number * share : (number + 1) * share]
    return token


HALF = BLOCK // 2
EXTRA = 32


def raw_inputs(kind, layer, arrays):
    if kind == "attention":
        return [
            (arrays[0], pl.BlockSpec((1,) + arrays[0].shape[1:], lambda i, s: (layer, 0, 0))),
            (arrays[1], pl.BlockSpec((1,) + arrays[1].shape[1:], lambda i, s: (layer, 0, 0))),
        ]
    if kind == "expand":
        return [(arrays[0], pl.BlockSpec((1, BLOCK, TILE), lambda i, s: (layer, 0, i)))]
    return [(arrays[0], pl.BlockSpec((1, BLOCK, TILE), lambda i, s: (layer, i, 0)))]


def raw_tile(kind, ins, targets):
    if kind != "attention":
        for target in targets:
            target[:BLOCK, :] = ins[0][0]
        return
    pairs = TILE // (2 * BLOCK)
    for tile in range(4):

        @pl.when(pl.program_id(0) == tile)
        def _(tile=tile):
            for target in targets:
                if tile == 0:
                    target[:BLOCK, :] = ins[0][0, :, :TILE]
                elif tile == 3:
                    target[:BLOCK, :] = ins[1][0]
                else:
                    for pair in range(pairs):
                        start = (pairs * (tile - 1) + pair) * BLOCK
                        at = pair * 2 * BLOCK
                        target[:BLOCK, at : at + BLOCK] = ins[0][0, :, TILE + start : TILE + start + BLOCK]
                        target[:BLOCK, at + BLOCK : at + 2 * BLOCK] = ins[0][
                            0, :, 2 * TILE + start : 2 * TILE + start + BLOCK
                        ]


def column_spec(rows, row_block=0):
    return pl.BlockSpec((rows, TILE), lambda i, s: (row_block, i))


def first_pack(raw, time_table, members, noise_buckets):
    layers = time_table.shape[0]
    buckets = jnp.broadcast_to(noise_buckets.astype(bf16), (layers, BLOCK))
    chunks = [(2 + 1 + index, layer, 0) for index in range(6) for layer in range(layers)]
    bias_chunks = members[6].shape[1] // BLOCK
    chunks += [(2 + 1 + 6, layer, part) for layer in range(layers) for part in range(bias_chunks)]
    chunks.append((2 + 1 + 7, 0, 0))
    per_tile = TILE // BLOCK

    def body(place, ins, outs, _):
        raw_tile("attention", ins[:2], outs)
        for tile in range(4):

            @pl.when(pl.program_id(0) == tile)
            def _(tile=tile):
                start = (tile % 2) * 16
                outs[0][BLOCK : BLOCK + 16, :] = ins[2][tile // 2, start : start + 16, :]
                for slot in range(per_tile):
                    index = tile * per_tile + slot
                    at = slot * BLOCK
                    row = jnp.zeros((1, BLOCK), bf16)
                    if index < len(chunks):
                        array, layer, part = chunks[index]
                        row = ins[array][layer : layer + 1, part * BLOCK : (part + 1) * BLOCK]
                    outs[0][BLOCK + 16 :, at : at + BLOCK] = jnp.broadcast_to(row.astype(f32), (16, BLOCK)).astype(bf16)

    return run(
        body,
        4,
        raw_inputs("attention", 0, raw)
        + [(time_table, None)]
        + [(member, None) for member in members]
        + [(buckets, None)],
        [((BLOCK + EXTRA, 4 * TILE), bf16, column_spec(BLOCK + EXTRA))],
    )[0]


def other_packs(kinds, raws, deps=()):
    inputs, counts = [], []
    for (kind, layer), raw in zip(kinds, raws):
        inputs += raw_inputs(kind, layer, raw)
        counts.append(len(raw))

    def body(place, ins, outs, _):
        at = 0
        for position, ((kind, _), taken) in enumerate(zip(kinds, counts)):
            raw_tile(kind, ins[at : at + taken], [outs[0].at[position * BLOCK : (position + 1) * BLOCK]])
            at += taken

    rows = len(kinds) * BLOCK
    return run(body, 4, inputs, [((rows, 4 * TILE), bf16, column_spec(rows))], deps=deps)[0]


def own_rows(rest, position, rows, deps=()):
    def body(place, ins, outs, _):
        outs[0][...] = ins[0][...]
        outs[1][...] = ins[0][...]

    out = ((rows, 4 * TILE), bf16, column_spec(BLOCK))
    return run(body, 4, [(rest, column_spec(BLOCK, position))], [out, out], deps=deps)


def diagonal_rows(x, y, buffers, deps=()):
    def body(place, ins, outs, _):
        outs[0][...] = ins[1][...]
        outs[1][...] = ins[0][...]

    rows, block = (buffers[0].shape[0], BLOCK // HALF) if buffers else (HALF, 0)

    def spec(at):
        return pl.BlockSpec((HALF, 4 * TILE), lambda i, s: (at, 0))

    out = ((rows, 4 * TILE), bf16, spec(block))
    return run(body, 1, [(x, spec(1)), (y, spec(0))], [out, out], deps=deps, aliases=buffers)


def first_step(rest, x, y, deps=()):
    half = EXTRA // 2

    def body(place, ins, outs, _):
        from_x, from_y, own = ins
        for out, source, at in ((outs[0], from_y, 0), (outs[1], from_x, 1)):
            out[:BLOCK, :] = own[...]
            out[BLOCK : BLOCK + HALF, :] = source[at * HALF : (at + 1) * HALF, :]
            out[BLOCK + HALF :, :] = source[BLOCK + at * half : BLOCK + (at + 1) * half, :]

    rows = BLOCK + HALF + half
    out = ((rows, 4 * TILE), bf16, column_spec(rows))
    whole = column_spec(x.shape[0])
    return run(body, 4, [(x, whole), (y, whole), (rest, column_spec(BLOCK))], [out, out], deps=deps)


class Gather:
    def __init__(self, kinds, raws, time_table, members, noise_buckets):
        self.count = len(kinds)
        self.first = first_pack(raws[0], time_table, members, noise_buckets)
        self.xs, self.ys = [swap(self.first, 2)], [swap(self.first, 4)]
        self.core_first = swap(self.first, 1)
        self.kinds, self.raws = kinds, raws
        self.core_xs, self.core_ys = [], []

    def others(self, deps):
        self.rest = other_packs(self.kinds[1:], self.raws[1:], deps)
        self.ready = tuple(own_rows(self.rest, 1, BLOCK + HALF))
        return self.ready[0]

    def prepare(self, deps=()):
        step = len(self.xs)
        self.ready = ()
        if step < self.count:
            self.ready = tuple(own_rows(self.rest, step - 1, BLOCK + HALF, deps))
            return self.ready[0]
        return deps[0]

    def step(self, deps=(), token=None):
        step = len(self.xs)
        if step == 2:
            deps = (self.core_rest,) + tuple(deps)
        if step > 1:
            deps = (self.core_xs[-1], self.core_ys[-1]) + tuple(deps)
            on_x, on_y = diagonal_rows(self.xs[-1], self.ys[-1], self.ready, deps)
        else:
            on_x, on_y = first_step(self.rest, self.xs[-1], self.ys[-1], deps)
            self.core_rest = swap(after(self.rest, on_x), 1)
        self.cross(on_x if token is None else token)
        self.xs.append(swap(on_x, 2))
        self.ys.append(swap(on_y, 4))
        return on_x

    def cross(self, token):
        self.core_xs.append(swap(after(self.xs[-1], token), 1))
        self.core_ys.append(swap(after(self.ys[-1], token), 1))

    def pack(self, k):
        row = 2 if k + 1 < self.count else 0
        own = [(self.first, 0, BLOCK), (self.core_first, 0, BLOCK)] if k == 0 else [(self.rest, k - 1, BLOCK), (self.core_rest, k - 1, BLOCK)]
        sides = (self.xs, self.core_xs, self.ys, self.core_ys)
        return (
            own
            + [(side[k], 0, BLOCK) for side in sides]
            + [(sides[i][k + 1], row, HALF) for i in (0, 2, 1, 3)]
        )

    def extras(self):
        whole = [(self.first, BLOCK, EXTRA), (self.core_first, BLOCK, EXTRA)]
        whole += [(side[0], BLOCK, EXTRA) for side in (self.xs, self.core_xs, self.ys, self.core_ys)]
        at, rows = BLOCK + HALF, EXTRA // 2
        parts = [
            [(self.xs[1], at, rows), (self.ys[1], at, rows)],
            [(self.core_xs[1], at, rows), (self.core_ys[1], at, rows)],
        ]
        return [[piece] for piece in whole] + parts


def vectors_of(extras, members, layers, table_rows, width):
    share = members[6].shape[1]
    bias_at, bucket_at = 6 * layers * BLOCK, 6 * layers * BLOCK + layers * share
    pieces = [piece for parts in extras for piece in parts]
    tables, rows_at, at = [], [], 0
    for parts in extras:
        tables.append(at)
        rows_at.append((at + len(parts) - 1, 0 if len(parts) == 2 else EXTRA // 2))
        at += len(parts)

    def body(place, ins, outs, _):
        me = place[0]
        row = [ins[at][start : start + 16, :].astype(f32)[0:1, :] for at, start in rows_at]
        mine = (me // 2) * 2 + place[1] // 2 == me
        bucket = jnp.where(mine, row[0][:, bucket_at : bucket_at + 1], row[1][:, bucket_at : bucket_at + 1])
        for layer in range(layers):
            scaling = jnp.ones((1, width), f32)
            for part in range(SMALL):
                owner = me ^ part
                for member in range(6):
                    start = (member * layers + layer) * BLOCK
                    outs[2 * layer][member : member + 1, block_at(place, part)] = row[part][:, start : start + BLOCK]
                start = bias_at + layer * share
                outs[2 * layer + 1][:, pl.ds(pl.multiple_of(owner * share, BLOCK), share)] = row[part][
                    :, start : start + share
                ]
                for half in range(2):
                    block = ins[tables[part]][0:16, (2 * layer + half) * TILE : (2 * layer + half + 1) * TILE].astype(f32)
                    place_of = lax.broadcasted_iota(jnp.int32, block.shape, 0) + (owner * table_rows + half * 16)
                    hit = place_of.astype(f32) == bucket
                    scaling += jnp.sum(jnp.where(hit, block, 0.0), axis=0, keepdims=True)
            outs[2 * layer][6:7, :] = scaling
            outs[2 * layer][7:8, :] = jnp.zeros((1, width), f32)
        for part in range(SMALL):
            outs[2 * layers][pl.ds(me ^ part, 1), :] = row[part][:, bucket_at : bucket_at + BLOCK]

    result = run(
        body,
        1,
        [
            (array, pl.BlockSpec((rows, 4 * TILE), lambda i, s, r=start // rows: (r, 0)))
            for array, start, rows in pieces
        ],
        [
            item
            for _ in range(layers)
            for item in (((8, width), f32, None), ((1, SMALL * share), f32, None))
        ]
        + [((SMALL, BLOCK), f32, None)],
    )
    pairs = [(result[2 * layer], result[2 * layer + 1]) for layer in range(layers)]
    return pairs, result[2 * layers][:, 0].astype(jnp.int32)


def small_and_changes(sums):
    columns = []
    for early, late, hidden_sum in sums:
        for member in (early[0], early[1], late[3], late[0], late[1], late[4], hidden_sum[0]):
            columns.append(member.reshape(SMALL * 4, -1))
    small = jnp.concatenate(columns, axis=1)
    changes = jnp.concatenate([early[2] + late[2] for early, late, _ in sums])
    return small.reshape((2, 2, 2, 2, 2, -1)), changes[None]


def cross(small, changes, axis, mine, move, add, *tokens):
    leaving = lax.dynamic_index_in_dim(small, 1 - mine, axis, keepdims=False)
    staying = lax.dynamic_index_in_dim(small, mine, axis, keepdims=False)
    moved = move(jnp.concatenate([leaving.reshape(-1), changes.reshape(-1)]))
    if tokens:
        moved = after(moved, *tokens)
    small = staying + moved[: leaving.size].reshape(leaving.shape)
    arrived = moved[leaving.size :].reshape(changes.shape)
    return small, changes + arrived if add else jnp.concatenate([changes, arrived], axis=0)


def fast_device(
    inputs,
    noise_buckets,
    first_gain,
    first_shift,
    attention_in,
    attention_out,
    attention_bias,
    second_gain,
    second_shift,
    expand_weight,
    expand_bias,
    reduce_weight,
    reduce_bias,
    time_table,
    cotangent,
):
    layers, width = first_gain.shape[0], inputs.shape[-1]
    count, planes = lax.axis_size("dp"), lax.axis_size("seq")
    me, plane = lax.axis_index("dp"), lax.axis_index("seq")
    sequence = (me // 2) * 2 + plane // 2

    kinds = [(kind, layer) for layer in range(layers) for kind in ("attention", "expand", "reduce")]
    raw_of = {"attention": (attention_in, attention_out), "expand": (expand_weight,), "reduce": (reduce_weight,)}
    members = (first_gain, first_shift, attention_bias, second_gain, second_shift, reduce_bias, expand_bias)
    gather = Gather(kinds, [raw_of[kind] for kind, _ in kinds], time_table, members, noise_buckets)
    moved = lax.ppermute(inputs[0], ("dp", "seq"), layout_moves(False))
    grad_low = lax.ppermute(cotangent[0], ("dp", "seq"), layout_moves(False))
    lower = (grad_low, swap(grad_low, 1))
    token = gather.others((moved, gather.first))
    gather.step((moved, lower[1], token))
    gather.step()
    vectors, buckets = vectors_of(gather.extras(), members, layers, time_table.shape[1], width)

    saved = []
    stream = moved
    normed = first_norm(stream, vectors[0][0])
    for layer in range(layers):
        vec, bias = vectors[layer]
        attention_pack = gather.pack(3 * layer)
        own_keys = project(normed, attention_pack, 1, 2, (token,) if layer else ())
        chunks = spread_keys(own_keys)
        queries = project(normed, attention_pack, 0, 1, (own_keys,))
        token = gather.step((gather.prepare((queries,)), queries), queries)
        if layer == 0:
            token = gather.prepare((token,))
        mixture, tops = attend_fast(queries, chunks, (token,))
        if layer == 0:
            token = gather.step((mixture,), mixture)
            token = gather.prepare((token,))
        else:
            gather.cross(mixture)
            token = mixture
        packs = (attention_pack, gather.pack(3 * layer + 1), gather.pack(3 * layer + 2))
        next_vec = vectors[layer + 1][0] if layer + 1 < layers else None
        middle, own_kept, slope, result, following = feed_forward(
            normed, mixture, packs, stream, vec, bias, next_vec, (token,)
        )
        if layer == 0:
            token = gather.step((following,), following)
        saved.append([stream, own_kept, queries, chunks, tops, middle, slope, packs])
        stream, normed = result, following
    outputs = lax.ppermute(following, ("dp", "seq"), layout_moves(True))

    grad = grad_low
    block = 0
    sums = [None] * layers
    shares = {}
    for entry in reversed(saved):
        entry[1] = (entry[1], swap(after(entry[1], following), 1))
    above = None
    for layer in reversed(range(layers)):
        vec, bias = vectors[layer]
        stream, kept, queries, chunks, tops, middle, slope, packs = saved[layer]
        of_reduce = Reduction(reduce_group(kept, lower, block), True)
        deps = (token,) if above is not None else ()
        *own_back, expand_bias_grad, middle_grad, late_sums, mixture_grad = feed_forward_back(
            grad, (lower[0], block), slope, middle, packs, vec, deps
        )
        back = [(own, swap(own, 1)) for own in own_back]
        deps = tuple(other for _, other in back)
        if above is None:
            token = advance([of_reduce], deps=(own_back[0], saved[0][1][1]))
        else:
            upper_reduce, upper_expand, of_attention = above
            token = advance([of_attention], deps=(own_back[0], outputs, upper_reduce.share))
            token = advance(fourths=[upper_expand], deps=(token,))
            token = advance([of_reduce], deps=(token,) + deps)
            deps = ()
        query_grad, near, near_leave, far, far_leave = attend_fast_back(
            queries, chunks, kept[0], mixture_grad, tops, (token,) + deps
        )
        far_leave, near_leave = swap(far_leave, 1), swap(near_leave, 1)
        of_expand = Reduction(expand_group(kept, back))
        token = query_grad
        if above is None:
            token = advance([of_expand], deps=(token,))
            token = advance(thirds=[of_reduce], deps=(token,))
        else:
            token = advance(thirds=[of_attention], deps=(token, upper_expand.share))
        far, near_leave = after(far, token, near_leave), after(near_leave, token)
        far = (wide(far) + wide(far_leave)).astype(bf16)
        far = (far, swap_seq(far, 1))
        token = far[0]
        if above is not None:
            token = advance(thirds=[of_reduce], deps=(token,))
            token = advance([of_expand], deps=(token, of_attention.second_x, of_attention.second_y))
        deps = (token,)
        if above is not None:
            deps = (token, of_reduce.second_x, of_reduce.second_y)
        grad, own_lower, early_sums, key_grad = first_back(
            query_grad, (near, near_leave, far[1]), packs[0], stream, middle_grad, vec, deps
        )
        lower, block = (own_lower, swap(own_lower, 1)), 1
        key_grad = (key_grad, swap(key_grad, 1))
        deps = (own_lower,)
        if above is None:
            deps = (own_lower,)
        if above is None:
            token = advance(thirds=[of_expand], fourths=[of_reduce], deps=deps)
        if above is not None:
            shares[("attention", layer + 1)] = of_attention
            shares[("expand", layer + 1)] = upper_expand
        upper_attention = of_attention if above is not None else None
        of_attention = Reduction(attention_group(kept, back, lower, key_grad))
        shares[("reduce", layer)] = of_reduce
        above = (of_reduce, of_expand, of_attention)
        sums[layer] = (early_sums, late_sums, expand_bias_grad)

    of_reduce, of_expand, of_last = above
    small, changes = small_and_changes(sums)
    small, changes = cross(small, changes, 4, plane % 2, lambda a: swap_seq(a, 1), True)
    small, changes = cross(small, changes, 3, plane // 2, lambda a: swap_seq(a, 2), False)
    token = advance(thirds=[of_expand], deps=(own_lower, small, changes))
    token = advance([of_last], deps=(token,))
    token = advance(fourths=[upper_attention, of_reduce], deps=(token,))
    token = advance(thirds=[of_last], deps=(token, upper_attention.share))
    input_grad = lax.ppermute(after(own_lower[:, TILE:], token), ("dp", "seq"), layout_moves(True)).astype(f32)
    token = advance(joint=(of_expand, of_last), deps=(token,))
    shares[("attention", 0)] = of_last
    shares[("expand", 0)] = of_expand
    shares = {name: reduction.share.astype(f32) for name, reduction in shares.items()}

    small, changes = after(small, token), after(changes, token)
    small, changes = cross(small, changes, 2, me % 2, lambda a: swap(a, 1), True)
    small, changes = cross(small, changes, 1, (me // 2) % 2, lambda a: swap(a, 2), False)
    small, changes = cross(small, changes, 0, me // 4, lambda a: swap(a, 4), False)
    row = small.reshape(-1)
    small_out, start = [[] for _ in range(7)], 0
    for layer in range(layers):
        for member in range(7):
            size = (width if member < 6 else 4 * width) // (count * planes)
            small_out[member].append(row[start : start + size])
            start += size
    small_out = [jnp.stack(member) for member in small_out]
    entries = jnp.arange(count)
    owners = 2 * ((me // 2) ^ (entries // 2)) + ((plane // 2) ^ (entries % 2))
    source_buckets = jnp.sum(jnp.where(owners[:, None] == entries[None, :], buckets[None, :], 0), axis=1)
    table_grad = chosen_rows(changes, source_buckets, layers, width)

    ins, outs, expands, reduces = [], [], [], []
    for layer in range(layers):
        share = shares[("attention", layer)]
        pairs = share[:, width : 3 * width].reshape(share.shape[0], width // BLOCK, 2, BLOCK)
        ins.append(
            jnp.concatenate(
                [share[:, :width], pairs[:, :, 0].reshape(-1, width), pairs[:, :, 1].reshape(-1, width)], axis=1
            )
        )
        outs.append(share[:, 3 * width :])
        expands.append(shares[("expand", layer)])
        reduces.append(shares[("reduce", layer)])
    return (
        outputs[None],
        input_grad[None],
        small_out[0],
        small_out[1],
        jnp.stack(ins),
        jnp.stack(outs),
        small_out[2],
        small_out[3],
        small_out[4],
        jnp.stack(expands),
        small_out[6],
        jnp.stack(reduces),
        small_out[5],
        table_grad,
    )


def on_device(
    inputs,
    noise_buckets,
    first_gain,
    first_shift,
    attention_in,
    attention_out,
    attention_bias,
    second_gain,
    second_shift,
    expand_weight,
    expand_bias,
    reduce_weight,
    reduce_bias,
    time_table,
    cotangent,
):
    layers = first_gain.shape[0]
    count, planes = lax.axis_size("dp"), lax.axis_size("seq")
    me, plane = lax.axis_index("dp"), lax.axis_index("seq")
    model_width = inputs.shape[-1]
    table_rows = time_table.shape[1]

    stream = lax.ppermute(inputs[0], ("dp", "seq"), layout_moves(False)).astype(f32)

    sequence = (me // 2) * 2 + plane // 2
    packs = []
    for layer in range(layers):
        rows = [
            time_table[layer],
            pack_small(
                [
                    member[layer]
                    for member in (
                        first_gain,
                        first_shift,
                        attention_bias,
                        second_gain,
                        second_shift,
                        reduce_bias,
                        expand_bias,
                    )
                ],
                WIDE,
            ),
            jnp.broadcast_to(noise_buckets.astype(bf16)[:, None], (1, model_width)),
        ]
        packs.append(jnp.concatenate(rows, axis=0))

    def unpack(pack):
        stacked, sources, _ = gather_small(pack, ("dp",))
        slot = me ^ jnp.arange(count) if count == SMALL else jnp.arange(count)
        per_pack = stacked.shape[1]
        flat = stacked.reshape(count * per_pack, model_width)

        def place(index):
            return (me ^ index) if count == SMALL else index

        buckets = jnp.stack(
            [lax.dynamic_index_in_dim(flat, place(index) * per_pack + per_pack - 1, 0, False)[0] for index in range(count)]
        ).astype(jnp.int32)
        bucket = lax.dynamic_index_in_dim(buckets, sequence, 0, False)
        row = place(bucket // table_rows) * per_pack + bucket % table_rows
        scaling = lax.dynamic_slice_in_dim(flat, row, 1, 0).astype(f32)
        vectors = jnp.stack(
            [
                lax.dynamic_slice_in_dim(
                    flat, place(index) * per_pack + table_rows, per_pack - 1 - table_rows, 0
                ).reshape(-1)
                for index in range(count)
            ]
        ).astype(f32)
        share = model_width // count
        members = [vectors[:, i * share : (i + 1) * share].reshape(1, -1) for i in range(6)]
        members.append(vectors[:, 6 * share : 6 * share + expand_bias.shape[1]].reshape(1, -1))
        return tuple(members) + (scaling,), buckets

    keys_at = model_width
    shards = []
    for layer in range(layers):
        shards += [
            attention_in[layer][:, keys_at:],
            attention_in[layer][:, :keys_at],
            attention_out[layer],
            expand_weight[layer],
            reduce_weight[layer],
        ]
    gathered = []
    for position, shard in enumerate(shards):
        if count == SMALL and position >= 2:
            shard = after(shard, gathered[position - 2][2], gathered[position - 2][4])
        gathered.append(gather_rows(shard, position % 2))

    all_vectors, buckets = [], None
    for layer in range(layers):
        vectors, buckets = unpack(packs[layer])
        all_vectors.append(vectors)

    saved, all_weights = [], []
    for layer in range(layers):
        w_keys, w_query, w_out, w_expand, w_reduce = gathered[5 * layer : 5 * layer + 5]
        weights = (w_query, w_keys, w_out, w_expand, w_reduce)
        all_weights.append(weights)
        stream, kept = layer_forward(stream, weights, all_vectors[layer])
        saved.append(kept)
    back_moves = layout_moves(True)
    outputs = lax.ppermute(stream.astype(bf16), ("dp", "seq"), back_moves)[None]

    grad_flow = lax.ppermute(cotangent[0], ("dp", "seq"), layout_moves(False)).astype(f32)
    dense, small, modulation = [None] * layers, [None] * layers, [None] * layers
    for layer in reversed(range(layers)):
        grad_flow, dense[layer], small[layer], modulation[layer] = layer_backward(
            saved[layer], all_weights[layer], all_vectors[layer], grad_flow
        )
    input_grad = lax.ppermute(grad_flow, ("dp", "seq"), back_moves)[None]

    devices = count * planes
    packed = jnp.concatenate(
        [member.reshape(devices, -1) for layer in range(layers) for member in small[layer]], axis=1
    )
    row = scatter_small(packed)
    small_out, start = [[] for _ in range(7)], 0
    for layer in range(layers):
        for member in range(7):
            width = small[layer][member].size // devices
            small_out[member].append(row[start : start + width])
            start += width
    small_out = [jnp.stack(member) for member in small_out]

    changes, from_dp, from_seq = gather_small(jnp.concatenate(modulation), ("dp", "seq"))
    table_grad = table_rows_of(changes, from_dp, from_seq, buckets, layers, model_width)

    dense_out = [jnp.stack([dense[layer][member] for layer in range(layers)]) for member in range(4)]
    return (
        outputs,
        input_grad,
        small_out[0],
        small_out[1],
        dense_out[0],
        dense_out[1],
        small_out[2],
        small_out[3],
        small_out[4],
        dense_out[2],
        small_out[6],
        dense_out[3],
        small_out[5],
        table_grad,
    )


def solution(mesh):
    eight_way = mesh.shape["dp"] == SMALL and mesh.shape["seq"] == 4
    return jax.shard_map(
        fast_device if eight_way else on_device,
        mesh=mesh,
        in_specs=(
            P("dp", "seq", None),
            P("dp"),
            P(None, "dp"),
            P(None, "dp"),
            P(None, "dp", None),
            P(None, "dp", None),
            P(None, "dp"),
            P(None, "dp"),
            P(None, "dp"),
            P(None, "dp", None),
            P(None, "dp"),
            P(None, "dp", None),
            P(None, "dp"),
            P(None, "dp", None),
            P("dp", "seq", None),
        ),
        out_specs=(
            P("dp", "seq", None),
            P("dp", "seq", None),
            P(None, ("dp", "seq")),
            P(None, ("dp", "seq")),
            P(None, ("dp", "seq"), None),
            P(None, ("dp", "seq"), None),
            P(None, ("dp", "seq")),
            P(None, ("dp", "seq")),
            P(None, ("dp", "seq")),
            P(None, ("dp", "seq"), None),
            P(None, ("dp", "seq")),
            P(None, ("dp", "seq"), None),
            P(None, ("dp", "seq")),
            P(None, ("dp", "seq"), None),
        ),
        check_vma=False,
    )
```

```python
import functools
import math

import jax
import jax.numpy as jnp
from jax import lax
from jax.experimental import pallas as pl
from jax.experimental.pallas import tpu as pltpu
from jax.sharding import PartitionSpec as P

HEAD = 64
BUCKETS = 256
SMALL = 8
WIDE = 1024

epsilon = 1e-05
bf16 = jnp.bfloat16
f32 = jnp.float32


def modulated_norm(activations, norm_gain, norm_shift, scaling):
    center = activations - jnp.mean(activations, axis=-1, keepdims=True)
    spread = jnp.mean(center * center, axis=-1, keepdims=True)
    return (center * lax.rsqrt(spread + epsilon) * norm_gain + norm_shift) * (1.0 + scaling)


def swap(array, bit):
    count = lax.axis_size("dp")
    return lax.ppermute(array, "dp", [(i, i ^ bit) for i in range(count)])


def swap_seq(array, bit):
    count = lax.axis_size("seq")
    return lax.ppermute(array, "seq", [(i, i ^ bit) for i in range(count)])


def after(array, *earlier):
    return lax.optimization_barrier((array,) + earlier)[0]


def layout_moves(back):
    moves = []
    for index in range(lax.axis_size("dp")):
        core, pair = index % 2, index - index % 2
        for plane in range(4):
            source = index * 4 + plane
            target = (pair + plane % 2) * 4 + 2 * core + plane // 2
            moves.append((target, source) if back else (source, target))
    return moves


def gather_rows(shard, route):
    if lax.axis_size("dp") != SMALL:
        return lax.all_gather(shard, "dp", axis=0, tiled=True)
    along_x = swap(shard, 2)
    along_y = swap(shard, 4)
    across = swap(along_x, 4) if route == 0 else swap(along_y, 2)
    mine = [shard, along_x, along_y, across]
    parts = []
    for part in mine:
        parts += [part, swap(part, 1)]
    return parts


def order_of(parts):
    me = lax.axis_index("dp")
    return [me ^ bit for bit in range(parts)]


def scatter_dense(left, right, orders):
    count, planes = lax.axis_size("dp"), lax.axis_size("seq")
    rows, columns = left.shape[1], right.shape[1]
    if count != SMALL:
        whole = jnp.einsum("tr,tc->rc", left, right, preferred_element_type=f32)
        return lax.psum_scatter(whole, ("dp", "seq"), scatter_dimension=0, tiled=True)
    me, plane = lax.axis_index("dp"), lax.axis_index("seq")
    block = rows // count
    width = columns // len(orders)

    def pick(masks):
        return jnp.concatenate(
            [lax.dynamic_slice_in_dim(left, (me ^ mask) * block, block, 1) for mask in masks], axis=1
        )

    def product(a, b):
        return jnp.einsum("tr,tc->rc", a, b, preferred_element_type=f32)

    pieces = []
    for position, (first, second) in enumerate(orders):
        part = right[:, position * width : (position + 1) * width]
        masks = [first | second, first, second, 0]
        arrived = swap(product(pick([mask | 1 for mask in masks]), part).astype(bf16), 1)
        half = 2 * block
        leaving = (product(pick(masks[:2]), part) + arrived[:half].astype(f32)).astype(bf16)
        staying = (product(pick(masks[2:]), part) + arrived[half:].astype(f32)).astype(bf16)
        arrived = swap(leaving, first)
        leaving = (staying[:block].astype(f32) + arrived[:block].astype(f32)).astype(bf16)
        staying = (staying[block:].astype(f32) + arrived[block:].astype(f32)).astype(bf16)
        arrived = swap(leaving, second)
        pieces.append((staying, arrived))
    total = jnp.concatenate([(a.astype(f32) + b.astype(f32)).astype(bf16) for a, b in pieces], axis=1)
    return scatter_planes(total, plane, planes)


def scatter_planes(total, plane, planes):
    rows, columns = total.shape
    low, high = plane & 1, plane >> 1
    cut = total.reshape(2, 2, rows // planes, columns)
    arrived = swap_seq(lax.dynamic_index_in_dim(cut, 1 - low, 1, keepdims=False), 1)
    kept = lax.dynamic_index_in_dim(cut, low, 1, keepdims=False)
    joined = kept.astype(f32) + arrived.astype(f32)
    arrived = swap_seq(lax.dynamic_index_in_dim(joined, 1 - high, 0, keepdims=False).astype(bf16), 2)
    return lax.dynamic_index_in_dim(joined, high, 0, keepdims=False) + arrived.astype(f32)


def scatter_small(array):
    count, planes = lax.axis_size("dp"), lax.axis_size("seq")
    if count != SMALL:
        return lax.psum_scatter(array, ("dp", "seq"), scatter_dimension=0, tiled=True)[0]
    me, plane = lax.axis_index("dp"), lax.axis_index("seq")
    columns = array.shape[1]
    shape = [count, planes]
    current = array.reshape(shape[0], shape[1], columns)
    for axis, index, send in ((0, me, swap), (1, plane, swap_seq)):
        bit = 1
        while current.shape[axis] > 1:
            pairs = current.shape[axis] // 2
            view = jnp.moveaxis(current, axis, 0).reshape(pairs, 2, -1, columns)
            mine = (index // bit) % 2
            leaving = lax.dynamic_index_in_dim(view, 1 - mine, 1, keepdims=False)
            staying = lax.dynamic_index_in_dim(view, mine, 1, keepdims=False)
            current = jnp.moveaxis((staying + send(leaving, bit)).reshape(pairs, -1, columns), 0, axis)
            bit *= 2
    return current.reshape(columns)


def gather_small(array, axes):
    if lax.axis_size("dp") != SMALL:
        stacked = lax.all_gather(array, axes, axis=0, tiled=False)
        stacked = stacked.reshape((-1,) + array.shape)
        places = jnp.arange(stacked.shape[0])
        if "seq" in axes:
            planes = lax.axis_size("seq")
            return stacked, places // planes, places % planes
        return stacked, places, None
    current = array[None]
    me = lax.axis_index("dp")
    for bit in (1, 2, 4):
        current = jnp.concatenate([current, swap(current, bit)], axis=0)
    sources = me ^ jnp.arange(SMALL)
    if "seq" not in axes:
        return current, sources, None
    plane = lax.axis_index("seq")
    for bit in (1, 2):
        current = jnp.concatenate([current, swap_seq(current, bit)], axis=0)
    places = jnp.arange(SMALL * 4)
    return current, me ^ (places % SMALL), plane ^ (places // SMALL)


def times(a, weight, out_type):
    return jnp.dot(a, weight, preferred_element_type=f32).astype(out_type)


def times_transposed(a, weight, out_type):
    return lax.dot_general(a, weight, (((1,), (1,)), ((), ())), preferred_element_type=f32).astype(out_type)


def spread_keys(own):
    far = swap_seq(own, 1)
    return [own, swap(own, 1), far, swap(far, 1)]


def heads_of(rows):
    return rows.reshape(rows.shape[0], rows.shape[1] // HEAD, HEAD)


def attend(queries, chunks):
    model_width = queries.shape[1]
    whole = jnp.concatenate(chunks, axis=0)
    key_heads, value_heads = heads_of(whole[:, :model_width]), heads_of(whole[:, model_width:])
    scores = jnp.einsum("qhd,khd->hqk", heads_of(queries), key_heads, preferred_element_type=f32)
    scores = scores * (1.0 / math.sqrt(HEAD))
    exponent = jnp.exp(scores - jnp.max(scores, axis=-1, keepdims=True))
    probs = exponent / jnp.sum(exponent, axis=-1, keepdims=True)
    probs_low = probs.astype(bf16)
    mixture = jnp.einsum("hqk,khd->qhd", probs_low, value_heads, preferred_element_type=f32)
    return mixture.reshape(queries.shape).astype(bf16), (probs, probs_low)


def attend_back(queries, chunks, kept, mixture, mixture_grad):
    probs, probs_low = kept
    model_width = queries.shape[1]
    factor = 1.0 / math.sqrt(HEAD)
    whole = jnp.concatenate(chunks, axis=0)
    key_heads, value_heads = heads_of(whole[:, :model_width]), heads_of(whole[:, model_width:])
    grad_heads = heads_of(mixture_grad)
    prob_grad = jnp.einsum("qhd,khd->hqk", grad_heads, value_heads, preferred_element_type=f32)
    along = jnp.sum(probs * prob_grad, axis=-1, keepdims=True)
    score_grad = (probs * (prob_grad - along)).astype(bf16)
    query_grad = jnp.einsum("hqk,khd->qhd", score_grad, key_heads, preferred_element_type=f32)
    query_grad = (query_grad * factor).astype(bf16).reshape(queries.shape)
    key_part = jnp.einsum("hqk,qhd->khd", score_grad, heads_of(queries), preferred_element_type=f32)
    value_part = jnp.einsum("hqk,qhd->khd", probs_low, grad_heads, preferred_element_type=f32)
    parts = jnp.concatenate(
        [
            (key_part * factor).reshape(whole.shape[0], model_width),
            value_part.reshape(whole.shape[0], model_width),
        ],
        axis=1,
    ).astype(bf16)
    return query_grad, parts


def join_key_grads(parts):
    local = parts.shape[0] // 4
    cut = [parts[i * local : (i + 1) * local] for i in range(4)]
    far = cut[2].astype(f32) + swap(cut[3], 1).astype(f32)
    far = swap_seq(far.astype(bf16), 1)
    near = cut[0].astype(f32) + swap(cut[1], 1).astype(f32)
    return (near + far.astype(f32)).astype(bf16)


def layer_forward(stream, weights, vectors):
    w_query, w_keys, w_out, w_expand, w_reduce = weights
    first_gain, first_shift, attention_bias, second_gain, second_shift, reduce_bias, expand_bias, scaling = vectors
    normed = modulated_norm(stream, first_gain, first_shift, scaling).astype(bf16)
    chunks = spread_keys(times(normed, w_keys, bf16))
    queries = times(normed, w_query, bf16)
    mixture, kept = attend(queries, chunks)
    middle = stream + (times(mixture, w_out, f32) + attention_bias)
    second = modulated_norm(middle, second_gain, second_shift, scaling).astype(bf16)
    hidden = times(second, w_expand, f32) + expand_bias
    active = jax.nn.gelu(hidden).astype(bf16)
    result = middle + (times(active, w_reduce, f32) + reduce_bias)
    return result, (stream, normed, queries, chunks, kept, mixture, middle, second, hidden, active)


def layer_backward(saved, weights, vectors, grad_out):
    w_query, w_keys, w_out, w_expand, w_reduce = weights
    first_gain, first_shift, attention_bias, second_gain, second_shift, reduce_bias, expand_bias, scaling = vectors
    stream, normed, queries, chunks, kept, mixture, middle, second, hidden, active = saved
    both = ((2, 4), (4, 2))
    grad_low = grad_out.astype(bf16)
    reduce_bias_grad = jnp.sum(grad_out, axis=0)
    reduce_weight_grad = scatter_dense(active, grad_low, both)
    active_grad = times_transposed(grad_low, w_reduce, f32)
    hidden_grad = jax.vjp(jax.nn.gelu, hidden)[1](active_grad)[0]
    expand_bias_grad = jnp.sum(hidden_grad, axis=0)
    hidden_low = hidden_grad.astype(bf16)
    second_grad = times_transposed(hidden_low, w_expand, f32)
    expand_weight_grad = scatter_dense(second, hidden_low, both)
    _, second_back = jax.vjp(modulated_norm, middle, second_gain, second_shift, scaling)
    middle_part, second_gain_grad, second_shift_grad, second_scaling_grad = second_back(second_grad)
    middle_grad = grad_out + middle_part
    attention_bias_grad = jnp.sum(middle_grad, axis=0)
    middle_low = middle_grad.astype(bf16)
    mixture_grad = times_transposed(middle_low, w_out, bf16)
    attention_out_grad = scatter_dense(mixture, middle_low, both)
    query_grad, parts = attend_back(queries, chunks, kept, mixture, mixture_grad)
    key_grad = join_key_grads(parts)
    normed_grad = times_transposed(query_grad, w_query, f32) + times_transposed(key_grad, w_keys, f32)
    project_grad = jnp.concatenate([query_grad, key_grad], axis=1)
    attention_in_grad = scatter_dense(normed, project_grad, both)
    _, first_back = jax.vjp(modulated_norm, stream, first_gain, first_shift, scaling)
    stream_part, first_gain_grad, first_shift_grad, first_scaling_grad = first_back(normed_grad)
    stream_grad = middle_grad + stream_part
    small = (
        first_gain_grad,
        first_shift_grad,
        attention_bias_grad,
        second_gain_grad,
        second_shift_grad,
        reduce_bias_grad,
        expand_bias_grad,
    )
    dense = (attention_in_grad, attention_out_grad, expand_weight_grad, reduce_weight_grad)
    return stream_grad, dense, small, (first_scaling_grad + second_scaling_grad)[0]


def pack_small(vectors, rows):
    flat = jnp.concatenate([vector.reshape(-1) for vector in vectors])
    length = -(-flat.shape[0] // WIDE) * WIDE
    return jnp.pad(flat, (0, length - flat.shape[0])).reshape(-1, WIDE)


def table_rows_of(changes, from_dp, from_seq, buckets, layers, model_width):
    count, planes = lax.axis_size("dp"), lax.axis_size("seq")
    owners = (from_dp // 2) * 2 + from_seq // 2
    source_buckets = jnp.sum(
        jnp.where(owners[:, None] == jnp.arange(count)[None, :], buckets[None, :], 0), axis=1
    )
    return chosen_rows(changes, source_buckets, layers, model_width)


def chosen_rows(changes, source_buckets, layers, model_width):
    count, planes = lax.axis_size("dp"), lax.axis_size("seq")
    table_share = BUCKETS // (count * planes)
    first_row = (lax.axis_index("dp") * planes + lax.axis_index("seq")) * table_share
    chosen = (source_buckets[None, :] == (first_row + jnp.arange(table_share))[:, None]).astype(f32)
    table_grad = jnp.dot(chosen, changes, precision=lax.Precision.HIGHEST)
    return jnp.stack(
        [table_grad[:, layer * model_width : (layer + 1) * model_width] for layer in range(layers)]
    )


VMEM_LIMIT = 64_000 * 1024
TILE = 1024
BLOCK = 128
NT = (((1,), (1,)), ((), ()))
TN = (((0,), (0,)), ((), ()))


def whole_spec(array):
    zeros = (0,) * len(array.shape)
    return pl.BlockSpec(array.shape, lambda *_: zeros)


def run(body, grid, inputs, outputs, scratch=(), deps=(), aliases=(), cost=4):
    deps = tuple(aliases) + tuple(deps)
    arrays = [array for array, _ in inputs]
    specs = [spec if spec is not None else whole_spec(array) for array, spec in inputs]
    shapes = [jax.ShapeDtypeStruct(shape, kind) for shape, kind, _ in outputs]
    out_specs = [
        spec if spec is not None else whole_spec(shape) for shape, (_, _, spec) in zip(shapes, outputs)
    ]
    count, extra = len(arrays), len(deps)

    def kernel(place, *refs):
        body(place, refs[:count], refs[count + extra : count + extra + len(shapes)], refs[count + extra + len(shapes) :])

    place = jnp.stack([lax.axis_index("dp"), lax.axis_index("seq")]).astype(jnp.int32)
    return pl.pallas_call(
        kernel,
        out_shape=shapes,
        grid_spec=pltpu.PrefetchScalarGridSpec(
            num_scalar_prefetch=1,
            grid=(grid,),
            in_specs=specs + [pl.BlockSpec(memory_space=pl.ANY)] * extra,
            out_specs=out_specs,
            scratch_shapes=list(scratch),
        ),
        input_output_aliases={1 + count + i: i for i in range(len(aliases))},
        compiler_params=pltpu.CompilerParams(vmem_limit_bytes=VMEM_LIMIT),
        cost_estimate=pl.CostEstimate(flops=0, bytes_accessed=cost * 3_000_000, transcendentals=0),
    )(place, *arrays, *deps)


class Flow:
    def __init__(self, sems):
        self.sems, self.count, self.pending = sems, 0, {}

    def start(self, key, source, target):
        copy = pltpu.make_async_copy(source, target, self.sems.at[self.count])
        self.count += 1
        copy.start()
        self.pending.setdefault(key, []).append(copy)

    def wait(self, key):
        for copy in self.pending.pop(key):
            copy.wait()

    def drain(self):
        for key in list(self.pending):
            self.wait(key)

    def pack(self, key, pack, refs, target, first, columns):
        at = 0
        for (_, block, rows), ref in zip(pack, refs):
            self.start(
                key,
                ref.at[pl.ds(block * rows, rows), pl.ds(first, columns)],
                target.at[pl.ds(at, rows), :] if target.shape[1] == columns else target.at[pl.ds(at, rows), pl.ds(first, columns)],
            )
            at += rows


def run_flow(body, arrays, packs, outputs, scratch, copies, deps=(), cost=8):
    buffers = [buffer for pack in packs for buffer, _, _ in pack]
    count, extra, made = len(arrays), len(buffers), len(outputs)

    def kernel(place, *refs):
        outs = refs[count + extra + len(deps) :][:made]
        held = refs[count + extra + len(deps) + made : -1]
        weights, at = [], count
        for pack in packs:
            weights.append(refs[at : at + len(pack)])
            at += len(pack)
        body(place, Flow(refs[-1]), refs[:count], weights, outs, held)

    place = jnp.stack([lax.axis_index("dp"), lax.axis_index("seq")]).astype(jnp.int32)
    anywhere = pl.BlockSpec(memory_space=pl.ANY)
    return pl.pallas_call(
        kernel,
        out_shape=[jax.ShapeDtypeStruct(shape, kind) for shape, kind in outputs],
        in_specs=[pl.BlockSpec(memory_space=pltpu.SMEM)] + [anywhere] * (count + extra + len(deps)),
        out_specs=[anywhere] * made,
        scratch_shapes=[pltpu.VMEM(shape, kind) for shape, kind in scratch] + [pltpu.SemaphoreType.DMA((copies,))],
        compiler_params=pltpu.CompilerParams(vmem_limit_bytes=VMEM_LIMIT),
        cost_estimate=pl.CostEstimate(flops=0, bytes_accessed=cost * 3_000_000, transcendentals=0),
    )(place, *arrays, *buffers, *deps)


def join(refs):
    return jnp.concatenate([ref[...] for ref in refs], axis=0)


def block_at(place, part, stride=BLOCK, offset=0):
    return pl.ds(pl.multiple_of((place[0] ^ part) * stride + offset, BLOCK), BLOCK)


def columns_in_order(place, ref, stride=BLOCK, offset=0):
    return jnp.concatenate(
        [ref[:, block_at(place, part, stride, offset)] for part in range(SMALL)], axis=1
    )


def normalise(v):
    center = v - jnp.mean(v, axis=-1, keepdims=True)
    inverse = lax.rsqrt(jnp.mean(center * center, axis=-1, keepdims=True) + epsilon)
    return center * inverse, inverse


def modulated(v, vec, gain_row):
    unit, _ = normalise(v)
    return (unit * vec[gain_row : gain_row + 1, :] + vec[gain_row + 1 : gain_row + 2, :]) * vec[6:7, :]


def modulated_back(v, vec, gain_row, grad):
    unit, inverse = normalise(v)
    gain, shift, scale = vec[gain_row : gain_row + 1, :], vec[gain_row + 1 : gain_row + 2, :], vec[6:7, :]
    scale_grad = jnp.sum(grad * (unit * gain + shift), axis=0, keepdims=True)
    inner = grad * scale
    gain_grad = jnp.sum(inner * unit, axis=0, keepdims=True)
    shift_grad = jnp.sum(inner, axis=0, keepdims=True)
    inner = inner * gain
    back = inverse * (
        inner
        - jnp.mean(inner, axis=-1, keepdims=True)
        - unit * jnp.mean(inner * unit, axis=-1, keepdims=True)
    )
    return back, gain_grad, shift_grad, scale_grad


ROOT = math.sqrt(2.0 / math.pi)
CUBIC = 0.044715


def first_norm(x, vec, deps=()):
    def body(place, ins, outs, _):
        outs[0][...] = modulated(ins[0][...].astype(f32), ins[1], 0).astype(bf16)

    return run(body, 1, [(x, None), (vec, None)], [(x.shape, bf16, None)], deps=deps)[0]


def project(a, pack, first_tile, tiles, deps=()):
    tokens, width = a.shape

    def body(place, flow, ins, packs, outs, scratch):
        a_ref, weights, result, ordered = scratch
        flow.start("a", ins[0], a_ref)
        for tile in range(tiles):
            flow.pack(tile, pack, packs[0], weights.at[tile], (first_tile + tile) * TILE, TILE)
        flow.wait("a")
        ordered[...] = columns_in_order(place, a_ref)
        for tile in range(tiles):
            flow.wait(tile)
            at = pl.ds(tile * TILE, TILE)
            result[:, at] = jnp.dot(ordered[...], weights[tile], preferred_element_type=f32).astype(bf16)
            flow.start("out", result.at[:, at], outs[0].at[:, at])
        flow.drain()

    return run_flow(
        body,
        [a],
        [pack],
        [((tokens, tiles * TILE), bf16)],
        [(a.shape, bf16), ((tiles, width, TILE), bf16), ((tokens, tiles * TILE), bf16), (a.shape, bf16)],
        1 + tiles * (len(pack) + 1),
        deps,
        4,
    )[0]


def key_specs(chunks):
    return [
        (chunk, pl.BlockSpec((chunk.shape[0], 4 * HEAD), lambda i, s: (0, i))) for chunk in chunks
    ]


def head_masks(rows):
    lane = lax.broadcasted_iota(jnp.int32, (rows, 2 * HEAD), 1)
    return lane < HEAD, lane >= HEAD


def attend_fast(queries, chunks, deps=()):
    tokens, width = queries.shape
    pairs = width // (2 * HEAD)

    def body(place, ins, outs, _):
        both = join(ins[1:5])
        keys, values = both[:, : 2 * HEAD], both[:, 2 * HEAD :]
        scaled = ins[0][...] * jnp.asarray(1.0 / math.sqrt(HEAD), bf16)
        halves, tops = [], []
        for head, mask in enumerate(head_masks(tokens)):
            query = jnp.where(mask, scaled, jnp.zeros_like(scaled))
            scores = lax.dot_general(keys, query, NT, preferred_element_type=f32)
            most = jnp.max(scores, axis=0, keepdims=True)
            exponent = jnp.exp(scores - most)
            total = jnp.sum(exponent, axis=0, keepdims=True)
            mixed = lax.dot_general(values, exponent.astype(bf16), TN, preferred_element_type=f32)
            halves.append(mixed[head * HEAD : (head + 1) * HEAD] / total)
            tops.append(most + jnp.log(total))
        outs[0][...] = jnp.concatenate(halves, axis=0).T.astype(bf16)
        outs[1][0, 0:1, :] = tops[0]
        outs[1][0, 1:2, :] = tops[1]

    return run(
        body,
        pairs,
        [(queries, pl.BlockSpec((tokens, 2 * HEAD), lambda i, s: (0, i)))] + key_specs(chunks),
        [
            (queries.shape, bf16, pl.BlockSpec((tokens, 2 * HEAD), lambda i, s: (0, i))),
            ((pairs, 8, tokens), f32, pl.BlockSpec((1, 8, tokens), lambda i, s: (i, 0, 0))),
        ],
        deps=deps,
        cost=15,
    )


def attend_fast_back(queries, chunks, kept, mixture_grad, tops, deps=()):
    tokens, width = queries.shape
    pairs = width // (2 * HEAD)

    def body(place, ins, outs, _):
        both = join(ins[1:5])
        keys, values = both[:, : 2 * HEAD], both[:, 2 * HEAD :]
        scaled = ins[0][...] * jnp.asarray(1.0 / math.sqrt(HEAD), bf16)
        grads = ins[6][...]
        masks = head_masks(tokens)
        select = jnp.concatenate([mask[0:1].astype(f32) for mask in masks] + [jnp.zeros((6, 2 * HEAD), f32)], axis=0)
        along = lax.dot_general(
            select,
            ins[5][...].astype(f32) * grads.astype(f32),
            NT,
            precision=lax.Precision.HIGHEST,
            preferred_element_type=f32,
        )
        key_grad = value_grad = None
        halves = []
        for head, mask in enumerate(masks):
            query = jnp.where(mask, scaled, jnp.zeros_like(scaled))
            grad = jnp.where(mask, grads, jnp.zeros_like(grads))
            scores = lax.dot_general(keys, query, NT, preferred_element_type=f32)
            probs = jnp.exp(scores - ins[7][0, head : head + 1, :])
            prob_grad = lax.dot_general(values, grad, NT, preferred_element_type=f32)
            score_grad = (probs * (prob_grad - along[head : head + 1, :])).astype(bf16)
            key_part = jnp.dot(score_grad, query, preferred_element_type=f32)
            value_part = jnp.dot(probs.astype(bf16), grad, preferred_element_type=f32)
            key_grad = key_part if head == 0 else key_grad + key_part
            value_grad = value_part if head == 0 else value_grad + value_part
            query_part = lax.dot_general(keys, score_grad, TN, preferred_element_type=f32)
            halves.append(query_part[head * HEAD : (head + 1) * HEAD])
        query_grad = jnp.concatenate(halves, axis=0) * (1.0 / math.sqrt(HEAD))
        outs[0][...] = query_grad.T.astype(bf16)
        for chunk in range(4):
            rows = slice(chunk * tokens, (chunk + 1) * tokens)
            outs[1 + chunk][:, : 2 * HEAD] = key_grad[rows].astype(bf16)
            outs[1 + chunk][:, 2 * HEAD :] = value_grad[rows].astype(bf16)

    pair_spec = pl.BlockSpec((tokens, 2 * HEAD), lambda i, s: (0, i))
    part = ((tokens, 2 * width), bf16, pl.BlockSpec((tokens, 4 * HEAD), lambda i, s: (0, i)))
    return run(
        body,
        pairs,
        [(queries, pair_spec)]
        + key_specs(chunks)
        + [
            (kept, pl.BlockSpec((tokens, 2 * HEAD), lambda i, s: (0, MIXTURE // (2 * HEAD) + i))),
            (mixture_grad, pair_spec),
            (tops, pl.BlockSpec((1, 8, tokens), lambda i, s: (i, 0, 0))),
        ],
        [(queries.shape, bf16, pair_spec)] + [part] * 4,
        deps=deps,
        cost=18,
    )


ACTIVE, SECOND, MIXTURE, NORMED, KEPT = 0, 4 * TILE, 5 * TILE, 6 * TILE, 7 * TILE


def columns(tile, count=1):
    return pl.ds(tile * TILE, count * TILE)


def feed_forward(normed, mixture, packs, stream, vec, bias, next_vec, deps=()):
    tokens, width = mixture.shape
    hidden_width = bias.shape[1]
    half = 2 * TILE

    def body(place, flow, ins, weights, outs, scratch):
        (mixture_ref, stream_ref, vec_ref, next_ref, bias_ref, kept, w_out, w_expand, w_reduce) = scratch[:9]
        (middle, slope, result, following, ordered) = scratch[9:]
        flow.start("first", ins[0], mixture_ref)
        flow.start("first", ins[2], vec_ref)
        flow.pack("out", packs[0], weights[0], w_out, 3 * TILE, TILE)
        flow.start("out", ins[1], stream_ref)
        flow.start("out", ins[4], bias_ref)
        for number in range(2):
            flow.pack(f"expand{number}", packs[1], weights[1], w_expand, number * half, half)
        flow.start("normed", ins[5], kept.at[:, pl.ds(NORMED, TILE)])
        flow.start("next", ins[3], next_ref)
        for number in range(2):
            flow.pack(f"reduce{number}", packs[2], weights[2], w_reduce, number * half, half)

        flow.wait("first")
        kept[:, MIXTURE:NORMED] = mixture_ref[...]
        ordered[...] = columns_in_order(place, mixture_ref)
        flow.wait("out")
        branch = jnp.dot(ordered[...], w_out[...], preferred_element_type=f32)
        middle[...] = stream_ref[...].astype(f32) + (branch + vec_ref[2:3, :])
        flow.start("middle", middle, outs[0])
        kept[:, SECOND:MIXTURE] = modulated(middle[...], vec_ref, 3).astype(bf16)
        ordered[...] = columns_in_order(place, kept, BLOCK, SECOND)
        for tile in range(4):
            if tile % 2 == 0:
                flow.wait(f"expand{tile // 2}")
            at = columns(tile)
            hidden = jnp.dot(ordered[...], w_expand[:, at], preferred_element_type=f32) + bias_ref[:, at]
            square = hidden * hidden
            bent = jnp.tanh(ROOT * hidden * (1.0 + CUBIC * square))
            share = 0.5 * (1.0 + bent)
            kept[:, at] = (hidden * share).astype(bf16)
            steep = share + (0.5 * ROOT) * hidden * (1.0 - bent * bent) * (1.0 + (3.0 * CUBIC) * square)
            slope[:, at] = steep.astype(bf16)
            if tile == 1:
                flow.start("slope", slope.at[:, columns(0, 2)], outs[2].at[:, columns(0, 2)])
        flow.start("slope", slope.at[:, columns(2, 2)], outs[2].at[:, columns(2, 2)])
        flow.wait("normed")
        flow.start("kept", kept, outs[1])
        for tile in range(4):
            if tile % 2 == 0:
                flow.wait(f"reduce{tile // 2}")
            a = columns_in_order(place, kept, 4 * BLOCK, tile * BLOCK)
            product = jnp.dot(a, w_reduce[:, columns(tile)], preferred_element_type=f32)
            result[...] = product if tile == 0 else result[...] + product
        result[...] = middle[...] + (result[...] + vec_ref[5:6, :])
        flow.start("result", result, outs[3])
        flow.wait("next")
        if next_vec is None:
            following[...] = result[...].astype(bf16)
        else:
            following[...] = modulated(result[...], next_ref, 0).astype(bf16)
        flow.start("following", following, outs[4])
        flow.drain()

    wide_shape = (tokens, hidden_width)
    rows = SMALL * BLOCK
    return run_flow(
        body,
        [mixture, stream, vec, vec if next_vec is None else next_vec, bias, normed],
        packs,
        [(mixture.shape, f32), ((tokens, KEPT), bf16), (wide_shape, bf16), (mixture.shape, f32), (mixture.shape, bf16)],
        [
            (mixture.shape, bf16),
            (stream.shape, stream.dtype),
            (vec.shape, f32),
            (vec.shape, f32),
            (bias.shape, f32),
            ((tokens, KEPT), bf16),
            ((rows, TILE), bf16),
            ((rows, hidden_width), bf16),
            ((rows, hidden_width), bf16),
            (mixture.shape, f32),
            (wide_shape, bf16),
            (mixture.shape, f32),
            (mixture.shape, bf16),
            (mixture.shape, bf16),
        ],
        6 + 5 * len(packs[0]) + 6,
        deps,
        12,
    )


def feed_forward_back(grad, grad_low, slope, middle, packs, vec, deps=()):
    tokens, width = grad.shape
    hidden_width = slope.shape[1]
    low, low_block = grad_low
    half = 2 * TILE

    def body(place, flow, ins, weights, outs, scratch):
        (grad_ref, low_ref, slope_ref, middle_ref, vec_ref, w_out, w_expand, w_reduce) = scratch[:8]
        (hidden, bias, middle_grad, middle_low, sums, mixture, total, ordered) = scratch[8:]
        flow.start("low", ins[1].at[:, columns(low_block)], low_ref)
        flow.pack("reduce0", packs[2], weights[2], w_reduce, 0, half)
        flow.start("slope", ins[2], slope_ref)
        flow.pack("reduce1", packs[2], weights[2], w_reduce, half, half)
        for number in range(2):
            flow.pack(f"expand{number}", packs[1], weights[1], w_expand, number * half, half)
        flow.start("norm", ins[3], middle_ref)
        flow.start("norm", ins[4], vec_ref)
        flow.start("norm", ins[0], grad_ref)
        flow.pack("out", packs[0], weights[0], w_out, 3 * TILE, TILE)

        flow.wait("low")
        for tile in range(4):
            if tile % 2 == 0:
                flow.wait(f"reduce{tile // 2}")
            product = lax.dot_general(low_ref[...], w_reduce[:, columns(tile)], NT, preferred_element_type=f32)
            if tile == 0:
                flow.wait("slope")
            for part in range(SMALL):
                at = block_at(place, part, 4 * BLOCK, tile * BLOCK)
                piece = product[:, part * BLOCK : (part + 1) * BLOCK] * slope_ref[:, at].astype(f32)
                hidden[:, at] = piece.astype(bf16)
                bias[:, at] = jnp.sum(piece, axis=0, keepdims=True)
        flow.start("hidden", hidden.at[:, columns(0, 2)], outs[0])
        flow.start("hidden", hidden.at[:, columns(2, 2)], outs[1])
        flow.start("bias", bias, outs[3])
        for tile in range(4):
            if tile % 2 == 0:
                flow.wait(f"expand{tile // 2}")
            product = lax.dot_general(
                hidden[:, columns(tile)], w_expand[:, columns(tile)], NT, preferred_element_type=f32
            )
            total[...] = product if tile == 0 else total[...] + product
        for part in range(SMALL):
            ordered[:, block_at(place, part)] = total[:, part * BLOCK : (part + 1) * BLOCK]
        flow.wait("norm")
        back, gain_grad, shift_grad, scale_grad = modulated_back(middle_ref[...], vec_ref, 3, ordered[...])
        upstream = grad_ref[...].astype(f32)
        middle_grad[...] = upstream + back
        middle_low[...] = middle_grad[...].astype(bf16)
        flow.start("middle", middle_low, outs[2])
        flow.start("middle", middle_grad, outs[4])
        flow.wait("out")
        product = lax.dot_general(middle_low[...], w_out[...], NT, preferred_element_type=f32).astype(bf16)
        for part in range(SMALL):
            mixture[:, block_at(place, part)] = product[:, part * BLOCK : (part + 1) * BLOCK]
        flow.start("mixture", mixture, outs[6])
        sums[0:1, :] = gain_grad
        sums[1:2, :] = shift_grad
        sums[2:3, :] = scale_grad
        sums[3:4, :] = jnp.sum(middle_grad[...], axis=0, keepdims=True)
        sums[4:5, :] = jnp.sum(upstream, axis=0, keepdims=True)
        sums[5:8, :] = jnp.zeros((3, width), f32)
        flow.start("sums", sums, outs[5])
        flow.drain()

    rows = SMALL * BLOCK
    return run_flow(
        body,
        [grad, low, slope, middle, vec],
        packs,
        [
            ((tokens, half), bf16),
            ((tokens, half), bf16),
            (grad.shape, bf16),
            ((1, hidden_width), f32),
            (grad.shape, f32),
            ((8, width), f32),
            (grad.shape, bf16),
        ],
        [
            (grad.shape, grad.dtype),
            (grad.shape, bf16),
            (slope.shape, bf16),
            (middle.shape, f32),
            (vec.shape, f32),
            ((rows, TILE), bf16),
            ((rows, hidden_width), bf16),
            ((rows, hidden_width), bf16),
            (slope.shape, bf16),
            ((1, hidden_width), f32),
            (grad.shape, f32),
            (grad.shape, bf16),
            ((8, width), f32),
            (grad.shape, bf16),
            (grad.shape, f32),
            (grad.shape, f32),
        ],
        5 + 5 * len(packs[0]) + 7,
        deps,
        12,
    )


def first_back(query_grad, key_parts, pack, stream, middle_grad, vec, deps=()):
    tokens, width = stream.shape
    shape = key_parts[0].shape

    def body(place, flow, ins, weights, outs, scratch):
        (lower, near_ref, leave_ref, far_ref, stream_ref, middle_ref, vec_ref, w_in) = scratch[:8]
        (key_ref, grad_ref, sums, total, ordered) = scratch[8:]
        flow.start("query", ins[0], lower.at[:, columns(0)])
        flow.pack("w0", pack, weights[0], w_in, 0, TILE)
        for source, target in zip(ins[1:4], (near_ref, leave_ref, far_ref)):
            flow.start("keys", source, target)
        flow.pack("w1", pack, weights[0], w_in, TILE, 2 * TILE)
        for source, target in zip(ins[4:7], (stream_ref, middle_ref, vec_ref)):
            flow.start("norm", source, target)
        flow.wait("query")
        flow.wait("w0")
        total[...] = lax.dot_general(lower[:, columns(0)], w_in[:, columns(0)], NT, preferred_element_type=f32)
        flow.wait("keys")
        key_ref[...] = (
            near_ref[...].astype(f32) + leave_ref[...].astype(f32) + far_ref[...].astype(f32)
        ).astype(bf16)
        flow.start("key", key_ref, outs[3])
        flow.wait("w1")
        total[...] += lax.dot_general(key_ref[...], w_in[:, columns(1, 2)], NT, preferred_element_type=f32)
        for part in range(SMALL):
            ordered[:, block_at(place, part)] = total[:, part * BLOCK : (part + 1) * BLOCK]
        flow.wait("norm")
        back, gain_grad, shift_grad, scale_grad = modulated_back(
            stream_ref[...].astype(f32), vec_ref, 0, ordered[...]
        )
        grad_ref[...] = middle_ref[...] + back
        lower[:, columns(1)] = grad_ref[...].astype(bf16)
        flow.start("lower", lower, outs[1])
        flow.start("grad", grad_ref, outs[0])
        sums[0:1, :] = gain_grad
        sums[1:2, :] = shift_grad
        sums[2:3, :] = scale_grad
        sums[3:8, :] = jnp.zeros((5, width), f32)
        flow.start("sums", sums, outs[2])
        flow.drain()

    rows = SMALL * BLOCK
    return run_flow(
        body,
        [query_grad, *key_parts, stream, middle_grad, vec],
        [pack],
        [(stream.shape, f32), ((tokens, 2 * TILE), bf16), ((8, width), f32), (shape, bf16)],
        [
            ((tokens, 2 * TILE), bf16),
            (shape, bf16),
            (shape, bf16),
            (shape, bf16),
            (stream.shape, stream.dtype),
            (stream.shape, f32),
            (vec.shape, f32),
            ((rows, 3 * TILE), bf16),
            (shape, bf16),
            (stream.shape, f32),
            ((8, width), f32),
            (stream.shape, f32),
            (stream.shape, f32),
        ],
        7 + 2 * len(pack) + 4,
        deps,
        6,
    )


ORDERS = ((6, 2, 4, 0), (6, 4, 2, 0))


class Group:
    def __init__(self, arrays, left_of, right_of):
        self.arrays, self.left_of, self.right_of = arrays, left_of, right_of

    def left(self, place, refs, tile):
        array, stride, offset = self.left_of[tile]
        return jnp.concatenate(
            [refs[array][:, block_at(place, mask, stride, offset)] for mask in ORDERS[tile // 2]], axis=1
        )

    def product(self, place, refs, tile):
        array, start = self.right_of[tile]
        return lax.dot_general(
            self.left(place, refs, tile), refs[array][:, start : start + TILE], TN, preferred_element_type=f32
        )


def reduce_group(kept, lower, block):
    return Group(
        [(lower, block * TILE, TILE), (kept, ACTIVE, 4 * TILE)],
        [(1, 4 * BLOCK, u * BLOCK) for u in range(4)],
        [(0, 0)] * 4,
    )


def expand_group(kept, back):
    return Group(
        [(kept, SECOND, TILE), (back[0], 0, 2 * TILE), (back[1], 0, 2 * TILE)],
        [(0, BLOCK, 0)] * 4,
        [(1, 0), (1, TILE), (2, 0), (2, TILE)],
    )


def attention_group(kept, back, lower, key_grad):
    return Group(
        [
            (kept, NORMED, TILE),
            (lower, 0, TILE),
            (key_grad, 0, 2 * TILE),
            (kept, MIXTURE, TILE),
            (back[2], 0, TILE),
        ],
        [(0, BLOCK, 0)] * 3 + [(3, BLOCK, 0)],
        [(1, 0), (2, 0), (2, TILE), (4, 0)],
    )


def wide(value):
    return value.astype(f32)


class Reduction:
    def __init__(self, group, stacked=False):
        self.group, self.stacked = group, stacked

    def scatter(self, *tokens):
        piece = after(self.piece, *tokens) if tokens else self.piece
        self.share = lax.psum_scatter(piece, "seq", scatter_dimension=0, tiled=True)


def advance(seconds=(), thirds=(), fourths=(), joint=(), deps=(), later=False):
    arrays, outputs, scratch, loads, works = [], [], [], [], []
    half = 2 * TILE
    quarter, eighth = (2 * BLOCK, half), (BLOCK, half)

    def bring(array, shape, source, target=lambda ref: ref, key=None):
        number = len(loads)
        slot = len(scratch) if shape is not None else len(scratch) - 1
        if shape is not None:
            scratch.append((shape, array.dtype))
        loads.append((len(arrays), slot, source, target, number if key is None else key))
        arrays.append(array)
        return slot, number

    def make(shape):
        outputs.append((shape, bf16))
        scratch.append((shape, bf16))
        return len(outputs) - 1, len(scratch) - 1

    for one in seconds:
        group, slots, keys = one.group, [], []
        for pair, first, width in group.arrays:
            tokens = pair[0].shape[0]
            for side, array in enumerate(pair):
                slot, key = bring(
                    array,
                    (2 * tokens, width) if side == 0 else None,
                    lambda ref, first=first, width=width: ref.at[:, pl.ds(first, width)],
                    lambda ref, side=side, tokens=tokens: ref.at[pl.ds(side * tokens, tokens), :],
                )
                keys.append(key)
            slots.append(slot)
        made = [make(quarter), make(quarter), make((2,) + quarter)]

        def product(place, flow, held, outs, group=group, slots=slots, keys=keys, made=made):
            refs = [held[slot] for slot in slots]
            waited = 0
            stay = made[2]
            for tile in range(4):
                needed = 2 * (max(group.left_of[tile][0], group.right_of[tile][0]) + 1)
                while waited < needed:
                    flow.wait(keys[waited])
                    waited += 1
                total = group.product(place, refs, tile)
                leave = made[tile // 2]
                held[leave[1]][:, columns(tile % 2)] = total[: 2 * BLOCK].astype(bf16)
                held[stay[1]][tile // 2, :, columns(tile % 2)] = total[2 * BLOCK :].astype(bf16)
                if tile % 2:
                    flow.start("out", held[leave[1]], outs[leave[0]])
                    flow.start("out", held[stay[1]].at[tile // 2], outs[stay[0]].at[tile // 2])

        works.append(product)
    for one in thirds:
        loaded = [
            bring(one.staying, (2,) + quarter, lambda ref: ref),
            bring(one.from_x, quarter, lambda ref: ref),
            bring(one.from_y, quarter, lambda ref: ref),
        ]
        made = [make(eighth), make(eighth), make((2,) + eighth)]

        def add(place, flow, held, outs, loaded=loaded, made=made):
            flow.wait(loaded[0][1])
            for number in range(2):
                flow.wait(loaded[1 + number][1])
                total = (wide(held[loaded[0][0]][number]) + wide(held[loaded[1 + number][0]][...])).astype(bf16)
                held[made[number][1]][...] = total[:BLOCK]
                held[made[2][1]][number] = total[BLOCK:]
                flow.start("out", held[made[number][1]], outs[made[number][0]])
                flow.start("out", held[made[2][1]].at[number], outs[made[2][0]].at[number])

        works.append(add)
    sums = [[one] for one in fourths] + ([list(joint)] if joint else [])
    for members in sums:
        alone = len(members) == 1
        stacked = alone and members[0].stacked
        loaded = [
            [
                bring(one.kept, (2,) + eighth, lambda ref: ref),
                bring(one.second_y, eighth, lambda ref: ref),
                bring(one.second_x, eighth, lambda ref: ref),
            ]
            for one in members
        ]
        made = make((4 * BLOCK, TILE) if stacked else (len(members) * BLOCK, 4 * TILE))

        def finish(place, flow, held, outs, loaded=loaded, made=made, stacked=stacked, alone=alone):
            result, share = held[made[1]], BLOCK // 4
            for number, (kept, *arrived) in enumerate(loaded):
                flow.wait(kept[1])
                for side in range(2):
                    flow.wait(arrived[side][1])
                    total = (wide(held[kept[0]][side]) + wide(held[arrived[side][0]][...])).astype(bf16)
                    if stacked:
                        for tile in range(2):
                            at = (2 * side + tile) * BLOCK
                            result[at : at + BLOCK, :] = total[:, tile * TILE : (tile + 1) * TILE]
                    elif alone:
                        result[:, columns(2 * side, 2)] = total
                    else:
                        for plane in range(4):
                            start = (plane * len(loaded) + number) * share
                            result[start : start + share, columns(2 * side, 2)] = total[
                                plane * share : (plane + 1) * share
                            ]
            flow.start("out", result, outs[made[0]])

        works.append(finish)

    def body(place, flow, ins, _, outs, held):
        for number, slot, source, target, key in loads:
            flow.start(key, source(ins[number]), target(held[slot]))
        for work in works:
            work(place, flow, held, outs)
        flow.drain()

    results = list(run_flow(body, arrays, [], outputs, scratch, len(loads) + 2 * len(outputs) + 2, deps, 7 if seconds else 4))
    token = results[-1] if joint and len(works) == 1 else results[0]
    for one in seconds:
        along_x, along_y, one.staying = results[:3]
        results = results[3:]
        one.from_x, one.from_y = swap(along_x, 2), swap(along_y, 4)
    for one in thirds:
        along_y, along_x, one.kept = results[:3]
        results = results[3:]
        one.second_y, one.second_x = swap(along_y, 4), swap(along_x, 2)
    for one in fourths:
        one.piece = results[0]
        results = results[1:]
        if not later:
            one.scatter()
    if joint:
        both = lax.psum_scatter(results[0], "seq", scatter_dimension=0, tiled=True)
        share = BLOCK // 4
        for number, one in enumerate(joint):
            one.share = both[number * share : (number + 1) * share]
    return token


HALF = BLOCK // 2
EXTRA = 32


def raw_inputs(kind, layer, arrays):
    if kind == "attention":
        return [
            (arrays[0], pl.BlockSpec((1,) + arrays[0].shape[1:], lambda i, s: (layer, 0, 0))),
            (arrays[1], pl.BlockSpec((1,) + arrays[1].shape[1:], lambda i, s: (layer, 0, 0))),
        ]
    if kind == "expand":
        return [(arrays[0], pl.BlockSpec((1, BLOCK, TILE), lambda i, s: (layer, 0, i)))]
    return [(arrays[0], pl.BlockSpec((1, BLOCK, TILE), lambda i, s: (layer, i, 0)))]


def raw_tile(kind, ins, targets):
    if kind != "attention":
        for target in targets:
            target[:BLOCK, :] = ins[0][0]
        return
    pairs = TILE // (2 * BLOCK)
    for tile in range(4):

        @pl.when(pl.program_id(0) == tile)
        def _(tile=tile):
            for target in targets:
                if tile == 0:
                    target[:BLOCK, :] = ins[0][0, :, :TILE]
                elif tile == 3:
                    target[:BLOCK, :] = ins[1][0]
                else:
                    for pair in range(pairs):
                        start = (pairs * (tile - 1) + pair) * BLOCK
                        at = pair * 2 * BLOCK
                        target[:BLOCK, at : at + BLOCK] = ins[0][0, :, TILE + start : TILE + start + BLOCK]
                        target[:BLOCK, at + BLOCK : at + 2 * BLOCK] = ins[0][
                            0, :, 2 * TILE + start : 2 * TILE + start + BLOCK
                        ]


def column_spec(rows, row_block=0):
    return pl.BlockSpec((rows, TILE), lambda i, s: (row_block, i))


def first_pack(raw, time_table, members, noise_buckets):
    layers = time_table.shape[0]
    buckets = jnp.broadcast_to(noise_buckets.astype(bf16), (layers, BLOCK))
    chunks = [(2 + 1 + index, layer, 0) for index in range(6) for layer in range(layers)]
    bias_chunks = members[6].shape[1] // BLOCK
    chunks += [(2 + 1 + 6, layer, part) for layer in range(layers) for part in range(bias_chunks)]
    chunks.append((2 + 1 + 7, 0, 0))
    per_tile = TILE // BLOCK

    def body(place, ins, outs, _):
        raw_tile("attention", ins[:2], outs)
        for tile in range(4):

            @pl.when(pl.program_id(0) == tile)
            def _(tile=tile):
                start = (tile % 2) * 16
                outs[0][BLOCK : BLOCK + 16, :] = ins[2][tile // 2, start : start + 16, :]
                for slot in range(per_tile):
                    index = tile * per_tile + slot
                    at = slot * BLOCK
                    row = jnp.zeros((1, BLOCK), bf16)
                    if index < len(chunks):
                        array, layer, part = chunks[index]
                        row = ins[array][layer : layer + 1, part * BLOCK : (part + 1) * BLOCK]
                    outs[0][BLOCK + 16 :, at : at + BLOCK] = jnp.broadcast_to(row.astype(f32), (16, BLOCK)).astype(bf16)

    return run(
        body,
        4,
        raw_inputs("attention", 0, raw)
        + [(time_table, None)]
        + [(member, None) for member in members]
        + [(buckets, None)],
        [((BLOCK + EXTRA, 4 * TILE), bf16, column_spec(BLOCK + EXTRA))],
    )[0]


def other_packs(kinds, raws, deps=()):
    inputs, counts = [], []
    for (kind, layer), raw in zip(kinds, raws):
        inputs += raw_inputs(kind, layer, raw)
        counts.append(len(raw))

    def body(place, ins, outs, _):
        at = 0
        for position, ((kind, _), taken) in enumerate(zip(kinds, counts)):
            raw_tile(kind, ins[at : at + taken], [outs[0].at[position * BLOCK : (position + 1) * BLOCK]])
            at += taken

    rows = len(kinds) * BLOCK
    return run(body, 4, inputs, [((rows, 4 * TILE), bf16, column_spec(rows))], deps=deps)[0]


def own_rows(rest, position, rows, deps=()):
    def body(place, ins, outs, _):
        outs[0][...] = ins[0][...]
        outs[1][...] = ins[0][...]

    out = ((rows, 4 * TILE), bf16, column_spec(BLOCK))
    return run(body, 4, [(rest, column_spec(BLOCK, position))], [out, out], deps=deps)


def diagonal_rows(x, y, buffers, deps=()):
    def body(place, ins, outs, _):
        outs[0][...] = ins[1][...]
        outs[1][...] = ins[0][...]

    rows, block = (buffers[0].shape[0], BLOCK // HALF) if buffers else (HALF, 0)

    def spec(at):
        return pl.BlockSpec((HALF, 4 * TILE), lambda i, s: (at, 0))

    out = ((rows, 4 * TILE), bf16, spec(block))
    return run(body, 1, [(x, spec(1)), (y, spec(0))], [out, out], deps=deps, aliases=buffers)


def first_step(rest, x, y, deps=()):
    half = EXTRA // 2

    def body(place, ins, outs, _):
        from_x, from_y, own = ins
        for out, source, at in ((outs[0], from_y, 0), (outs[1], from_x, 1)):
            out[:BLOCK, :] = own[...]
            out[BLOCK : BLOCK + HALF, :] = source[at * HALF : (at + 1) * HALF, :]
            out[BLOCK + HALF :, :] = source[BLOCK + at * half : BLOCK + (at + 1) * half, :]

    rows = BLOCK + HALF + half
    out = ((rows, 4 * TILE), bf16, column_spec(rows))
    whole = column_spec(x.shape[0])
    return run(body, 4, [(x, whole), (y, whole), (rest, column_spec(BLOCK))], [out, out], deps=deps)


class Gather:
    def __init__(self, kinds, raws, time_table, members, noise_buckets):
        self.count = len(kinds)
        self.first = first_pack(raws[0], time_table, members, noise_buckets)
        self.xs, self.ys = [swap(self.first, 2)], [swap(self.first, 4)]
        self.core_first = swap(self.first, 1)
        self.kinds, self.raws = kinds, raws
        self.core_xs, self.core_ys = [], []

    def others(self, deps):
        self.rest = other_packs(self.kinds[1:], self.raws[1:], deps)
        self.ready = tuple(own_rows(self.rest, 1, BLOCK + HALF))
        return self.ready[0]

    def prepare(self, deps=()):
        step = len(self.xs)
        self.ready = ()
        if step < self.count:
            self.ready = tuple(own_rows(self.rest, step - 1, BLOCK + HALF, deps))
            return self.ready[0]
        return deps[0]

    def step(self, deps=(), token=None):
        step = len(self.xs)
        if step == 2:
            deps = (self.core_rest,) + tuple(deps)
        if step > 1:
            deps = (self.core_xs[-1], self.core_ys[-1]) + tuple(deps)
            on_x, on_y = diagonal_rows(self.xs[-1], self.ys[-1], self.ready, deps)
        else:
            on_x, on_y = first_step(self.rest, self.xs[-1], self.ys[-1], deps)
            self.core_rest = swap(after(self.rest, on_x), 1)
        self.cross(on_x if token is None else token)
        self.xs.append(swap(on_x, 2))
        self.ys.append(swap(on_y, 4))
        return on_x

    def cross(self, token):
        self.core_xs.append(swap(after(self.xs[-1], token), 1))
        self.core_ys.append(swap(after(self.ys[-1], token), 1))

    def pack(self, k):
        row = 2 if k + 1 < self.count else 0
        own = [(self.first, 0, BLOCK), (self.core_first, 0, BLOCK)] if k == 0 else [(self.rest, k - 1, BLOCK), (self.core_rest, k - 1, BLOCK)]
        sides = (self.xs, self.core_xs, self.ys, self.core_ys)
        return (
            own
            + [(side[k], 0, BLOCK) for side in sides]
            + [(sides[i][k + 1], row, HALF) for i in (0, 2, 1, 3)]
        )

    def extras(self):
        whole = [(self.first, BLOCK, EXTRA), (self.core_first, BLOCK, EXTRA)]
        whole += [(side[0], BLOCK, EXTRA) for side in (self.xs, self.core_xs, self.ys, self.core_ys)]
        at, rows = BLOCK + HALF, EXTRA // 2
        parts = [
            [(self.xs[1], at, rows), (self.ys[1], at, rows)],
            [(self.core_xs[1], at, rows), (self.core_ys[1], at, rows)],
        ]
        return [[piece] for piece in whole] + parts


def vectors_of(extras, members, layers, table_rows, width):
    share = members[6].shape[1]
    bias_at, bucket_at = 6 * layers * BLOCK, 6 * layers * BLOCK + layers * share
    pieces = [piece for parts in extras for piece in parts]
    tables, rows_at, at = [], [], 0
    for parts in extras:
        tables.append(at)
        rows_at.append((at + len(parts) - 1, 0 if len(parts) == 2 else EXTRA // 2))
        at += len(parts)

    def body(place, ins, outs, _):
        me = place[0]
        row = [ins[at][start : start + 16, :].astype(f32)[0:1, :] for at, start in rows_at]
        mine = (me // 2) * 2 + place[1] // 2 == me
        bucket = jnp.where(mine, row[0][:, bucket_at : bucket_at + 1], row[1][:, bucket_at : bucket_at + 1])
        for layer in range(layers):
            scaling = jnp.ones((1, width), f32)
            for part in range(SMALL):
                owner = me ^ part
                for member in range(6):
                    start = (member * layers + layer) * BLOCK
                    outs[2 * layer][member : member + 1, block_at(place, part)] = row[part][:, start : start + BLOCK]
                start = bias_at + layer * share
                outs[2 * layer + 1][:, pl.ds(pl.multiple_of(owner * share, BLOCK), share)] = row[part][
                    :, start : start + share
                ]
                for half in range(2):
                    block = ins[tables[part]][0:16, (2 * layer + half) * TILE : (2 * layer + half + 1) * TILE].astype(f32)
                    place_of = lax.broadcasted_iota(jnp.int32, block.shape, 0) + (owner * table_rows + half * 16)
                    hit = place_of.astype(f32) == bucket
                    scaling += jnp.sum(jnp.where(hit, block, 0.0), axis=0, keepdims=True)
            outs[2 * layer][6:7, :] = scaling
            outs[2 * layer][7:8, :] = jnp.zeros((1, width), f32)
        for part in range(SMALL):
            outs[2 * layers][pl.ds(me ^ part, 1), :] = row[part][:, bucket_at : bucket_at + BLOCK]

    result = run(
        body,
        1,
        [
            (array, pl.BlockSpec((rows, 4 * TILE), lambda i, s, r=start // rows: (r, 0)))
            for array, start, rows in pieces
        ],
        [
            item
            for _ in range(layers)
            for item in (((8, width), f32, None), ((1, SMALL * share), f32, None))
        ]
        + [((SMALL, BLOCK), f32, None)],
    )
    pairs = [(result[2 * layer], result[2 * layer + 1]) for layer in range(layers)]
    return pairs, result[2 * layers][:, 0].astype(jnp.int32)


def small_and_changes(sums):
    columns = []
    for early, late, hidden_sum in sums:
        for member in (early[0], early[1], late[3], late[0], late[1], late[4], hidden_sum[0]):
            columns.append(member.reshape(SMALL * 4, -1))
    small = jnp.concatenate(columns, axis=1)
    changes = jnp.concatenate([early[2] + late[2] for early, late, _ in sums])
    return small.reshape((2, 2, 2, 2, 2, -1)), changes[None]


def cross(small, changes, axis, mine, move, add, *tokens):
    leaving = lax.dynamic_index_in_dim(small, 1 - mine, axis, keepdims=False)
    staying = lax.dynamic_index_in_dim(small, mine, axis, keepdims=False)
    moved = move(jnp.concatenate([leaving.reshape(-1), changes.reshape(-1)]))
    if tokens:
        moved = after(moved, *tokens)
    small = staying + moved[: leaving.size].reshape(leaving.shape)
    arrived = moved[leaving.size :].reshape(changes.shape)
    return small, changes + arrived if add else jnp.concatenate([changes, arrived], axis=0)


def relay(array, back):
    moves = layout_moves(back)
    moved = lax.ppermute(array, ("dp", "seq"), [(a, b) for a, b in moves if a != b])
    core, plane = lax.axis_index("dp") % 2, lax.axis_index("seq")
    return moved, lambda moved: jnp.where(plane == 3 * core, array, moved)


def fast_device(
    inputs,
    noise_buckets,
    first_gain,
    first_shift,
    attention_in,
    attention_out,
    attention_bias,
    second_gain,
    second_shift,
    expand_weight,
    expand_bias,
    reduce_weight,
    reduce_bias,
    time_table,
    cotangent,
):
    layers, width = first_gain.shape[0], inputs.shape[-1]
    count, planes = lax.axis_size("dp"), lax.axis_size("seq")
    me, plane = lax.axis_index("dp"), lax.axis_index("seq")
    sequence = (me // 2) * 2 + plane // 2

    kinds = [(kind, layer) for layer in range(layers) for kind in ("attention", "expand", "reduce")]
    raw_of = {"attention": (attention_in, attention_out), "expand": (expand_weight,), "reduce": (reduce_weight,)}
    members = (first_gain, first_shift, attention_bias, second_gain, second_shift, reduce_bias, expand_bias)
    gather = Gather(kinds, [raw_of[kind] for kind, _ in kinds], time_table, members, noise_buckets)
    moved, finish = relay(inputs[0], False)
    moved = finish(moved)
    token = gather.others((gather.first,))
    token = gather.step((moved, token))
    grad_low, finish = relay(after(cotangent[0], token), False)
    grad_low = finish(grad_low)
    gather.step((grad_low,))
    vectors, buckets = vectors_of(gather.extras(), members, layers, time_table.shape[1], width)

    saved = []
    stream = moved
    normed = first_norm(stream, vectors[0][0])
    for layer in range(layers):
        vec, bias = vectors[layer]
        attention_pack = gather.pack(3 * layer)
        own_keys = project(normed, attention_pack, 1, 2, (token,) if layer else ())
        chunks = spread_keys(own_keys)
        queries = project(normed, attention_pack, 0, 1, (own_keys,))
        token = gather.step((gather.prepare((queries,)), queries), queries)
        if layer == 0:
            token = gather.prepare((token,))
        mixture, tops = attend_fast(queries, chunks, (token,))
        if layer == 0:
            token = gather.step((mixture,), mixture)
            token = gather.prepare((token,))
        else:
            gather.cross(mixture)
            token = mixture
        packs = (attention_pack, gather.pack(3 * layer + 1), gather.pack(3 * layer + 2))
        next_vec = vectors[layer + 1][0] if layer + 1 < layers else None
        middle, own_kept, slope, result, following = feed_forward(
            normed, mixture, packs, stream, vec, bias, next_vec, (token,)
        )
        if layer == 0:
            token = gather.step((following,), following)
        saved.append([stream, own_kept, queries, chunks, tops, middle, slope, packs])
        stream, normed = result, following

    grad = grad_low
    lower, block = (grad_low, swap(after(grad_low, following), 1)), 0
    sums = [None] * layers
    shares = {}
    for entry in reversed(saved):
        entry[1] = (entry[1], swap(after(entry[1], following), 1))
    above = None
    for layer in reversed(range(layers)):
        vec, bias = vectors[layer]
        stream, kept, queries, chunks, tops, middle, slope, packs = saved[layer]
        of_reduce = Reduction(reduce_group(kept, lower, block), True)
        deps = ()
        if above is not None:
            upper_reduce, upper_expand, of_attention = above
            deps = (advance([of_attention], deps=(token,)),)
        *own_back, expand_bias_grad, middle_grad, late_sums, mixture_grad = feed_forward_back(
            grad, (lower[0], block), slope, middle, packs, vec, deps
        )
        if above is None:
            back = [(own, swap(own, 1)) for own in own_back]
            token = advance([of_reduce], deps=(own_back[0], saved[0][1][1]))
            deps = (token,) + tuple(other for _, other in back)
            moved_result, finish = relay(after(result, token), True)
            outputs = finish(lax.optimization_barrier(moved_result)).astype(bf16)
        else:
            deps = (upper_expand.second_x, upper_expand.second_y)
        query_grad, near, near_leave, far, far_leave = attend_fast_back(
            queries, chunks, kept[0], mixture_grad, tops, deps
        )
        far_leave, near_leave = swap(far_leave, 1), swap(near_leave, 1)
        token = query_grad
        if above is None:
            of_expand = Reduction(expand_group(kept, back))
            token = advance([of_expand], deps=(token,))
            token = advance(thirds=[of_reduce], deps=(token, moved_result))
        else:
            token = advance(thirds=[of_attention], deps=(token, upper_reduce.share))
        far, near_leave = after(far, token, near_leave), after(near_leave, token)
        far = (wide(far) + wide(far_leave)).astype(bf16)
        far = (far, swap_seq(far, 1))
        token = far[0]
        if above is not None:
            back = [(own, swap(after(own, token), 1)) for own in own_back[:2]]
            of_expand = Reduction(expand_group(kept, back))
            token = advance([of_reduce], deps=(token, back[0][1], back[1][1], of_attention.second_x, of_attention.second_y))
            token = advance([of_expand], deps=(token,))
        grad, own_lower, early_sums, key_grad = first_back(
            query_grad, (near, near_leave, far[1]), packs[0], stream, middle_grad, vec, (token,)
        )
        lower, block = (own_lower, swap(own_lower, 1)), 1
        key_grad = (key_grad, swap(key_grad, 1))
        if above is None:
            token = advance(thirds=[of_expand], fourths=[of_reduce], deps=(own_lower,))
        else:
            back.append((own_back[2], swap(after(own_back[2], own_lower), 1)))
            token = own_lower
            shares[("attention", layer + 1)] = of_attention
            shares[("expand", layer + 1)] = upper_expand
            upper_attention = of_attention
        of_attention = Reduction(attention_group(kept, back, lower, key_grad))
        shares[("reduce", layer)] = of_reduce
        above = (of_reduce, of_expand, of_attention)
        sums[layer] = (early_sums, late_sums, expand_bias_grad)

    of_reduce, of_expand, of_last = above
    token = advance(thirds=[of_reduce], fourths=[upper_expand], deps=(token,))
    token = advance([of_last], fourths=[upper_attention], deps=(token,), later=True)
    token = advance(fourths=[of_reduce], deps=(token,))
    upper_attention.scatter(token)
    token = advance(thirds=[of_expand], deps=(token,))
    token = advance(thirds=[of_last], deps=(token, upper_expand.share, upper_attention.share))
    small, changes = small_and_changes(sums)
    small, changes = after(small, token), after(changes, token)
    small, changes = cross(small, changes, 4, plane % 2, lambda a: swap_seq(a, 1), True)
    small, changes = cross(small, changes, 3, plane // 2, lambda a: swap_seq(a, 2), False)
    token = advance(joint=(of_expand, of_last), deps=(token, small, changes))
    input_grad, finish = relay(after(own_lower[:, TILE:], token), True)
    input_grad = finish(input_grad).astype(f32)
    shares[("attention", 0)] = of_last
    shares[("expand", 0)] = of_expand
    shares = {name: reduction.share.astype(f32) for name, reduction in shares.items()}

    small, changes = after(small, token), after(changes, token)
    small, changes = cross(small, changes, 2, me % 2, lambda a: swap(a, 1), True)
    small, changes = cross(small, changes, 1, (me // 2) % 2, lambda a: swap(a, 2), False)
    small, changes = cross(small, changes, 0, me // 4, lambda a: swap(a, 4), False)
    row = small.reshape(-1)
    small_out, start = [[] for _ in range(7)], 0
    for layer in range(layers):
        for member in range(7):
            size = (width if member < 6 else 4 * width) // (count * planes)
            small_out[member].append(row[start : start + size])
            start += size
    small_out = [jnp.stack(member) for member in small_out]
    entries = jnp.arange(count)
    owners = 2 * ((me // 2) ^ (entries // 2)) + ((plane // 2) ^ (entries % 2))
    source_buckets = jnp.sum(jnp.where(owners[:, None] == entries[None, :], buckets[None, :], 0), axis=1)
    table_grad = chosen_rows(changes, source_buckets, layers, width)

    ins, outs, expands, reduces = [], [], [], []
    for layer in range(layers):
        share = shares[("attention", layer)]
        pairs = share[:, width : 3 * width].reshape(share.shape[0], width // BLOCK, 2, BLOCK)
        ins.append(
            jnp.concatenate(
                [share[:, :width], pairs[:, :, 0].reshape(-1, width), pairs[:, :, 1].reshape(-1, width)], axis=1
            )
        )
        outs.append(share[:, 3 * width :])
        expands.append(shares[("expand", layer)])
        reduces.append(shares[("reduce", layer)])
    return (
        outputs[None],
        input_grad[None],
        small_out[0],
        small_out[1],
        jnp.stack(ins),
        jnp.stack(outs),
        small_out[2],
        small_out[3],
        small_out[4],
        jnp.stack(expands),
        small_out[6],
        jnp.stack(reduces),
        small_out[5],
        table_grad,
    )


def on_device(
    inputs,
    noise_buckets,
    first_gain,
    first_shift,
    attention_in,
    attention_out,
    attention_bias,
    second_gain,
    second_shift,
    expand_weight,
    expand_bias,
    reduce_weight,
    reduce_bias,
    time_table,
    cotangent,
):
    layers = first_gain.shape[0]
    count, planes = lax.axis_size("dp"), lax.axis_size("seq")
    me, plane = lax.axis_index("dp"), lax.axis_index("seq")
    model_width = inputs.shape[-1]
    table_rows = time_table.shape[1]

    stream = lax.ppermute(inputs[0], ("dp", "seq"), layout_moves(False)).astype(f32)

    sequence = (me // 2) * 2 + plane // 2
    packs = []
    for layer in range(layers):
        rows = [
            time_table[layer],
            pack_small(
                [
                    member[layer]
                    for member in (
                        first_gain,
                        first_shift,
                        attention_bias,
                        second_gain,
                        second_shift,
                        reduce_bias,
                        expand_bias,
                    )
                ],
                WIDE,
            ),
            jnp.broadcast_to(noise_buckets.astype(bf16)[:, None], (1, model_width)),
        ]
        packs.append(jnp.concatenate(rows, axis=0))

    def unpack(pack):
        stacked, sources, _ = gather_small(pack, ("dp",))
        slot = me ^ jnp.arange(count) if count == SMALL else jnp.arange(count)
        per_pack = stacked.shape[1]
        flat = stacked.reshape(count * per_pack, model_width)

        def place(index):
            return (me ^ index) if count == SMALL else index

        buckets = jnp.stack(
            [lax.dynamic_index_in_dim(flat, place(index) * per_pack + per_pack - 1, 0, False)[0] for index in range(count)]
        ).astype(jnp.int32)
        bucket = lax.dynamic_index_in_dim(buckets, sequence, 0, False)
        row = place(bucket // table_rows) * per_pack + bucket % table_rows
        scaling = lax.dynamic_slice_in_dim(flat, row, 1, 0).astype(f32)
        vectors = jnp.stack(
            [
                lax.dynamic_slice_in_dim(
                    flat, place(index) * per_pack + table_rows, per_pack - 1 - table_rows, 0
                ).reshape(-1)
                for index in range(count)
            ]
        ).astype(f32)
        share = model_width // count
        members = [vectors[:, i * share : (i + 1) * share].reshape(1, -1) for i in range(6)]
        members.append(vectors[:, 6 * share : 6 * share + expand_bias.shape[1]].reshape(1, -1))
        return tuple(members) + (scaling,), buckets

    keys_at = model_width
    shards = []
    for layer in range(layers):
        shards += [
            attention_in[layer][:, keys_at:],
            attention_in[layer][:, :keys_at],
            attention_out[layer],
            expand_weight[layer],
            reduce_weight[layer],
        ]
    gathered = []
    for position, shard in enumerate(shards):
        if count == SMALL and position >= 2:
            shard = after(shard, gathered[position - 2][2], gathered[position - 2][4])
        gathered.append(gather_rows(shard, position % 2))

    all_vectors, buckets = [], None
    for layer in range(layers):
        vectors, buckets = unpack(packs[layer])
        all_vectors.append(vectors)

    saved, all_weights = [], []
    for layer in range(layers):
        w_keys, w_query, w_out, w_expand, w_reduce = gathered[5 * layer : 5 * layer + 5]
        weights = (w_query, w_keys, w_out, w_expand, w_reduce)
        all_weights.append(weights)
        stream, kept = layer_forward(stream, weights, all_vectors[layer])
        saved.append(kept)
    back_moves = layout_moves(True)
    outputs = lax.ppermute(stream.astype(bf16), ("dp", "seq"), back_moves)[None]

    grad_flow = lax.ppermute(cotangent[0], ("dp", "seq"), layout_moves(False)).astype(f32)
    dense, small, modulation = [None] * layers, [None] * layers, [None] * layers
    for layer in reversed(range(layers)):
        grad_flow, dense[layer], small[layer], modulation[layer] = layer_backward(
            saved[layer], all_weights[layer], all_vectors[layer], grad_flow
        )
    input_grad = lax.ppermute(grad_flow, ("dp", "seq"), back_moves)[None]

    devices = count * planes
    packed = jnp.concatenate(
        [member.reshape(devices, -1) for layer in range(layers) for member in small[layer]], axis=1
    )
    row = scatter_small(packed)
    small_out, start = [[] for _ in range(7)], 0
    for layer in range(layers):
        for member in range(7):
            width = small[layer][member].size // devices
            small_out[member].append(row[start : start + width])
            start += width
    small_out = [jnp.stack(member) for member in small_out]

    changes, from_dp, from_seq = gather_small(jnp.concatenate(modulation), ("dp", "seq"))
    table_grad = table_rows_of(changes, from_dp, from_seq, buckets, layers, model_width)

    dense_out = [jnp.stack([dense[layer][member] for layer in range(layers)]) for member in range(4)]
    return (
        outputs,
        input_grad,
        small_out[0],
        small_out[1],
        dense_out[0],
        dense_out[1],
        small_out[2],
        small_out[3],
        small_out[4],
        dense_out[2],
        small_out[6],
        dense_out[3],
        small_out[5],
        table_grad,
    )


def solution(mesh):
    eight_way = mesh.shape["dp"] == SMALL and mesh.shape["seq"] == 4
    return jax.shard_map(
        fast_device if eight_way else on_device,
        mesh=mesh,
        in_specs=(
            P("dp", "seq", None),
            P("dp"),
            P(None, "dp"),
            P(None, "dp"),
            P(None, "dp", None),
            P(None, "dp", None),
            P(None, "dp"),
            P(None, "dp"),
            P(None, "dp"),
            P(None, "dp", None),
            P(None, "dp"),
            P(None, "dp", None),
            P(None, "dp"),
            P(None, "dp", None),
            P("dp", "seq", None),
        ),
        out_specs=(
            P("dp", "seq", None),
            P("dp", "seq", None),
            P(None, ("dp", "seq")),
            P(None, ("dp", "seq")),
            P(None, ("dp", "seq"), None),
            P(None, ("dp", "seq"), None),
            P(None, ("dp", "seq")),
            P(None, ("dp", "seq")),
            P(None, ("dp", "seq")),
            P(None, ("dp", "seq"), None),
            P(None, ("dp", "seq")),
            P(None, ("dp", "seq"), None),
            P(None, ("dp", "seq")),
            P(None, ("dp", "seq"), None),
        ),
        check_vma=False,
    )
```

```python
import functools
import math

import jax
import jax.numpy as jnp
from jax import lax
from jax.experimental import pallas as pl
from jax.experimental.pallas import tpu as pltpu
from jax.sharding import PartitionSpec as P

HEAD = 64
BUCKETS = 256
SMALL = 8
WIDE = 1024

epsilon = 1e-05
bf16 = jnp.bfloat16
f32 = jnp.float32


def modulated_norm(activations, norm_gain, norm_shift, scaling):
    center = activations - jnp.mean(activations, axis=-1, keepdims=True)
    spread = jnp.mean(center * center, axis=-1, keepdims=True)
    return (center * lax.rsqrt(spread + epsilon) * norm_gain + norm_shift) * (1.0 + scaling)


def swap(array, bit):
    count = lax.axis_size("dp")
    return lax.ppermute(array, "dp", [(i, i ^ bit) for i in range(count)])


def swap_seq(array, bit):
    count = lax.axis_size("seq")
    return lax.ppermute(array, "seq", [(i, i ^ bit) for i in range(count)])


def after(array, *earlier):
    return lax.optimization_barrier((array,) + earlier)[0]


def layout_moves(back):
    moves = []
    for index in range(lax.axis_size("dp")):
        core, pair = index % 2, index - index % 2
        for plane in range(4):
            source = index * 4 + plane
            target = (pair + plane % 2) * 4 + 2 * core + plane // 2
            moves.append((target, source) if back else (source, target))
    return moves


def gather_rows(shard, route):
    if lax.axis_size("dp") != SMALL:
        return lax.all_gather(shard, "dp", axis=0, tiled=True)
    along_x = swap(shard, 2)
    along_y = swap(shard, 4)
    across = swap(along_x, 4) if route == 0 else swap(along_y, 2)
    mine = [shard, along_x, along_y, across]
    parts = []
    for part in mine:
        parts += [part, swap(part, 1)]
    return parts


def order_of(parts):
    me = lax.axis_index("dp")
    return [me ^ bit for bit in range(parts)]


def scatter_dense(left, right, orders):
    count, planes = lax.axis_size("dp"), lax.axis_size("seq")
    rows, columns = left.shape[1], right.shape[1]
    if count != SMALL:
        whole = jnp.einsum("tr,tc->rc", left, right, preferred_element_type=f32)
        return lax.psum_scatter(whole, ("dp", "seq"), scatter_dimension=0, tiled=True)
    me, plane = lax.axis_index("dp"), lax.axis_index("seq")
    block = rows // count
    width = columns // len(orders)

    def pick(masks):
        return jnp.concatenate(
            [lax.dynamic_slice_in_dim(left, (me ^ mask) * block, block, 1) for mask in masks], axis=1
        )

    def product(a, b):
        return jnp.einsum("tr,tc->rc", a, b, preferred_element_type=f32)

    pieces = []
    for position, (first, second) in enumerate(orders):
        part = right[:, position * width : (position + 1) * width]
        masks = [first | second, first, second, 0]
        arrived = swap(product(pick([mask | 1 for mask in masks]), part).astype(bf16), 1)
        half = 2 * block
        leaving = (product(pick(masks[:2]), part) + arrived[:half].astype(f32)).astype(bf16)
        staying = (product(pick(masks[2:]), part) + arrived[half:].astype(f32)).astype(bf16)
        arrived = swap(leaving, first)
        leaving = (staying[:block].astype(f32) + arrived[:block].astype(f32)).astype(bf16)
        staying = (staying[block:].astype(f32) + arrived[block:].astype(f32)).astype(bf16)
        arrived = swap(leaving, second)
        pieces.append((staying, arrived))
    total = jnp.concatenate([(a.astype(f32) + b.astype(f32)).astype(bf16) for a, b in pieces], axis=1)
    return scatter_planes(total, plane, planes)


def scatter_planes(total, plane, planes):
    rows, columns = total.shape
    low, high = plane & 1, plane >> 1
    cut = total.reshape(2, 2, rows // planes, columns)
    arrived = swap_seq(lax.dynamic_index_in_dim(cut, 1 - low, 1, keepdims=False), 1)
    kept = lax.dynamic_index_in_dim(cut, low, 1, keepdims=False)
    joined = kept.astype(f32) + arrived.astype(f32)
    arrived = swap_seq(lax.dynamic_index_in_dim(joined, 1 - high, 0, keepdims=False).astype(bf16), 2)
    return lax.dynamic_index_in_dim(joined, high, 0, keepdims=False) + arrived.astype(f32)


def scatter_small(array):
    count, planes = lax.axis_size("dp"), lax.axis_size("seq")
    if count != SMALL:
        return lax.psum_scatter(array, ("dp", "seq"), scatter_dimension=0, tiled=True)[0]
    me, plane = lax.axis_index("dp"), lax.axis_index("seq")
    columns = array.shape[1]
    shape = [count, planes]
    current = array.reshape(shape[0], shape[1], columns)
    for axis, index, send in ((0, me, swap), (1, plane, swap_seq)):
        bit = 1
        while current.shape[axis] > 1:
            pairs = current.shape[axis] // 2
            view = jnp.moveaxis(current, axis, 0).reshape(pairs, 2, -1, columns)
            mine = (index // bit) % 2
            leaving = lax.dynamic_index_in_dim(view, 1 - mine, 1, keepdims=False)
            staying = lax.dynamic_index_in_dim(view, mine, 1, keepdims=False)
            current = jnp.moveaxis((staying + send(leaving, bit)).reshape(pairs, -1, columns), 0, axis)
            bit *= 2
    return current.reshape(columns)


def gather_small(array, axes):
    if lax.axis_size("dp") != SMALL:
        stacked = lax.all_gather(array, axes, axis=0, tiled=False)
        stacked = stacked.reshape((-1,) + array.shape)
        places = jnp.arange(stacked.shape[0])
        if "seq" in axes:
            planes = lax.axis_size("seq")
            return stacked, places // planes, places % planes
        return stacked, places, None
    current = array[None]
    me = lax.axis_index("dp")
    for bit in (1, 2, 4):
        current = jnp.concatenate([current, swap(current, bit)], axis=0)
    sources = me ^ jnp.arange(SMALL)
    if "seq" not in axes:
        return current, sources, None
    plane = lax.axis_index("seq")
    for bit in (1, 2):
        current = jnp.concatenate([current, swap_seq(current, bit)], axis=0)
    places = jnp.arange(SMALL * 4)
    return current, me ^ (places % SMALL), plane ^ (places // SMALL)


def times(a, weight, out_type):
    return jnp.dot(a, weight, preferred_element_type=f32).astype(out_type)


def times_transposed(a, weight, out_type):
    return lax.dot_general(a, weight, (((1,), (1,)), ((), ())), preferred_element_type=f32).astype(out_type)


def spread_keys(own):
    far = swap_seq(own, 1)
    return [own, swap(own, 1), far, swap(far, 1)]


def heads_of(rows):
    return rows.reshape(rows.shape[0], rows.shape[1] // HEAD, HEAD)


def attend(queries, chunks):
    model_width = queries.shape[1]
    whole = jnp.concatenate(chunks, axis=0)
    key_heads, value_heads = heads_of(whole[:, :model_width]), heads_of(whole[:, model_width:])
    scores = jnp.einsum("qhd,khd->hqk", heads_of(queries), key_heads, preferred_element_type=f32)
    scores = scores * (1.0 / math.sqrt(HEAD))
    exponent = jnp.exp(scores - jnp.max(scores, axis=-1, keepdims=True))
    probs = exponent / jnp.sum(exponent, axis=-1, keepdims=True)
    probs_low = probs.astype(bf16)
    mixture = jnp.einsum("hqk,khd->qhd", probs_low, value_heads, preferred_element_type=f32)
    return mixture.reshape(queries.shape).astype(bf16), (probs, probs_low)


def attend_back(queries, chunks, kept, mixture, mixture_grad):
    probs, probs_low = kept
    model_width = queries.shape[1]
    factor = 1.0 / math.sqrt(HEAD)
    whole = jnp.concatenate(chunks, axis=0)
    key_heads, value_heads = heads_of(whole[:, :model_width]), heads_of(whole[:, model_width:])
    grad_heads = heads_of(mixture_grad)
    prob_grad = jnp.einsum("qhd,khd->hqk", grad_heads, value_heads, preferred_element_type=f32)
    along = jnp.sum(probs * prob_grad, axis=-1, keepdims=True)
    score_grad = (probs * (prob_grad - along)).astype(bf16)
    query_grad = jnp.einsum("hqk,khd->qhd", score_grad, key_heads, preferred_element_type=f32)
    query_grad = (query_grad * factor).astype(bf16).reshape(queries.shape)
    key_part = jnp.einsum("hqk,qhd->khd", score_grad, heads_of(queries), preferred_element_type=f32)
    value_part = jnp.einsum("hqk,qhd->khd", probs_low, grad_heads, preferred_element_type=f32)
    parts = jnp.concatenate(
        [
            (key_part * factor).reshape(whole.shape[0], model_width),
            value_part.reshape(whole.shape[0], model_width),
        ],
        axis=1,
    ).astype(bf16)
    return query_grad, parts


def join_key_grads(parts):
    local = parts.shape[0] // 4
    cut = [parts[i * local : (i + 1) * local] for i in range(4)]
    far = cut[2].astype(f32) + swap(cut[3], 1).astype(f32)
    far = swap_seq(far.astype(bf16), 1)
    near = cut[0].astype(f32) + swap(cut[1], 1).astype(f32)
    return (near + far.astype(f32)).astype(bf16)


def layer_forward(stream, weights, vectors):
    w_query, w_keys, w_out, w_expand, w_reduce = weights
    first_gain, first_shift, attention_bias, second_gain, second_shift, reduce_bias, expand_bias, scaling = vectors
    normed = modulated_norm(stream, first_gain, first_shift, scaling).astype(bf16)
    chunks = spread_keys(times(normed, w_keys, bf16))
    queries = times(normed, w_query, bf16)
    mixture, kept = attend(queries, chunks)
    middle = stream + (times(mixture, w_out, f32) + attention_bias)
    second = modulated_norm(middle, second_gain, second_shift, scaling).astype(bf16)
    hidden = times(second, w_expand, f32) + expand_bias
    active = jax.nn.gelu(hidden).astype(bf16)
    result = middle + (times(active, w_reduce, f32) + reduce_bias)
    return result, (stream, normed, queries, chunks, kept, mixture, middle, second, hidden, active)


def layer_backward(saved, weights, vectors, grad_out):
    w_query, w_keys, w_out, w_expand, w_reduce = weights
    first_gain, first_shift, attention_bias, second_gain, second_shift, reduce_bias, expand_bias, scaling = vectors
    stream, normed, queries, chunks, kept, mixture, middle, second, hidden, active = saved
    both = ((2, 4), (4, 2))
    grad_low = grad_out.astype(bf16)
    reduce_bias_grad = jnp.sum(grad_out, axis=0)
    reduce_weight_grad = scatter_dense(active, grad_low, both)
    active_grad = times_transposed(grad_low, w_reduce, f32)
    hidden_grad = jax.vjp(jax.nn.gelu, hidden)[1](active_grad)[0]
    expand_bias_grad = jnp.sum(hidden_grad, axis=0)
    hidden_low = hidden_grad.astype(bf16)
    second_grad = times_transposed(hidden_low, w_expand, f32)
    expand_weight_grad = scatter_dense(second, hidden_low, both)
    _, second_back = jax.vjp(modulated_norm, middle, second_gain, second_shift, scaling)
    middle_part, second_gain_grad, second_shift_grad, second_scaling_grad = second_back(second_grad)
    middle_grad = grad_out + middle_part
    attention_bias_grad = jnp.sum(middle_grad, axis=0)
    middle_low = middle_grad.astype(bf16)
    mixture_grad = times_transposed(middle_low, w_out, bf16)
    attention_out_grad = scatter_dense(mixture, middle_low, both)
    query_grad, parts = attend_back(queries, chunks, kept, mixture, mixture_grad)
    key_grad = join_key_grads(parts)
    normed_grad = times_transposed(query_grad, w_query, f32) + times_transposed(key_grad, w_keys, f32)
    project_grad = jnp.concatenate([query_grad, key_grad], axis=1)
    attention_in_grad = scatter_dense(normed, project_grad, both)
    _, first_back = jax.vjp(modulated_norm, stream, first_gain, first_shift, scaling)
    stream_part, first_gain_grad, first_shift_grad, first_scaling_grad = first_back(normed_grad)
    stream_grad = middle_grad + stream_part
    small = (
        first_gain_grad,
        first_shift_grad,
        attention_bias_grad,
        second_gain_grad,
        second_shift_grad,
        reduce_bias_grad,
        expand_bias_grad,
    )
    dense = (attention_in_grad, attention_out_grad, expand_weight_grad, reduce_weight_grad)
    return stream_grad, dense, small, (first_scaling_grad + second_scaling_grad)[0]


def pack_small(vectors, rows):
    flat = jnp.concatenate([vector.reshape(-1) for vector in vectors])
    length = -(-flat.shape[0] // WIDE) * WIDE
    return jnp.pad(flat, (0, length - flat.shape[0])).reshape(-1, WIDE)


def table_rows_of(changes, from_dp, from_seq, buckets, layers, model_width):
    count, planes = lax.axis_size("dp"), lax.axis_size("seq")
    owners = (from_dp // 2) * 2 + from_seq // 2
    source_buckets = jnp.sum(
        jnp.where(owners[:, None] == jnp.arange(count)[None, :], buckets[None, :], 0), axis=1
    )
    return chosen_rows(changes, source_buckets, layers, model_width)


def chosen_rows(changes, source_buckets, layers, model_width):
    count, planes = lax.axis_size("dp"), lax.axis_size("seq")
    table_share = BUCKETS // (count * planes)
    first_row = (lax.axis_index("dp") * planes + lax.axis_index("seq")) * table_share
    chosen = (source_buckets[None, :] == (first_row + jnp.arange(table_share))[:, None]).astype(f32)
    table_grad = jnp.dot(chosen, changes, precision=lax.Precision.HIGHEST)
    return jnp.stack(
        [table_grad[:, layer * model_width : (layer + 1) * model_width] for layer in range(layers)]
    )


VMEM_LIMIT = 65_400 * 1024
TILE = 1024
BLOCK = 128
NT = (((1,), (1,)), ((), ()))
TN = (((0,), (0,)), ((), ()))


def whole_spec(array):
    zeros = (0,) * len(array.shape)
    return pl.BlockSpec(array.shape, lambda *_: zeros)


def run(body, grid, inputs, outputs, scratch=(), deps=(), aliases=(), cost=4):
    deps = tuple(aliases) + tuple(deps)
    arrays = [array for array, _ in inputs]
    specs = [spec if spec is not None else whole_spec(array) for array, spec in inputs]
    shapes = [jax.ShapeDtypeStruct(shape, kind) for shape, kind, _ in outputs]
    out_specs = [
        spec if spec is not None else whole_spec(shape) for shape, (_, _, spec) in zip(shapes, outputs)
    ]
    count, extra = len(arrays), len(deps)

    def kernel(place, *refs):
        body(place, refs[:count], refs[count + extra : count + extra + len(shapes)], refs[count + extra + len(shapes) :])

    place = jnp.stack([lax.axis_index("dp"), lax.axis_index("seq")]).astype(jnp.int32)
    return pl.pallas_call(
        kernel,
        out_shape=shapes,
        grid_spec=pltpu.PrefetchScalarGridSpec(
            num_scalar_prefetch=1,
            grid=(grid,),
            in_specs=specs + [pl.BlockSpec(memory_space=pl.ANY)] * extra,
            out_specs=out_specs,
            scratch_shapes=list(scratch),
        ),
        input_output_aliases={1 + count + i: i for i in range(len(aliases))},
        compiler_params=pltpu.CompilerParams(vmem_limit_bytes=VMEM_LIMIT),
        cost_estimate=pl.CostEstimate(flops=0, bytes_accessed=cost * 3_000_000, transcendentals=0),
    )(place, *arrays, *deps)


class Flow:
    def __init__(self, sems):
        self.sems, self.count, self.pending = sems, 0, {}

    def start(self, key, source, target):
        copy = pltpu.make_async_copy(source, target, self.sems.at[self.count])
        self.count += 1
        copy.start()
        self.pending.setdefault(key, []).append(copy)

    def wait(self, key):
        for copy in self.pending.pop(key):
            copy.wait()

    def drain(self):
        for key in list(self.pending):
            self.wait(key)

    def pack(self, key, pack, refs, target, first, columns):
        at = 0
        for (_, block, rows), ref in zip(pack, refs):
            self.start(
                key,
                ref.at[pl.ds(block * rows, rows), pl.ds(first, columns)],
                target.at[pl.ds(at, rows), :] if target.shape[1] == columns else target.at[pl.ds(at, rows), pl.ds(first, columns)],
            )
            at += rows


def run_flow(body, arrays, packs, outputs, scratch, copies, deps=(), cost=8):
    buffers = [buffer for pack in packs for buffer, _, _ in pack]
    count, extra, made = len(arrays), len(buffers), len(outputs)

    def kernel(place, *refs):
        outs = refs[count + extra + len(deps) :][:made]
        held = refs[count + extra + len(deps) + made : -1]
        weights, at = [], count
        for pack in packs:
            weights.append(refs[at : at + len(pack)])
            at += len(pack)
        body(place, Flow(refs[-1]), refs[:count], weights, outs, held)

    place = jnp.stack([lax.axis_index("dp"), lax.axis_index("seq")]).astype(jnp.int32)
    anywhere = pl.BlockSpec(memory_space=pl.ANY)
    return pl.pallas_call(
        kernel,
        out_shape=[jax.ShapeDtypeStruct(shape, kind) for shape, kind in outputs],
        in_specs=[pl.BlockSpec(memory_space=pltpu.SMEM)] + [anywhere] * (count + extra + len(deps)),
        out_specs=[anywhere] * made,
        scratch_shapes=[pltpu.VMEM(shape, kind) for shape, kind in scratch] + [pltpu.SemaphoreType.DMA((copies,))],
        compiler_params=pltpu.CompilerParams(vmem_limit_bytes=VMEM_LIMIT),
        cost_estimate=pl.CostEstimate(flops=0, bytes_accessed=cost * 3_000_000, transcendentals=0),
    )(place, *arrays, *buffers, *deps)


def join(refs):
    return jnp.concatenate([ref[...] for ref in refs], axis=0)


def block_at(place, part, stride=BLOCK, offset=0):
    return pl.ds(pl.multiple_of((place[0] ^ part) * stride + offset, BLOCK), BLOCK)


def columns_in_order(place, ref, stride=BLOCK, offset=0):
    return jnp.concatenate(
        [ref[:, block_at(place, part, stride, offset)] for part in range(SMALL)], axis=1
    )


def normalise(v):
    center = v - jnp.mean(v, axis=-1, keepdims=True)
    inverse = lax.rsqrt(jnp.mean(center * center, axis=-1, keepdims=True) + epsilon)
    return center * inverse, inverse


def modulated(v, vec, gain_row):
    unit, _ = normalise(v)
    return (unit * vec[gain_row : gain_row + 1, :] + vec[gain_row + 1 : gain_row + 2, :]) * vec[6:7, :]


def modulated_back(v, vec, gain_row, grad):
    unit, inverse = normalise(v)
    gain, shift, scale = vec[gain_row : gain_row + 1, :], vec[gain_row + 1 : gain_row + 2, :], vec[6:7, :]
    scale_grad = jnp.sum(grad * (unit * gain + shift), axis=0, keepdims=True)
    inner = grad * scale
    gain_grad = jnp.sum(inner * unit, axis=0, keepdims=True)
    shift_grad = jnp.sum(inner, axis=0, keepdims=True)
    inner = inner * gain
    back = inverse * (
        inner
        - jnp.mean(inner, axis=-1, keepdims=True)
        - unit * jnp.mean(inner * unit, axis=-1, keepdims=True)
    )
    return back, gain_grad, shift_grad, scale_grad


ROOT = math.sqrt(2.0 / math.pi)
CUBIC = 0.044715


def first_norm(x, vec, deps=()):
    def body(place, ins, outs, _):
        outs[0][...] = modulated(ins[0][...].astype(f32), ins[1], 0).astype(bf16)

    return run(body, 1, [(x, None), (vec, None)], [(x.shape, bf16, None)], deps=deps)[0]


def project(a, pack, first_tile, tiles, deps=()):
    tokens, width = a.shape

    def body(place, flow, ins, packs, outs, scratch):
        a_ref, weights, result, ordered = scratch
        flow.start("a", ins[0], a_ref)
        for tile in range(tiles):
            flow.pack(tile, pack, packs[0], weights.at[tile], (first_tile + tile) * TILE, TILE)
        flow.wait("a")
        ordered[...] = columns_in_order(place, a_ref)
        for tile in range(tiles):
            flow.wait(tile)
            at = pl.ds(tile * TILE, TILE)
            result[:, at] = jnp.dot(ordered[...], weights[tile], preferred_element_type=f32).astype(bf16)
            flow.start("out", result.at[:, at], outs[0].at[:, at])
        flow.drain()

    return run_flow(
        body,
        [a],
        [pack],
        [((tokens, tiles * TILE), bf16)],
        [(a.shape, bf16), ((tiles, width, TILE), bf16), ((tokens, tiles * TILE), bf16), (a.shape, bf16)],
        1 + tiles * (len(pack) + 1),
        deps,
        4,
    )[0]


def key_specs(chunks):
    return [
        (chunk, pl.BlockSpec((chunk.shape[0], 4 * HEAD), lambda i, s: (0, i))) for chunk in chunks
    ]


def head_masks(rows):
    lane = lax.broadcasted_iota(jnp.int32, (rows, 2 * HEAD), 1)
    return lane < HEAD, lane >= HEAD


def both_heads(rows):
    zeros = jnp.zeros_like(rows)
    return jnp.concatenate([jnp.where(mask, rows, zeros) for mask in head_masks(rows.shape[0])], axis=0)


def attend_fast(queries, chunks, deps=()):
    tokens, width = queries.shape
    pairs = width // (2 * HEAD)

    def body(place, ins, outs, _):
        both = join(ins[1:5])
        keys, values = both[:, : 2 * HEAD], both[:, 2 * HEAD :]
        query = both_heads(ins[0][...] * jnp.asarray(1.0 / math.sqrt(HEAD), bf16))
        scores = lax.dot_general(keys, query, NT, preferred_element_type=f32)
        most = jnp.max(scores, axis=0, keepdims=True)
        exponent = jnp.exp(scores - most)
        total = jnp.sum(exponent, axis=0, keepdims=True)
        mixed = lax.dot_general(values, exponent.astype(bf16), TN, preferred_element_type=f32)
        halves = [
            mixed[head * HEAD : (head + 1) * HEAD, head * tokens : (head + 1) * tokens]
            / total[:, head * tokens : (head + 1) * tokens]
            for head in range(2)
        ]
        outs[0][...] = jnp.concatenate(halves, axis=0).T.astype(bf16)
        top = most + jnp.log(total)
        outs[1][0, 0:1, :] = top[:, :tokens]
        outs[1][0, 1:2, :] = top[:, tokens:]

    return run(
        body,
        pairs,
        [(queries, pl.BlockSpec((tokens, 2 * HEAD), lambda i, s: (0, i)))] + key_specs(chunks),
        [
            (queries.shape, bf16, pl.BlockSpec((tokens, 2 * HEAD), lambda i, s: (0, i))),
            ((pairs, 8, tokens), f32, pl.BlockSpec((1, 8, tokens), lambda i, s: (i, 0, 0))),
        ],
        deps=deps,
        cost=15,
    )


def attend_fast_back(queries, chunks, kept, mixture_grad, tops, deps=()):
    tokens, width = queries.shape
    pairs = width // (2 * HEAD)

    def body(place, ins, outs, _):
        both = join(ins[1:5])
        keys, values = both[:, : 2 * HEAD], both[:, 2 * HEAD :]
        scaled = ins[0][...] * jnp.asarray(1.0 / math.sqrt(HEAD), bf16)
        grads = ins[6][...]
        masks = head_masks(tokens)
        select = jnp.concatenate([mask[0:1].astype(f32) for mask in masks] + [jnp.zeros((6, 2 * HEAD), f32)], axis=0)
        along = lax.dot_general(
            select,
            ins[5][...].astype(f32) * grads.astype(f32),
            NT,
            precision=lax.Precision.HIGHEST,
            preferred_element_type=f32,
        )
        query, grad = both_heads(scaled), both_heads(grads)
        scores = lax.dot_general(keys, query, NT, preferred_element_type=f32)
        top = jnp.concatenate([ins[7][0, head : head + 1, :] for head in range(2)], axis=1)
        probs = jnp.exp(scores - top)
        prob_grad = lax.dot_general(values, grad, NT, preferred_element_type=f32)
        pulled = jnp.concatenate([along[head : head + 1, :] for head in range(2)], axis=1)
        score_grad = (probs * (prob_grad - pulled)).astype(bf16)
        key_grad = jnp.dot(score_grad, query, preferred_element_type=f32)
        value_grad = jnp.dot(probs.astype(bf16), grad, preferred_element_type=f32)
        query_part = lax.dot_general(keys, score_grad, TN, preferred_element_type=f32)
        halves = [
            query_part[head * HEAD : (head + 1) * HEAD, head * tokens : (head + 1) * tokens] for head in range(2)
        ]
        query_grad = jnp.concatenate(halves, axis=0) * (1.0 / math.sqrt(HEAD))
        outs[0][...] = query_grad.T.astype(bf16)
        for chunk in range(4):
            rows = slice(chunk * tokens, (chunk + 1) * tokens)
            outs[1 + chunk][:, : 2 * HEAD] = key_grad[rows].astype(bf16)
            outs[1 + chunk][:, 2 * HEAD :] = value_grad[rows].astype(bf16)

    pair_spec = pl.BlockSpec((tokens, 2 * HEAD), lambda i, s: (0, i))
    part = ((tokens, 2 * width), bf16, pl.BlockSpec((tokens, 4 * HEAD), lambda i, s: (0, i)))
    return run(
        body,
        pairs,
        [(queries, pair_spec)]
        + key_specs(chunks)
        + [
            (kept, pl.BlockSpec((tokens, 2 * HEAD), lambda i, s: (0, MIXTURE // (2 * HEAD) + i))),
            (mixture_grad, pair_spec),
            (tops, pl.BlockSpec((1, 8, tokens), lambda i, s: (i, 0, 0))),
        ],
        [(queries.shape, bf16, pair_spec)] + [part] * 4,
        deps=deps,
        cost=18,
    )


ACTIVE, SECOND, MIXTURE, NORMED, KEPT = 0, 4 * TILE, 5 * TILE, 6 * TILE, 7 * TILE


def columns(tile, count=1):
    return pl.ds(tile * TILE, count * TILE)


def feed_forward(normed, mixture, packs, stream, vec, bias, next_vec, deps=()):
    tokens, width = mixture.shape
    hidden_width = bias.shape[1]
    half = 2 * TILE

    def body(place, flow, ins, weights, outs, scratch):
        (mixture_ref, stream_ref, vec_ref, next_ref, bias_ref, kept, w_out, w_expand, w_reduce) = scratch[:9]
        (middle, slope, result, following, ordered) = scratch[9:]
        flow.start("first", ins[0], mixture_ref)
        flow.start("first", ins[2], vec_ref)
        flow.pack("out", packs[0], weights[0], w_out, 3 * TILE, TILE)
        flow.start("out", ins[1], stream_ref)
        flow.start("out", ins[4], bias_ref)
        for number in range(2):
            flow.pack(f"expand{number}", packs[1], weights[1], w_expand, number * half, half)
        flow.start("normed", ins[5], kept.at[:, pl.ds(NORMED, TILE)])
        flow.start("next", ins[3], next_ref)
        for number in range(2):
            flow.pack(f"reduce{number}", packs[2], weights[2], w_reduce, number * half, half)

        flow.wait("first")
        kept[:, MIXTURE:NORMED] = mixture_ref[...]
        ordered[...] = columns_in_order(place, mixture_ref)
        flow.wait("out")
        branch = jnp.dot(ordered[...], w_out[...], preferred_element_type=f32)
        middle[...] = stream_ref[...].astype(f32) + (branch + vec_ref[2:3, :])
        flow.start("middle", middle, outs[0])
        kept[:, SECOND:MIXTURE] = modulated(middle[...], vec_ref, 3).astype(bf16)
        ordered[...] = columns_in_order(place, kept, BLOCK, SECOND)
        for tile in range(4):
            if tile % 2 == 0:
                flow.wait(f"expand{tile // 2}")
            at = columns(tile)
            hidden = jnp.dot(ordered[...], w_expand[:, at], preferred_element_type=f32) + bias_ref[:, at]
            square = hidden * hidden
            bent = jnp.tanh(ROOT * hidden * (1.0 + CUBIC * square))
            share = 0.5 * (1.0 + bent)
            kept[:, at] = (hidden * share).astype(bf16)
            steep = share + (0.5 * ROOT) * hidden * (1.0 - bent * bent) * (1.0 + (3.0 * CUBIC) * square)
            slope[:, at] = steep.astype(bf16)
            if tile == 1:
                flow.start("slope", slope.at[:, columns(0, 2)], outs[2].at[:, columns(0, 2)])
        flow.start("slope", slope.at[:, columns(2, 2)], outs[2].at[:, columns(2, 2)])
        flow.wait("normed")
        flow.start("kept", kept, outs[1])
        for tile in range(4):
            if tile % 2 == 0:
                flow.wait(f"reduce{tile // 2}")
            a = columns_in_order(place, kept, 4 * BLOCK, tile * BLOCK)
            product = jnp.dot(a, w_reduce[:, columns(tile)], preferred_element_type=f32)
            result[...] = product if tile == 0 else result[...] + product
        result[...] = middle[...] + (result[...] + vec_ref[5:6, :])
        flow.start("result", result, outs[3])
        flow.wait("next")
        if next_vec is None:
            following[...] = result[...].astype(bf16)
        else:
            following[...] = modulated(result[...], next_ref, 0).astype(bf16)
        flow.start("following", following, outs[4])
        flow.drain()

    wide_shape = (tokens, hidden_width)
    rows = SMALL * BLOCK
    return run_flow(
        body,
        [mixture, stream, vec, vec if next_vec is None else next_vec, bias, normed],
        packs,
        [(mixture.shape, f32), ((tokens, KEPT), bf16), (wide_shape, bf16), (mixture.shape, f32), (mixture.shape, bf16)],
        [
            (mixture.shape, bf16),
            (stream.shape, stream.dtype),
            (vec.shape, f32),
            (vec.shape, f32),
            (bias.shape, f32),
            ((tokens, KEPT), bf16),
            ((rows, TILE), bf16),
            ((rows, hidden_width), bf16),
            ((rows, hidden_width), bf16),
            (mixture.shape, f32),
            (wide_shape, bf16),
            (mixture.shape, f32),
            (mixture.shape, bf16),
            (mixture.shape, bf16),
        ],
        6 + 5 * len(packs[0]) + 6,
        deps,
        12,
    )


def feed_forward_back(grad, grad_low, slope, middle, packs, vec, deps=()):
    tokens, width = grad.shape
    hidden_width = slope.shape[1]
    low, low_block = grad_low
    half = 2 * TILE

    def body(place, flow, ins, weights, outs, scratch):
        (grad_ref, low_ref, slope_ref, middle_ref, vec_ref, w_out, w_expand, w_reduce) = scratch[:8]
        (hidden, bias, middle_grad, middle_low, sums, mixture, total, ordered) = scratch[8:]
        flow.start("low", ins[1].at[:, columns(low_block)], low_ref)
        flow.pack("reduce0", packs[2], weights[2], w_reduce, 0, half)
        flow.start("slope", ins[2], slope_ref)
        flow.pack("reduce1", packs[2], weights[2], w_reduce, half, half)
        for number in range(2):
            flow.pack(f"expand{number}", packs[1], weights[1], w_expand, number * half, half)
        flow.start("norm", ins[3], middle_ref)
        flow.start("norm", ins[4], vec_ref)
        flow.start("norm", ins[0], grad_ref)
        flow.pack("out", packs[0], weights[0], w_out, 3 * TILE, TILE)

        flow.wait("low")
        for tile in range(4):
            if tile % 2 == 0:
                flow.wait(f"reduce{tile // 2}")
            product = lax.dot_general(low_ref[...], w_reduce[:, columns(tile)], NT, preferred_element_type=f32)
            if tile == 0:
                flow.wait("slope")
            for part in range(SMALL):
                at = block_at(place, part, 4 * BLOCK, tile * BLOCK)
                piece = product[:, part * BLOCK : (part + 1) * BLOCK] * slope_ref[:, at].astype(f32)
                hidden[:, at] = piece.astype(bf16)
                bias[:, at] = jnp.sum(piece, axis=0, keepdims=True)
        flow.start("hidden", hidden.at[:, columns(0, 2)], outs[0])
        flow.start("hidden", hidden.at[:, columns(2, 2)], outs[1])
        flow.start("bias", bias, outs[3])
        for tile in range(4):
            if tile % 2 == 0:
                flow.wait(f"expand{tile // 2}")
            product = lax.dot_general(
                hidden[:, columns(tile)], w_expand[:, columns(tile)], NT, preferred_element_type=f32
            )
            total[...] = product if tile == 0 else total[...] + product
        for part in range(SMALL):
            ordered[:, block_at(place, part)] = total[:, part * BLOCK : (part + 1) * BLOCK]
        flow.wait("norm")
        back, gain_grad, shift_grad, scale_grad = modulated_back(middle_ref[...], vec_ref, 3, ordered[...])
        upstream = grad_ref[...].astype(f32)
        middle_grad[...] = upstream + back
        middle_low[...] = middle_grad[...].astype(bf16)
        flow.start("middle", middle_low, outs[2])
        flow.start("middle", middle_grad, outs[4])
        flow.wait("out")
        product = lax.dot_general(middle_low[...], w_out[...], NT, preferred_element_type=f32).astype(bf16)
        for part in range(SMALL):
            mixture[:, block_at(place, part)] = product[:, part * BLOCK : (part + 1) * BLOCK]
        flow.start("mixture", mixture, outs[6])
        sums[0:1, :] = gain_grad
        sums[1:2, :] = shift_grad
        sums[2:3, :] = scale_grad
        sums[3:4, :] = jnp.sum(middle_grad[...], axis=0, keepdims=True)
        sums[4:5, :] = jnp.sum(upstream, axis=0, keepdims=True)
        sums[5:8, :] = jnp.zeros((3, width), f32)
        flow.start("sums", sums, outs[5])
        flow.drain()

    rows = SMALL * BLOCK
    return run_flow(
        body,
        [grad, low, slope, middle, vec],
        packs,
        [
            ((tokens, half), bf16),
            ((tokens, half), bf16),
            (grad.shape, bf16),
            ((1, hidden_width), f32),
            (grad.shape, f32),
            ((8, width), f32),
            (grad.shape, bf16),
        ],
        [
            (grad.shape, grad.dtype),
            (grad.shape, bf16),
            (slope.shape, bf16),
            (middle.shape, f32),
            (vec.shape, f32),
            ((rows, TILE), bf16),
            ((rows, hidden_width), bf16),
            ((rows, hidden_width), bf16),
            (slope.shape, bf16),
            ((1, hidden_width), f32),
            (grad.shape, f32),
            (grad.shape, bf16),
            ((8, width), f32),
            (grad.shape, bf16),
            (grad.shape, f32),
            (grad.shape, f32),
        ],
        5 + 5 * len(packs[0]) + 7,
        deps,
        12,
    )


def first_back(query_grad, key_parts, pack, stream, middle_grad, vec, deps=()):
    tokens, width = stream.shape
    shape = key_parts[0].shape

    def body(place, flow, ins, weights, outs, scratch):
        (lower, near_ref, leave_ref, far_ref, stream_ref, middle_ref, vec_ref, w_in) = scratch[:8]
        (key_ref, grad_ref, sums, total, ordered) = scratch[8:]
        flow.start("query", ins[0], lower.at[:, columns(0)])
        flow.pack("w0", pack, weights[0], w_in, 0, TILE)
        for source, target in zip(ins[1:4], (near_ref, leave_ref, far_ref)):
            flow.start("keys", source, target)
        flow.pack("w1", pack, weights[0], w_in, TILE, 2 * TILE)
        for source, target in zip(ins[4:7], (stream_ref, middle_ref, vec_ref)):
            flow.start("norm", source, target)
        flow.wait("query")
        flow.wait("w0")
        total[...] = lax.dot_general(lower[:, columns(0)], w_in[:, columns(0)], NT, preferred_element_type=f32)
        flow.wait("keys")
        key_ref[...] = (
            near_ref[...].astype(f32) + leave_ref[...].astype(f32) + far_ref[...].astype(f32)
        ).astype(bf16)
        flow.start("key", key_ref, outs[3])
        flow.wait("w1")
        total[...] += lax.dot_general(key_ref[...], w_in[:, columns(1, 2)], NT, preferred_element_type=f32)
        for part in range(SMALL):
            ordered[:, block_at(place, part)] = total[:, part * BLOCK : (part + 1) * BLOCK]
        flow.wait("norm")
        back, gain_grad, shift_grad, scale_grad = modulated_back(
            stream_ref[...].astype(f32), vec_ref, 0, ordered[...]
        )
        grad_ref[...] = middle_ref[...] + back
        lower[:, columns(1)] = grad_ref[...].astype(bf16)
        flow.start("lower", lower, outs[1])
        flow.start("grad", grad_ref, outs[0])
        sums[0:1, :] = gain_grad
        sums[1:2, :] = shift_grad
        sums[2:3, :] = scale_grad
        sums[3:8, :] = jnp.zeros((5, width), f32)
        flow.start("sums", sums, outs[2])
        flow.drain()

    rows = SMALL * BLOCK
    return run_flow(
        body,
        [query_grad, *key_parts, stream, middle_grad, vec],
        [pack],
        [(stream.shape, f32), ((tokens, 2 * TILE), bf16), ((8, width), f32), (shape, bf16)],
        [
            ((tokens, 2 * TILE), bf16),
            (shape, bf16),
            (shape, bf16),
            (shape, bf16),
            (stream.shape, stream.dtype),
            (stream.shape, f32),
            (vec.shape, f32),
            ((rows, 3 * TILE), bf16),
            (shape, bf16),
            (stream.shape, f32),
            ((8, width), f32),
            (stream.shape, f32),
            (stream.shape, f32),
        ],
        7 + 2 * len(pack) + 4,
        deps,
        6,
    )


ORDERS = ((6, 2, 4, 0), (6, 4, 2, 0))


class Group:
    def __init__(self, arrays, left_of, right_of):
        self.arrays, self.left_of, self.right_of = arrays, left_of, right_of

    def left(self, place, refs, tile):
        array, stride, offset = self.left_of[tile]
        return jnp.concatenate(
            [refs[array][:, block_at(place, mask, stride, offset)] for mask in ORDERS[tile // 2]], axis=1
        )

    def product(self, place, refs, tile):
        array, start = self.right_of[tile]
        return lax.dot_general(
            self.left(place, refs, tile), refs[array][:, start : start + TILE], TN, preferred_element_type=f32
        )


def reduce_group(kept, lower, block):
    return Group(
        [(lower, block * TILE, TILE), (kept, ACTIVE, 4 * TILE)],
        [(1, 4 * BLOCK, u * BLOCK) for u in range(4)],
        [(0, 0)] * 4,
    )


def expand_group(kept, back):
    return Group(
        [(kept, SECOND, TILE), (back[0], 0, 2 * TILE), (back[1], 0, 2 * TILE)],
        [(0, BLOCK, 0)] * 4,
        [(1, 0), (1, TILE), (2, 0), (2, TILE)],
    )


def attention_group(kept, back, lower, key_grad):
    return Group(
        [
            (kept, NORMED, TILE),
            (lower, 0, TILE),
            (key_grad, 0, 2 * TILE),
            (kept, MIXTURE, TILE),
            (back[2], 0, TILE),
        ],
        [(0, BLOCK, 0)] * 3 + [(3, BLOCK, 0)],
        [(1, 0), (2, 0), (2, TILE), (4, 0)],
    )


def wide(value):
    return value.astype(f32)


class Reduction:
    def __init__(self, group, stacked=False):
        self.group, self.stacked = group, stacked

    def scatter(self, *tokens):
        piece = after(self.piece, *tokens) if tokens else self.piece
        self.share = lax.psum_scatter(piece, "seq", scatter_dimension=0, tiled=True)


def advance(seconds=(), thirds=(), fourths=(), joint=(), deps=(), later=False):
    arrays, outputs, scratch, loads, works = [], [], [], [], []
    half = 2 * TILE
    quarter, eighth = (2 * BLOCK, half), (BLOCK, half)

    def bring(array, shape, source, target=lambda ref: ref, key=None):
        number = len(loads)
        slot = len(scratch) if shape is not None else len(scratch) - 1
        if shape is not None:
            scratch.append((shape, array.dtype))
        loads.append((len(arrays), slot, source, target, number if key is None else key))
        arrays.append(array)
        return slot, number

    def make(shape):
        outputs.append((shape, bf16))
        scratch.append((shape, bf16))
        return len(outputs) - 1, len(scratch) - 1

    for one in seconds:
        group, slots, keys = one.group, [], []
        for pair, first, width in group.arrays:
            tokens = pair[0].shape[0]
            for side, array in enumerate(pair):
                slot, key = bring(
                    array,
                    (2 * tokens, width) if side == 0 else None,
                    lambda ref, first=first, width=width: ref.at[:, pl.ds(first, width)],
                    lambda ref, side=side, tokens=tokens: ref.at[pl.ds(side * tokens, tokens), :],
                )
                keys.append(key)
            slots.append(slot)
        made = [make(quarter), make(quarter), make((2,) + quarter)]

        def product(place, flow, held, outs, group=group, slots=slots, keys=keys, made=made):
            refs = [held[slot] for slot in slots]
            waited = 0
            stay = made[2]
            for tile in range(4):
                needed = 2 * (max(group.left_of[tile][0], group.right_of[tile][0]) + 1)
                while waited < needed:
                    flow.wait(keys[waited])
                    waited += 1
                total = group.product(place, refs, tile)
                leave = made[tile // 2]
                held[leave[1]][:, columns(tile % 2)] = total[: 2 * BLOCK].astype(bf16)
                held[stay[1]][tile // 2, :, columns(tile % 2)] = total[2 * BLOCK :].astype(bf16)
                if tile % 2:
                    flow.start("out", held[leave[1]], outs[leave[0]])
                    flow.start("out", held[stay[1]].at[tile // 2], outs[stay[0]].at[tile // 2])

        works.append(product)
    for one in thirds:
        loaded = [
            bring(one.staying, (2,) + quarter, lambda ref: ref),
            bring(one.from_x, quarter, lambda ref: ref),
            bring(one.from_y, quarter, lambda ref: ref),
        ]
        made = [make(eighth), make(eighth), make((2,) + eighth)]

        def add(place, flow, held, outs, loaded=loaded, made=made):
            flow.wait(loaded[0][1])
            for number in range(2):
                flow.wait(loaded[1 + number][1])
                total = (wide(held[loaded[0][0]][number]) + wide(held[loaded[1 + number][0]][...])).astype(bf16)
                held[made[number][1]][...] = total[:BLOCK]
                held[made[2][1]][number] = total[BLOCK:]
                flow.start("out", held[made[number][1]], outs[made[number][0]])
                flow.start("out", held[made[2][1]].at[number], outs[made[2][0]].at[number])

        works.append(add)
    sums = [[one] for one in fourths] + ([list(joint)] if joint else [])
    for members in sums:
        alone = len(members) == 1
        stacked = alone and members[0].stacked
        loaded = [
            [
                bring(one.kept, (2,) + eighth, lambda ref: ref),
                bring(one.second_y, eighth, lambda ref: ref),
                bring(one.second_x, eighth, lambda ref: ref),
            ]
            for one in members
        ]
        made = make((4 * BLOCK, TILE) if stacked else (len(members) * BLOCK, 4 * TILE))

        def finish(place, flow, held, outs, loaded=loaded, made=made, stacked=stacked, alone=alone):
            result, share = held[made[1]], BLOCK // 4
            for number, (kept, *arrived) in enumerate(loaded):
                flow.wait(kept[1])
                for side in range(2):
                    flow.wait(arrived[side][1])
                    total = (wide(held[kept[0]][side]) + wide(held[arrived[side][0]][...])).astype(bf16)
                    if stacked:
                        for tile in range(2):
                            at = (2 * side + tile) * BLOCK
                            result[at : at + BLOCK, :] = total[:, tile * TILE : (tile + 1) * TILE]
                    elif alone:
                        result[:, columns(2 * side, 2)] = total
                    else:
                        for plane in range(4):
                            start = (plane * len(loaded) + number) * share
                            result[start : start + share, columns(2 * side, 2)] = total[
                                plane * share : (plane + 1) * share
                            ]
            flow.start("out", result, outs[made[0]])

        works.append(finish)

    def body(place, flow, ins, _, outs, held):
        for number, slot, source, target, key in loads:
            flow.start(key, source(ins[number]), target(held[slot]))
        for work in works:
            work(place, flow, held, outs)
        flow.drain()

    results = list(run_flow(body, arrays, [], outputs, scratch, len(loads) + 2 * len(outputs) + 2, deps, 7 if seconds else 4))
    token = results[-1] if joint and len(works) == 1 else results[0]
    for one in seconds:
        along_x, along_y, one.staying = results[:3]
        results = results[3:]
        one.from_x, one.from_y = swap(along_x, 2), swap(along_y, 4)
    for one in thirds:
        along_y, along_x, one.kept = results[:3]
        results = results[3:]
        one.second_y, one.second_x = swap(along_y, 4), swap(along_x, 2)
    for one in fourths:
        one.piece = results[0]
        results = results[1:]
        if not later:
            one.scatter()
    if joint:
        both = lax.psum_scatter(results[0], "seq", scatter_dimension=0, tiled=True)
        share = BLOCK // 4
        for number, one in enumerate(joint):
            one.share = both[number * share : (number + 1) * share]
    return token


HALF = BLOCK // 2
EXTRA = 32


def raw_inputs(kind, layer, arrays):
    if kind == "attention":
        return [
            (arrays[0], pl.BlockSpec((1,) + arrays[0].shape[1:], lambda i, s: (layer, 0, 0))),
            (arrays[1], pl.BlockSpec((1,) + arrays[1].shape[1:], lambda i, s: (layer, 0, 0))),
        ]
    if kind == "expand":
        return [(arrays[0], pl.BlockSpec((1, BLOCK, TILE), lambda i, s: (layer, 0, i)))]
    return [(arrays[0], pl.BlockSpec((1, BLOCK, TILE), lambda i, s: (layer, i, 0)))]


def raw_tile(kind, ins, targets):
    if kind != "attention":
        for target in targets:
            target[:BLOCK, :] = ins[0][0]
        return
    pairs = TILE // (2 * BLOCK)
    for tile in range(4):

        @pl.when(pl.program_id(0) == tile)
        def _(tile=tile):
            for target in targets:
                if tile == 0:
                    target[:BLOCK, :] = ins[0][0, :, :TILE]
                elif tile == 3:
                    target[:BLOCK, :] = ins[1][0]
                else:
                    for pair in range(pairs):
                        start = (pairs * (tile - 1) + pair) * BLOCK
                        at = pair * 2 * BLOCK
                        target[:BLOCK, at : at + BLOCK] = ins[0][0, :, TILE + start : TILE + start + BLOCK]
                        target[:BLOCK, at + BLOCK : at + 2 * BLOCK] = ins[0][
                            0, :, 2 * TILE + start : 2 * TILE + start + BLOCK
                        ]


def column_spec(rows, row_block=0):
    return pl.BlockSpec((rows, TILE), lambda i, s: (row_block, i))


def first_pack(raw, time_table, members, noise_buckets):
    layers = time_table.shape[0]
    buckets = jnp.broadcast_to(noise_buckets.astype(bf16), (layers, BLOCK))
    chunks = [(2 + 1 + index, layer, 0) for index in range(6) for layer in range(layers)]
    bias_chunks = members[6].shape[1] // BLOCK
    chunks += [(2 + 1 + 6, layer, part) for layer in range(layers) for part in range(bias_chunks)]
    chunks.append((2 + 1 + 7, 0, 0))
    per_tile = TILE // BLOCK

    def body(place, ins, outs, _):
        raw_tile("attention", ins[:2], outs)
        for tile in range(4):

            @pl.when(pl.program_id(0) == tile)
            def _(tile=tile):
                start = (tile % 2) * 16
                outs[0][BLOCK : BLOCK + 16, :] = ins[2][tile // 2, start : start + 16, :]
                for slot in range(per_tile):
                    index = tile * per_tile + slot
                    at = slot * BLOCK
                    row = jnp.zeros((1, BLOCK), bf16)
                    if index < len(chunks):
                        array, layer, part = chunks[index]
                        row = ins[array][layer : layer + 1, part * BLOCK : (part + 1) * BLOCK]
                    outs[0][BLOCK + 16 :, at : at + BLOCK] = jnp.broadcast_to(row.astype(f32), (16, BLOCK)).astype(bf16)

    return run(
        body,
        4,
        raw_inputs("attention", 0, raw)
        + [(time_table, None)]
        + [(member, None) for member in members]
        + [(buckets, None)],
        [((BLOCK + EXTRA, 4 * TILE), bf16, column_spec(BLOCK + EXTRA))],
    )[0]


def other_packs(kinds, raws, deps=()):
    inputs, counts = [], []
    for (kind, layer), raw in zip(kinds, raws):
        inputs += raw_inputs(kind, layer, raw)
        counts.append(len(raw))

    def body(place, ins, outs, _):
        at = 0
        for position, ((kind, _), taken) in enumerate(zip(kinds, counts)):
            raw_tile(kind, ins[at : at + taken], [outs[0].at[position * BLOCK : (position + 1) * BLOCK]])
            at += taken

    rows = len(kinds) * BLOCK
    return run(body, 4, inputs, [((rows, 4 * TILE), bf16, column_spec(rows))], deps=deps)[0]


def own_rows(rest, position, rows, deps=()):
    def body(place, ins, outs, _):
        outs[0][...] = ins[0][...]
        outs[1][...] = ins[0][...]

    out = ((rows, 4 * TILE), bf16, column_spec(BLOCK))
    return run(body, 4, [(rest, column_spec(BLOCK, position))], [out, out], deps=deps)


def diagonal_rows(x, y, buffers, deps=()):
    def body(place, ins, outs, _):
        outs[0][...] = ins[1][...]
        outs[1][...] = ins[0][...]

    rows, block = (buffers[0].shape[0], BLOCK // HALF) if buffers else (HALF, 0)

    def spec(at):
        return pl.BlockSpec((HALF, 4 * TILE), lambda i, s: (at, 0))

    out = ((rows, 4 * TILE), bf16, spec(block))
    return run(body, 1, [(x, spec(1)), (y, spec(0))], [out, out], deps=deps, aliases=buffers)


def first_step(rest, x, y, deps=()):
    half = EXTRA // 2

    def body(place, ins, outs, _):
        from_x, from_y, own = ins
        for out, source, at in ((outs[0], from_y, 0), (outs[1], from_x, 1)):
            out[:BLOCK, :] = own[...]
            out[BLOCK : BLOCK + HALF, :] = source[at * HALF : (at + 1) * HALF, :]
            out[BLOCK + HALF :, :] = source[BLOCK + at * half : BLOCK + (at + 1) * half, :]

    rows = BLOCK + HALF + half
    out = ((rows, 4 * TILE), bf16, column_spec(rows))
    whole = column_spec(x.shape[0])
    return run(body, 4, [(x, whole), (y, whole), (rest, column_spec(BLOCK))], [out, out], deps=deps)


class Gather:
    def __init__(self, kinds, raws, time_table, members, noise_buckets):
        self.count = len(kinds)
        self.first = first_pack(raws[0], time_table, members, noise_buckets)
        self.xs, self.ys = [swap(self.first, 2)], [swap(self.first, 4)]
        self.core_first = swap(self.first, 1)
        self.kinds, self.raws = kinds, raws
        self.core_xs, self.core_ys = [], []

    def others(self, deps):
        self.rest = other_packs(self.kinds[1:], self.raws[1:], deps)
        self.ready = tuple(own_rows(self.rest, 1, BLOCK + HALF))
        return self.ready[0]

    def prepare(self, deps=()):
        step = len(self.xs)
        self.ready = ()
        if step < self.count:
            self.ready = tuple(own_rows(self.rest, step - 1, BLOCK + HALF, deps))
            return self.ready[0]
        return deps[0]

    def step(self, deps=(), token=None):
        step = len(self.xs)
        if step == 2:
            deps = (self.core_rest,) + tuple(deps)
        if step > 1:
            deps = (self.core_xs[-1], self.core_ys[-1]) + tuple(deps)
            on_x, on_y = diagonal_rows(self.xs[-1], self.ys[-1], self.ready, deps)
        else:
            on_x, on_y = first_step(self.rest, self.xs[-1], self.ys[-1], deps)
            self.core_rest = swap(after(self.rest, on_x), 1)
        self.cross(on_x if token is None else token)
        self.xs.append(swap(on_x, 2))
        self.ys.append(swap(on_y, 4))
        return on_x

    def cross(self, token):
        self.core_xs.append(swap(after(self.xs[-1], token), 1))
        self.core_ys.append(swap(after(self.ys[-1], token), 1))

    def pack(self, k):
        row = 2 if k + 1 < self.count else 0
        own = [(self.first, 0, BLOCK), (self.core_first, 0, BLOCK)] if k == 0 else [(self.rest, k - 1, BLOCK), (self.core_rest, k - 1, BLOCK)]
        sides = (self.xs, self.core_xs, self.ys, self.core_ys)
        return (
            own
            + [(side[k], 0, BLOCK) for side in sides]
            + [(sides[i][k + 1], row, HALF) for i in (0, 2, 1, 3)]
        )

    def extras(self):
        whole = [(self.first, BLOCK, EXTRA), (self.core_first, BLOCK, EXTRA)]
        whole += [(side[0], BLOCK, EXTRA) for side in (self.xs, self.core_xs, self.ys, self.core_ys)]
        at, rows = BLOCK + HALF, EXTRA // 2
        parts = [
            [(self.xs[1], at, rows), (self.ys[1], at, rows)],
            [(self.core_xs[1], at, rows), (self.core_ys[1], at, rows)],
        ]
        return [[piece] for piece in whole] + parts


def vectors_of(extras, members, layers, table_rows, width):
    share = members[6].shape[1]
    bias_at, bucket_at = 6 * layers * BLOCK, 6 * layers * BLOCK + layers * share
    pieces = [piece for parts in extras for piece in parts]
    tables, rows_at, at = [], [], 0
    for parts in extras:
        tables.append(at)
        rows_at.append((at + len(parts) - 1, 0 if len(parts) == 2 else EXTRA // 2))
        at += len(parts)

    def body(place, ins, outs, _):
        me = place[0]
        row = [ins[at][start : start + 16, :].astype(f32)[0:1, :] for at, start in rows_at]
        mine = (me // 2) * 2 + place[1] // 2 == me
        bucket = jnp.where(mine, row[0][:, bucket_at : bucket_at + 1], row[1][:, bucket_at : bucket_at + 1])
        for layer in range(layers):
            scaling = jnp.ones((1, width), f32)
            for part in range(SMALL):
                owner = me ^ part
                for member in range(6):
                    start = (member * layers + layer) * BLOCK
                    outs[2 * layer][member : member + 1, block_at(place, part)] = row[part][:, start : start + BLOCK]
                start = bias_at + layer * share
                outs[2 * layer + 1][:, pl.ds(pl.multiple_of(owner * share, BLOCK), share)] = row[part][
                    :, start : start + share
                ]
                for half in range(2):
                    block = ins[tables[part]][0:16, (2 * layer + half) * TILE : (2 * layer + half + 1) * TILE].astype(f32)
                    place_of = lax.broadcasted_iota(jnp.int32, block.shape, 0) + (owner * table_rows + half * 16)
                    hit = place_of.astype(f32) == bucket
                    scaling += jnp.sum(jnp.where(hit, block, 0.0), axis=0, keepdims=True)
            outs[2 * layer][6:7, :] = scaling
            outs[2 * layer][7:8, :] = jnp.zeros((1, width), f32)
        for part in range(SMALL):
            outs[2 * layers][pl.ds(me ^ part, 1), :] = row[part][:, bucket_at : bucket_at + BLOCK]

    result = run(
        body,
        1,
        [
            (array, pl.BlockSpec((rows, 4 * TILE), lambda i, s, r=start // rows: (r, 0)))
            for array, start, rows in pieces
        ],
        [
            item
            for _ in range(layers)
            for item in (((8, width), f32, None), ((1, SMALL * share), f32, None))
        ]
        + [((SMALL, BLOCK), f32, None)],
    )
    pairs = [(result[2 * layer], result[2 * layer + 1]) for layer in range(layers)]
    return pairs, result[2 * layers][:, 0].astype(jnp.int32)


def small_and_changes(sums):
    columns = []
    for early, late, hidden_sum in sums:
        for member in (early[0], early[1], late[3], late[0], late[1], late[4], hidden_sum[0]):
            columns.append(member.reshape(SMALL * 4, -1))
    small = jnp.concatenate(columns, axis=1)
    changes = jnp.concatenate([early[2] + late[2] for early, late, _ in sums])
    return small.reshape((2, 2, 2, 2, 2, -1)), changes[None]


def cross(small, changes, axis, mine, move, add, *tokens):
    leaving = lax.dynamic_index_in_dim(small, 1 - mine, axis, keepdims=False)
    staying = lax.dynamic_index_in_dim(small, mine, axis, keepdims=False)
    moved = move(jnp.concatenate([leaving.reshape(-1), changes.reshape(-1)]))
    if tokens:
        moved = after(moved, *tokens)
    small = staying + moved[: leaving.size].reshape(leaving.shape)
    arrived = moved[leaving.size :].reshape(changes.shape)
    return small, changes + arrived if add else jnp.concatenate([changes, arrived], axis=0)


def relay(array, back):
    moves = layout_moves(back)
    moved = lax.ppermute(array, ("dp", "seq"), [(a, b) for a, b in moves if a != b])
    core, plane = lax.axis_index("dp") % 2, lax.axis_index("seq")
    return moved, lambda moved: jnp.where(plane == 3 * core, array, moved)


def fast_device(
    inputs,
    noise_buckets,
    first_gain,
    first_shift,
    attention_in,
    attention_out,
    attention_bias,
    second_gain,
    second_shift,
    expand_weight,
    expand_bias,
    reduce_weight,
    reduce_bias,
    time_table,
    cotangent,
):
    layers, width = first_gain.shape[0], inputs.shape[-1]
    count, planes = lax.axis_size("dp"), lax.axis_size("seq")
    me, plane = lax.axis_index("dp"), lax.axis_index("seq")
    sequence = (me // 2) * 2 + plane // 2

    kinds = [(kind, layer) for layer in range(layers) for kind in ("attention", "expand", "reduce")]
    raw_of = {"attention": (attention_in, attention_out), "expand": (expand_weight,), "reduce": (reduce_weight,)}
    members = (first_gain, first_shift, attention_bias, second_gain, second_shift, reduce_bias, expand_bias)
    gather = Gather(kinds, [raw_of[kind] for kind, _ in kinds], time_table, members, noise_buckets)
    moved, finish = relay(inputs[0], False)
    moved = finish(moved)
    token = gather.others((gather.first,))
    token = gather.step((moved, token))
    grad_low, finish = relay(after(cotangent[0], token), False)
    grad_low = finish(grad_low)
    gather.step((grad_low,))
    vectors, buckets = vectors_of(gather.extras(), members, layers, time_table.shape[1], width)

    saved = []
    stream = moved
    normed = first_norm(stream, vectors[0][0])
    for layer in range(layers):
        vec, bias = vectors[layer]
        attention_pack = gather.pack(3 * layer)
        own_keys = project(normed, attention_pack, 1, 2, (token,) if layer else ())
        chunks = spread_keys(own_keys)
        queries = project(normed, attention_pack, 0, 1, (own_keys,))
        token = gather.step((gather.prepare((queries,)), queries), queries)
        if layer == 0:
            token = gather.prepare((token,))
        mixture, tops = attend_fast(queries, chunks, (token,))
        if layer == 0:
            token = gather.step((mixture,), mixture)
            token = gather.prepare((token,))
        else:
            gather.cross(mixture)
            token = mixture
        packs = (attention_pack, gather.pack(3 * layer + 1), gather.pack(3 * layer + 2))
        next_vec = vectors[layer + 1][0] if layer + 1 < layers else None
        middle, own_kept, slope, result, following = feed_forward(
            normed, mixture, packs, stream, vec, bias, next_vec, (token,)
        )
        if layer == 0:
            token = gather.step((following,), following)
        saved.append([stream, own_kept, queries, chunks, tops, middle, slope, packs])
        stream, normed = result, following

    grad = grad_low
    lower, block = (grad_low, swap(after(grad_low, following), 1)), 0
    sums = [None] * layers
    shares = {}
    for entry in reversed(saved):
        entry[1] = (entry[1], swap(after(entry[1], following), 1))
    above = None
    for layer in reversed(range(layers)):
        vec, bias = vectors[layer]
        stream, kept, queries, chunks, tops, middle, slope, packs = saved[layer]
        of_reduce = Reduction(reduce_group(kept, lower, block), True)
        deps = ()
        if above is not None:
            upper_reduce, upper_expand, of_attention = above
            deps = (advance([of_attention], deps=(token,)),)
        *own_back, expand_bias_grad, middle_grad, late_sums, mixture_grad = feed_forward_back(
            grad, (lower[0], block), slope, middle, packs, vec, deps
        )
        if above is None:
            back = [(own, swap(own, 1)) for own in own_back]
            token = advance([of_reduce], deps=(own_back[0], saved[0][1][1]))
            deps = (token,) + tuple(other for _, other in back)
        else:
            deps = (upper_expand.second_x, upper_expand.second_y)
        query_grad, near, near_leave, far, far_leave = attend_fast_back(
            queries, chunks, kept[0], mixture_grad, tops, deps
        )
        far_leave, near_leave = swap(far_leave, 1), swap(near_leave, 1)
        token = query_grad
        if above is None:
            of_expand = Reduction(expand_group(kept, back))
            token = advance([of_expand], deps=(token,))
            token = advance(thirds=[of_reduce], deps=(token,))
        else:
            token = advance(thirds=[of_attention], deps=(token, upper_reduce.share, moved_result))
        far, near_leave = after(far, token, near_leave), after(near_leave, token)
        far = (wide(far) + wide(far_leave)).astype(bf16)
        far = (far, swap_seq(far, 1))
        token = far[0]
        if above is not None:
            back = [(own, swap(after(own, token), 1)) for own in own_back[:2]]
            of_expand = Reduction(expand_group(kept, back))
            token = advance([of_reduce], deps=(token, back[0][1], back[1][1], of_attention.second_x, of_attention.second_y))
            token = advance([of_expand], deps=(token,))
        deps = (token, of_expand.from_x, of_expand.from_y) if above is None else (token,)
        grad, own_lower, early_sums, key_grad = first_back(
            query_grad, (near, near_leave, far[1]), packs[0], stream, middle_grad, vec, deps
        )
        lower, block = (own_lower, swap(own_lower, 1)), 1
        key_grad = (key_grad, swap(key_grad, 1))
        if above is None:
            token = advance(thirds=[of_expand], fourths=[of_reduce], deps=(own_lower,))
            moved_result, finish = relay(after(result, token), True)
            outputs = finish(lax.optimization_barrier(moved_result)).astype(bf16)
        else:
            back.append((own_back[2], swap(after(own_back[2], own_lower), 1)))
            token = own_lower
            shares[("attention", layer + 1)] = of_attention
            shares[("expand", layer + 1)] = upper_expand
            upper_attention = of_attention
        of_attention = Reduction(attention_group(kept, back, lower, key_grad))
        shares[("reduce", layer)] = of_reduce
        above = (of_reduce, of_expand, of_attention)
        sums[layer] = (early_sums, late_sums, expand_bias_grad)

    of_reduce, of_expand, of_last = above
    token = advance(thirds=[of_reduce], joint=(upper_expand, upper_attention), deps=(token,))
    token = advance([of_last], deps=(token,))
    token = advance(fourths=[of_reduce], deps=(token,))
    token = advance(thirds=[of_expand], deps=(token,))
    token = advance(thirds=[of_last], deps=(token, upper_expand.share))
    token = advance(fourths=[of_expand], deps=(token,))
    small, changes = small_and_changes(sums)
    small, changes = after(small, token), after(changes, token)
    small, changes = cross(small, changes, 4, plane % 2, lambda a: swap_seq(a, 1), True)
    small, changes = cross(small, changes, 3, plane // 2, lambda a: swap_seq(a, 2), False)
    token = advance(fourths=[of_last], deps=(token, small, changes))
    input_grad, finish = relay(after(own_lower[:, TILE:], token), True)
    input_grad = finish(input_grad).astype(f32)
    shares[("attention", 0)] = of_last
    shares[("expand", 0)] = of_expand
    shares = {name: reduction.share.astype(f32) for name, reduction in shares.items()}

    small, changes = after(small, token), after(changes, token)
    small, changes = cross(small, changes, 2, me % 2, lambda a: swap(a, 1), True)
    small, changes = cross(small, changes, 1, (me // 2) % 2, lambda a: swap(a, 2), False)
    small, changes = cross(small, changes, 0, me // 4, lambda a: swap(a, 4), False)
    row = small.reshape(-1)
    small_out, start = [[] for _ in range(7)], 0
    for layer in range(layers):
        for member in range(7):
            size = (width if member < 6 else 4 * width) // (count * planes)
            small_out[member].append(row[start : start + size])
            start += size
    small_out = [jnp.stack(member) for member in small_out]
    entries = jnp.arange(count)
    owners = 2 * ((me // 2) ^ (entries // 2)) + ((plane // 2) ^ (entries % 2))
    source_buckets = jnp.sum(jnp.where(owners[:, None] == entries[None, :], buckets[None, :], 0), axis=1)
    table_grad = chosen_rows(changes, source_buckets, layers, width)

    ins, outs, expands, reduces = [], [], [], []
    for layer in range(layers):
        share = shares[("attention", layer)]
        pairs = share[:, width : 3 * width].reshape(share.shape[0], width // BLOCK, 2, BLOCK)
        ins.append(
            jnp.concatenate(
                [share[:, :width], pairs[:, :, 0].reshape(-1, width), pairs[:, :, 1].reshape(-1, width)], axis=1
            )
        )
        outs.append(share[:, 3 * width :])
        expands.append(shares[("expand", layer)])
        reduces.append(shares[("reduce", layer)])
    return (
        outputs[None],
        input_grad[None],
        small_out[0],
        small_out[1],
        jnp.stack(ins),
        jnp.stack(outs),
        small_out[2],
        small_out[3],
        small_out[4],
        jnp.stack(expands),
        small_out[6],
        jnp.stack(reduces),
        small_out[5],
        table_grad,
    )


def on_device(
    inputs,
    noise_buckets,
    first_gain,
    first_shift,
    attention_in,
    attention_out,
    attention_bias,
    second_gain,
    second_shift,
    expand_weight,
    expand_bias,
    reduce_weight,
    reduce_bias,
    time_table,
    cotangent,
):
    layers = first_gain.shape[0]
    count, planes = lax.axis_size("dp"), lax.axis_size("seq")
    me, plane = lax.axis_index("dp"), lax.axis_index("seq")
    model_width = inputs.shape[-1]
    table_rows = time_table.shape[1]

    stream = lax.ppermute(inputs[0], ("dp", "seq"), layout_moves(False)).astype(f32)

    sequence = (me // 2) * 2 + plane // 2
    packs = []
    for layer in range(layers):
        rows = [
            time_table[layer],
            pack_small(
                [
                    member[layer]
                    for member in (
                        first_gain,
                        first_shift,
                        attention_bias,
                        second_gain,
                        second_shift,
                        reduce_bias,
                        expand_bias,
                    )
                ],
                WIDE,
            ),
            jnp.broadcast_to(noise_buckets.astype(bf16)[:, None], (1, model_width)),
        ]
        packs.append(jnp.concatenate(rows, axis=0))

    def unpack(pack):
        stacked, sources, _ = gather_small(pack, ("dp",))
        slot = me ^ jnp.arange(count) if count == SMALL else jnp.arange(count)
        per_pack = stacked.shape[1]
        flat = stacked.reshape(count * per_pack, model_width)

        def place(index):
            return (me ^ index) if count == SMALL else index

        buckets = jnp.stack(
            [lax.dynamic_index_in_dim(flat, place(index) * per_pack + per_pack - 1, 0, False)[0] for index in range(count)]
        ).astype(jnp.int32)
        bucket = lax.dynamic_index_in_dim(buckets, sequence, 0, False)
        row = place(bucket // table_rows) * per_pack + bucket % table_rows
        scaling = lax.dynamic_slice_in_dim(flat, row, 1, 0).astype(f32)
        vectors = jnp.stack(
            [
                lax.dynamic_slice_in_dim(
                    flat, place(index) * per_pack + table_rows, per_pack - 1 - table_rows, 0
                ).reshape(-1)
                for index in range(count)
            ]
        ).astype(f32)
        share = model_width // count
        members = [vectors[:, i * share : (i + 1) * share].reshape(1, -1) for i in range(6)]
        members.append(vectors[:, 6 * share : 6 * share + expand_bias.shape[1]].reshape(1, -1))
        return tuple(members) + (scaling,), buckets

    keys_at = model_width
    shards = []
    for layer in range(layers):
        shards += [
            attention_in[layer][:, keys_at:],
            attention_in[layer][:, :keys_at],
            attention_out[layer],
            expand_weight[layer],
            reduce_weight[layer],
        ]
    gathered = []
    for position, shard in enumerate(shards):
        if count == SMALL and position >= 2:
            shard = after(shard, gathered[position - 2][2], gathered[position - 2][4])
        gathered.append(gather_rows(shard, position % 2))

    all_vectors, buckets = [], None
    for layer in range(layers):
        vectors, buckets = unpack(packs[layer])
        all_vectors.append(vectors)

    saved, all_weights = [], []
    for layer in range(layers):
        w_keys, w_query, w_out, w_expand, w_reduce = gathered[5 * layer : 5 * layer + 5]
        weights = (w_query, w_keys, w_out, w_expand, w_reduce)
        all_weights.append(weights)
        stream, kept = layer_forward(stream, weights, all_vectors[layer])
        saved.append(kept)
    back_moves = layout_moves(True)
    outputs = lax.ppermute(stream.astype(bf16), ("dp", "seq"), back_moves)[None]

    grad_flow = lax.ppermute(cotangent[0], ("dp", "seq"), layout_moves(False)).astype(f32)
    dense, small, modulation = [None] * layers, [None] * layers, [None] * layers
    for layer in reversed(range(layers)):
        grad_flow, dense[layer], small[layer], modulation[layer] = layer_backward(
            saved[layer], all_weights[layer], all_vectors[layer], grad_flow
        )
    input_grad = lax.ppermute(grad_flow, ("dp", "seq"), back_moves)[None]

    devices = count * planes
    packed = jnp.concatenate(
        [member.reshape(devices, -1) for layer in range(layers) for member in small[layer]], axis=1
    )
    row = scatter_small(packed)
    small_out, start = [[] for _ in range(7)], 0
    for layer in range(layers):
        for member in range(7):
            width = small[layer][member].size // devices
            small_out[member].append(row[start : start + width])
            start += width
    small_out = [jnp.stack(member) for member in small_out]

    changes, from_dp, from_seq = gather_small(jnp.concatenate(modulation), ("dp", "seq"))
    table_grad = table_rows_of(changes, from_dp, from_seq, buckets, layers, model_width)

    dense_out = [jnp.stack([dense[layer][member] for layer in range(layers)]) for member in range(4)]
    return (
        outputs,
        input_grad,
        small_out[0],
        small_out[1],
        dense_out[0],
        dense_out[1],
        small_out[2],
        small_out[3],
        small_out[4],
        dense_out[2],
        small_out[6],
        dense_out[3],
        small_out[5],
        table_grad,
    )


def solution(mesh):
    eight_way = mesh.shape["dp"] == SMALL and mesh.shape["seq"] == 4
    return jax.shard_map(
        fast_device if eight_way else on_device,
        mesh=mesh,
        in_specs=(
            P("dp", "seq", None),
            P("dp"),
            P(None, "dp"),
            P(None, "dp"),
            P(None, "dp", None),
            P(None, "dp", None),
            P(None, "dp"),
            P(None, "dp"),
            P(None, "dp"),
            P(None, "dp", None),
            P(None, "dp"),
            P(None, "dp", None),
            P(None, "dp"),
            P(None, "dp", None),
            P("dp", "seq", None),
        ),
        out_specs=(
            P("dp", "seq", None),
            P("dp", "seq", None),
            P(None, ("dp", "seq")),
            P(None, ("dp", "seq")),
            P(None, ("dp", "seq"), None),
            P(None, ("dp", "seq"), None),
            P(None, ("dp", "seq")),
            P(None, ("dp", "seq")),
            P(None, ("dp", "seq")),
            P(None, ("dp", "seq"), None),
            P(None, ("dp", "seq")),
            P(None, ("dp", "seq"), None),
            P(None, ("dp", "seq")),
            P(None, ("dp", "seq"), None),
        ),
        check_vma=False,
    )
```

```python
import functools
import math

import jax
import jax.numpy as jnp
from jax import lax
from jax.experimental import pallas as pl
from jax.experimental.pallas import tpu as pltpu
from jax.sharding import PartitionSpec as P

HEAD = 64
BUCKETS = 256
SMALL = 8
WIDE = 1024

epsilon = 1e-05
bf16 = jnp.bfloat16
f32 = jnp.float32


def modulated_norm(activations, norm_gain, norm_shift, scaling):
    center = activations - jnp.mean(activations, axis=-1, keepdims=True)
    spread = jnp.mean(center * center, axis=-1, keepdims=True)
    return (center * lax.rsqrt(spread + epsilon) * norm_gain + norm_shift) * (1.0 + scaling)


def swap(array, bit):
    count = lax.axis_size("dp")
    return lax.ppermute(array, "dp", [(i, i ^ bit) for i in range(count)])


def swap_seq(array, bit):
    count = lax.axis_size("seq")
    return lax.ppermute(array, "seq", [(i, i ^ bit) for i in range(count)])


def after(array, *earlier):
    return lax.optimization_barrier((array,) + earlier)[0]


def layout_moves(back):
    moves = []
    for index in range(lax.axis_size("dp")):
        core, pair = index % 2, index - index % 2
        for plane in range(4):
            source = index * 4 + plane
            target = (pair + plane % 2) * 4 + 2 * core + plane // 2
            moves.append((target, source) if back else (source, target))
    return moves


def gather_rows(shard, route):
    if lax.axis_size("dp") != SMALL:
        return lax.all_gather(shard, "dp", axis=0, tiled=True)
    along_x = swap(shard, 2)
    along_y = swap(shard, 4)
    across = swap(along_x, 4) if route == 0 else swap(along_y, 2)
    mine = [shard, along_x, along_y, across]
    parts = []
    for part in mine:
        parts += [part, swap(part, 1)]
    return parts


def order_of(parts):
    me = lax.axis_index("dp")
    return [me ^ bit for bit in range(parts)]


def scatter_dense(left, right, orders):
    count, planes = lax.axis_size("dp"), lax.axis_size("seq")
    rows, columns = left.shape[1], right.shape[1]
    if count != SMALL:
        whole = jnp.einsum("tr,tc->rc", left, right, preferred_element_type=f32)
        return lax.psum_scatter(whole, ("dp", "seq"), scatter_dimension=0, tiled=True)
    me, plane = lax.axis_index("dp"), lax.axis_index("seq")
    block = rows // count
    width = columns // len(orders)

    def pick(masks):
        return jnp.concatenate(
            [lax.dynamic_slice_in_dim(left, (me ^ mask) * block, block, 1) for mask in masks], axis=1
        )

    def product(a, b):
        return jnp.einsum("tr,tc->rc", a, b, preferred_element_type=f32)

    pieces = []
    for position, (first, second) in enumerate(orders):
        part = right[:, position * width : (position + 1) * width]
        masks = [first | second, first, second, 0]
        arrived = swap(product(pick([mask | 1 for mask in masks]), part).astype(bf16), 1)
        half = 2 * block
        leaving = (product(pick(masks[:2]), part) + arrived[:half].astype(f32)).astype(bf16)
        staying = (product(pick(masks[2:]), part) + arrived[half:].astype(f32)).astype(bf16)
        arrived = swap(leaving, first)
        leaving = (staying[:block].astype(f32) + arrived[:block].astype(f32)).astype(bf16)
        staying = (staying[block:].astype(f32) + arrived[block:].astype(f32)).astype(bf16)
        arrived = swap(leaving, second)
        pieces.append((staying, arrived))
    total = jnp.concatenate([(a.astype(f32) + b.astype(f32)).astype(bf16) for a, b in pieces], axis=1)
    return scatter_planes(total, plane, planes)


def scatter_planes(total, plane, planes):
    rows, columns = total.shape
    low, high = plane & 1, plane >> 1
    cut = total.reshape(2, 2, rows // planes, columns)
    arrived = swap_seq(lax.dynamic_index_in_dim(cut, 1 - low, 1, keepdims=False), 1)
    kept = lax.dynamic_index_in_dim(cut, low, 1, keepdims=False)
    joined = kept.astype(f32) + arrived.astype(f32)
    arrived = swap_seq(lax.dynamic_index_in_dim(joined, 1 - high, 0, keepdims=False).astype(bf16), 2)
    return lax.dynamic_index_in_dim(joined, high, 0, keepdims=False) + arrived.astype(f32)


def scatter_small(array):
    count, planes = lax.axis_size("dp"), lax.axis_size("seq")
    if count != SMALL:
        return lax.psum_scatter(array, ("dp", "seq"), scatter_dimension=0, tiled=True)[0]
    me, plane = lax.axis_index("dp"), lax.axis_index("seq")
    columns = array.shape[1]
    shape = [count, planes]
    current = array.reshape(shape[0], shape[1], columns)
    for axis, index, send in ((0, me, swap), (1, plane, swap_seq)):
        bit = 1
        while current.shape[axis] > 1:
            pairs = current.shape[axis] // 2
            view = jnp.moveaxis(current, axis, 0).reshape(pairs, 2, -1, columns)
            mine = (index // bit) % 2
            leaving = lax.dynamic_index_in_dim(view, 1 - mine, 1, keepdims=False)
            staying = lax.dynamic_index_in_dim(view, mine, 1, keepdims=False)
            current = jnp.moveaxis((staying + send(leaving, bit)).reshape(pairs, -1, columns), 0, axis)
            bit *= 2
    return current.reshape(columns)


def gather_small(array, axes):
    if lax.axis_size("dp") != SMALL:
        stacked = lax.all_gather(array, axes, axis=0, tiled=False)
        stacked = stacked.reshape((-1,) + array.shape)
        places = jnp.arange(stacked.shape[0])
        if "seq" in axes:
            planes = lax.axis_size("seq")
            return stacked, places // planes, places % planes
        return stacked, places, None
    current = array[None]
    me = lax.axis_index("dp")
    for bit in (1, 2, 4):
        current = jnp.concatenate([current, swap(current, bit)], axis=0)
    sources = me ^ jnp.arange(SMALL)
    if "seq" not in axes:
        return current, sources, None
    plane = lax.axis_index("seq")
    for bit in (1, 2):
        current = jnp.concatenate([current, swap_seq(current, bit)], axis=0)
    places = jnp.arange(SMALL * 4)
    return current, me ^ (places % SMALL), plane ^ (places // SMALL)


def times(a, weight, out_type):
    return jnp.dot(a, weight, preferred_element_type=f32).astype(out_type)


def times_transposed(a, weight, out_type):
    return lax.dot_general(a, weight, (((1,), (1,)), ((), ())), preferred_element_type=f32).astype(out_type)


def spread_keys(own):
    far = swap_seq(own, 1)
    return [own, swap(own, 1), far, swap(far, 1)]


def heads_of(rows):
    return rows.reshape(rows.shape[0], rows.shape[1] // HEAD, HEAD)


def attend(queries, chunks):
    model_width = queries.shape[1]
    whole = jnp.concatenate(chunks, axis=0)
    key_heads, value_heads = heads_of(whole[:, :model_width]), heads_of(whole[:, model_width:])
    scores = jnp.einsum("qhd,khd->hqk", heads_of(queries), key_heads, preferred_element_type=f32)
    scores = scores * (1.0 / math.sqrt(HEAD))
    exponent = jnp.exp(scores - jnp.max(scores, axis=-1, keepdims=True))
    probs = exponent / jnp.sum(exponent, axis=-1, keepdims=True)
    probs_low = probs.astype(bf16)
    mixture = jnp.einsum("hqk,khd->qhd", probs_low, value_heads, preferred_element_type=f32)
    return mixture.reshape(queries.shape).astype(bf16), (probs, probs_low)


def attend_back(queries, chunks, kept, mixture, mixture_grad):
    probs, probs_low = kept
    model_width = queries.shape[1]
    factor = 1.0 / math.sqrt(HEAD)
    whole = jnp.concatenate(chunks, axis=0)
    key_heads, value_heads = heads_of(whole[:, :model_width]), heads_of(whole[:, model_width:])
    grad_heads = heads_of(mixture_grad)
    prob_grad = jnp.einsum("qhd,khd->hqk", grad_heads, value_heads, preferred_element_type=f32)
    along = jnp.sum(probs * prob_grad, axis=-1, keepdims=True)
    score_grad = (probs * (prob_grad - along)).astype(bf16)
    query_grad = jnp.einsum("hqk,khd->qhd", score_grad, key_heads, preferred_element_type=f32)
    query_grad = (query_grad * factor).astype(bf16).reshape(queries.shape)
    key_part = jnp.einsum("hqk,qhd->khd", score_grad, heads_of(queries), preferred_element_type=f32)
    value_part = jnp.einsum("hqk,qhd->khd", probs_low, grad_heads, preferred_element_type=f32)
    parts = jnp.concatenate(
        [
            (key_part * factor).reshape(whole.shape[0], model_width),
            value_part.reshape(whole.shape[0], model_width),
        ],
        axis=1,
    ).astype(bf16)
    return query_grad, parts


def join_key_grads(parts):
    local = parts.shape[0] // 4
    cut = [parts[i * local : (i + 1) * local] for i in range(4)]
    far = cut[2].astype(f32) + swap(cut[3], 1).astype(f32)
    far = swap_seq(far.astype(bf16), 1)
    near = cut[0].astype(f32) + swap(cut[1], 1).astype(f32)
    return (near + far.astype(f32)).astype(bf16)


def layer_forward(stream, weights, vectors):
    w_query, w_keys, w_out, w_expand, w_reduce = weights
    first_gain, first_shift, attention_bias, second_gain, second_shift, reduce_bias, expand_bias, scaling = vectors
    normed = modulated_norm(stream, first_gain, first_shift, scaling).astype(bf16)
    chunks = spread_keys(times(normed, w_keys, bf16))
    queries = times(normed, w_query, bf16)
    mixture, kept = attend(queries, chunks)
    middle = stream + (times(mixture, w_out, f32) + attention_bias)
    second = modulated_norm(middle, second_gain, second_shift, scaling).astype(bf16)
    hidden = times(second, w_expand, f32) + expand_bias
    active = jax.nn.gelu(hidden).astype(bf16)
    result = middle + (times(active, w_reduce, f32) + reduce_bias)
    return result, (stream, normed, queries, chunks, kept, mixture, middle, second, hidden, active)


def layer_backward(saved, weights, vectors, grad_out):
    w_query, w_keys, w_out, w_expand, w_reduce = weights
    first_gain, first_shift, attention_bias, second_gain, second_shift, reduce_bias, expand_bias, scaling = vectors
    stream, normed, queries, chunks, kept, mixture, middle, second, hidden, active = saved
    both = ((2, 4), (4, 2))
    grad_low = grad_out.astype(bf16)
    reduce_bias_grad = jnp.sum(grad_out, axis=0)
    reduce_weight_grad = scatter_dense(active, grad_low, both)
    active_grad = times_transposed(grad_low, w_reduce, f32)
    hidden_grad = jax.vjp(jax.nn.gelu, hidden)[1](active_grad)[0]
    expand_bias_grad = jnp.sum(hidden_grad, axis=0)
    hidden_low = hidden_grad.astype(bf16)
    second_grad = times_transposed(hidden_low, w_expand, f32)
    expand_weight_grad = scatter_dense(second, hidden_low, both)
    _, second_back = jax.vjp(modulated_norm, middle, second_gain, second_shift, scaling)
    middle_part, second_gain_grad, second_shift_grad, second_scaling_grad = second_back(second_grad)
    middle_grad = grad_out + middle_part
    attention_bias_grad = jnp.sum(middle_grad, axis=0)
    middle_low = middle_grad.astype(bf16)
    mixture_grad = times_transposed(middle_low, w_out, bf16)
    attention_out_grad = scatter_dense(mixture, middle_low, both)
    query_grad, parts = attend_back(queries, chunks, kept, mixture, mixture_grad)
    key_grad = join_key_grads(parts)
    normed_grad = times_transposed(query_grad, w_query, f32) + times_transposed(key_grad, w_keys, f32)
    project_grad = jnp.concatenate([query_grad, key_grad], axis=1)
    attention_in_grad = scatter_dense(normed, project_grad, both)
    _, first_back = jax.vjp(modulated_norm, stream, first_gain, first_shift, scaling)
    stream_part, first_gain_grad, first_shift_grad, first_scaling_grad = first_back(normed_grad)
    stream_grad = middle_grad + stream_part
    small = (
        first_gain_grad,
        first_shift_grad,
        attention_bias_grad,
        second_gain_grad,
        second_shift_grad,
        reduce_bias_grad,
        expand_bias_grad,
    )
    dense = (attention_in_grad, attention_out_grad, expand_weight_grad, reduce_weight_grad)
    return stream_grad, dense, small, (first_scaling_grad + second_scaling_grad)[0]


def pack_small(vectors, rows):
    flat = jnp.concatenate([vector.reshape(-1) for vector in vectors])
    length = -(-flat.shape[0] // WIDE) * WIDE
    return jnp.pad(flat, (0, length - flat.shape[0])).reshape(-1, WIDE)


def table_rows_of(changes, from_dp, from_seq, buckets, layers, model_width):
    count, planes = lax.axis_size("dp"), lax.axis_size("seq")
    owners = (from_dp // 2) * 2 + from_seq // 2
    source_buckets = jnp.sum(
        jnp.where(owners[:, None] == jnp.arange(count)[None, :], buckets[None, :], 0), axis=1
    )
    return chosen_rows(changes, source_buckets, layers, model_width)


def chosen_rows(changes, source_buckets, layers, model_width):
    count, planes = lax.axis_size("dp"), lax.axis_size("seq")
    table_share = BUCKETS // (count * planes)
    first_row = (lax.axis_index("dp") * planes + lax.axis_index("seq")) * table_share
    chosen = (source_buckets[None, :] == (first_row + jnp.arange(table_share))[:, None]).astype(f32)
    table_grad = jnp.dot(chosen, changes, precision=lax.Precision.HIGHEST)
    return jnp.stack(
        [table_grad[:, layer * model_width : (layer + 1) * model_width] for layer in range(layers)]
    )


VMEM_LIMIT = 65_400 * 1024
TILE = 1024
BLOCK = 128
NT = (((1,), (1,)), ((), ()))
TN = (((0,), (0,)), ((), ()))


def whole_spec(array):
    zeros = (0,) * len(array.shape)
    return pl.BlockSpec(array.shape, lambda *_: zeros)


def run(body, grid, inputs, outputs, scratch=(), deps=(), aliases=(), cost=4):
    deps = tuple(aliases) + tuple(deps)
    arrays = [array for array, _ in inputs]
    specs = [spec if spec is not None else whole_spec(array) for array, spec in inputs]
    shapes = [jax.ShapeDtypeStruct(shape, kind) for shape, kind, _ in outputs]
    out_specs = [
        spec if spec is not None else whole_spec(shape) for shape, (_, _, spec) in zip(shapes, outputs)
    ]
    count, extra = len(arrays), len(deps)

    def kernel(place, *refs):
        body(place, refs[:count], refs[count + extra : count + extra + len(shapes)], refs[count + extra + len(shapes) :])

    place = jnp.stack([lax.axis_index("dp"), lax.axis_index("seq")]).astype(jnp.int32)
    return pl.pallas_call(
        kernel,
        out_shape=shapes,
        grid_spec=pltpu.PrefetchScalarGridSpec(
            num_scalar_prefetch=1,
            grid=(grid,),
            in_specs=specs + [pl.BlockSpec(memory_space=pl.ANY)] * extra,
            out_specs=out_specs,
            scratch_shapes=list(scratch),
        ),
        input_output_aliases={1 + count + i: i for i in range(len(aliases))},
        compiler_params=pltpu.CompilerParams(vmem_limit_bytes=VMEM_LIMIT),
        cost_estimate=pl.CostEstimate(flops=0, bytes_accessed=cost * 3_000_000, transcendentals=0),
    )(place, *arrays, *deps)


class Flow:
    def __init__(self, sems):
        self.sems, self.count, self.pending = sems, 0, {}

    def start(self, key, source, target):
        copy = pltpu.make_async_copy(source, target, self.sems.at[self.count])
        self.count += 1
        copy.start()
        self.pending.setdefault(key, []).append(copy)

    def wait(self, key):
        for copy in self.pending.pop(key):
            copy.wait()

    def drain(self):
        for key in list(self.pending):
            self.wait(key)

    def pack(self, key, pack, refs, target, first, columns):
        at = 0
        for (_, block, rows), ref in zip(pack, refs):
            self.start(
                key,
                ref.at[pl.ds(block * rows, rows), pl.ds(first, columns)],
                target.at[pl.ds(at, rows), :] if target.shape[1] == columns else target.at[pl.ds(at, rows), pl.ds(first, columns)],
            )
            at += rows


def run_flow(body, arrays, packs, outputs, scratch, copies, deps=(), cost=8):
    buffers = [buffer for pack in packs for buffer, _, _ in pack]
    count, extra, made = len(arrays), len(buffers), len(outputs)

    def kernel(place, *refs):
        outs = refs[count + extra + len(deps) :][:made]
        held = refs[count + extra + len(deps) + made : -1]
        weights, at = [], count
        for pack in packs:
            weights.append(refs[at : at + len(pack)])
            at += len(pack)
        body(place, Flow(refs[-1]), refs[:count], weights, outs, held)

    place = jnp.stack([lax.axis_index("dp"), lax.axis_index("seq")]).astype(jnp.int32)
    anywhere = pl.BlockSpec(memory_space=pl.ANY)
    return pl.pallas_call(
        kernel,
        out_shape=[jax.ShapeDtypeStruct(shape, kind) for shape, kind in outputs],
        in_specs=[pl.BlockSpec(memory_space=pltpu.SMEM)] + [anywhere] * (count + extra + len(deps)),
        out_specs=[anywhere] * made,
        scratch_shapes=[pltpu.VMEM(shape, kind) for shape, kind in scratch] + [pltpu.SemaphoreType.DMA((copies,))],
        compiler_params=pltpu.CompilerParams(vmem_limit_bytes=VMEM_LIMIT),
        cost_estimate=pl.CostEstimate(flops=0, bytes_accessed=cost * 3_000_000, transcendentals=0),
    )(place, *arrays, *buffers, *deps)


def join(refs):
    return jnp.concatenate([ref[...] for ref in refs], axis=0)


def block_at(place, part, stride=BLOCK, offset=0):
    return pl.ds(pl.multiple_of((place[0] ^ part) * stride + offset, BLOCK), BLOCK)


def columns_in_order(place, ref, stride=BLOCK, offset=0):
    return jnp.concatenate(
        [ref[:, block_at(place, part, stride, offset)] for part in range(SMALL)], axis=1
    )


def normalise(v):
    center = v - jnp.mean(v, axis=-1, keepdims=True)
    inverse = lax.rsqrt(jnp.mean(center * center, axis=-1, keepdims=True) + epsilon)
    return center * inverse, inverse


def modulated(v, vec, gain_row):
    unit, _ = normalise(v)
    return (unit * vec[gain_row : gain_row + 1, :] + vec[gain_row + 1 : gain_row + 2, :]) * vec[6:7, :]


def modulated_back(v, vec, gain_row, grad):
    unit, inverse = normalise(v)
    gain, shift, scale = vec[gain_row : gain_row + 1, :], vec[gain_row + 1 : gain_row + 2, :], vec[6:7, :]
    scale_grad = jnp.sum(grad * (unit * gain + shift), axis=0, keepdims=True)
    inner = grad * scale
    gain_grad = jnp.sum(inner * unit, axis=0, keepdims=True)
    shift_grad = jnp.sum(inner, axis=0, keepdims=True)
    inner = inner * gain
    back = inverse * (
        inner
        - jnp.mean(inner, axis=-1, keepdims=True)
        - unit * jnp.mean(inner * unit, axis=-1, keepdims=True)
    )
    return back, gain_grad, shift_grad, scale_grad


ROOT = math.sqrt(2.0 / math.pi)
CUBIC = 0.044715


def first_norm(x, vec, deps=()):
    def body(place, ins, outs, _):
        outs[0][...] = modulated(ins[0][...].astype(f32), ins[1], 0).astype(bf16)

    return run(body, 1, [(x, None), (vec, None)], [(x.shape, bf16, None)], deps=deps)[0]


def project(a, pack, first_tile, tiles, deps=()):
    tokens, width = a.shape

    def body(place, flow, ins, packs, outs, scratch):
        a_ref, weights, result, ordered = scratch
        flow.start("a", ins[0], a_ref)
        for tile in range(tiles):
            flow.pack(tile, pack, packs[0], weights.at[tile], (first_tile + tile) * TILE, TILE)
        flow.wait("a")
        ordered[...] = columns_in_order(place, a_ref)
        for tile in range(tiles):
            flow.wait(tile)
            at = pl.ds(tile * TILE, TILE)
            result[:, at] = jnp.dot(ordered[...], weights[tile], preferred_element_type=f32).astype(bf16)
            flow.start("out", result.at[:, at], outs[0].at[:, at])
        flow.drain()

    return run_flow(
        body,
        [a],
        [pack],
        [((tokens, tiles * TILE), bf16)],
        [(a.shape, bf16), ((tiles, width, TILE), bf16), ((tokens, tiles * TILE), bf16), (a.shape, bf16)],
        1 + tiles * (len(pack) + 1),
        deps,
        4,
    )[0]


def key_specs(chunks):
    return [
        (chunk, pl.BlockSpec((chunk.shape[0], 4 * HEAD), lambda i, s: (0, i))) for chunk in chunks
    ]


def head_masks(rows):
    lane = lax.broadcasted_iota(jnp.int32, (rows, 2 * HEAD), 1)
    return lane < HEAD, lane >= HEAD


def both_heads(rows):
    zeros = jnp.zeros_like(rows)
    return jnp.concatenate([jnp.where(mask, rows, zeros) for mask in head_masks(rows.shape[0])], axis=0)


def attend_fast(queries, chunks, deps=()):
    tokens, width = queries.shape
    pairs = width // (2 * HEAD)

    def body(place, ins, outs, _):
        both = join(ins[1:5])
        keys, values = both[:, : 2 * HEAD], both[:, 2 * HEAD :]
        query = both_heads(ins[0][...] * jnp.asarray(1.0 / math.sqrt(HEAD), bf16))
        scores = lax.dot_general(keys, query, NT, preferred_element_type=f32)
        most = jnp.max(scores, axis=0, keepdims=True)
        exponent = jnp.exp(scores - most)
        total = jnp.sum(exponent, axis=0, keepdims=True)
        mixed = lax.dot_general(values, exponent.astype(bf16), TN, preferred_element_type=f32)
        halves = [
            mixed[head * HEAD : (head + 1) * HEAD, head * tokens : (head + 1) * tokens]
            / total[:, head * tokens : (head + 1) * tokens]
            for head in range(2)
        ]
        outs[0][...] = jnp.concatenate(halves, axis=0).T.astype(bf16)
        top = most + jnp.log(total)
        outs[1][0, 0:1, :] = top[:, :tokens]
        outs[1][0, 1:2, :] = top[:, tokens:]

    return run(
        body,
        pairs,
        [(queries, pl.BlockSpec((tokens, 2 * HEAD), lambda i, s: (0, i)))] + key_specs(chunks),
        [
            (queries.shape, bf16, pl.BlockSpec((tokens, 2 * HEAD), lambda i, s: (0, i))),
            ((pairs, 8, tokens), f32, pl.BlockSpec((1, 8, tokens), lambda i, s: (i, 0, 0))),
        ],
        deps=deps,
        cost=15,
    )


def attend_fast_back(queries, chunks, kept, mixture_grad, tops, deps=()):
    tokens, width = queries.shape
    pairs = width // (2 * HEAD)

    def body(place, ins, outs, _):
        both = join(ins[1:5])
        keys, values = both[:, : 2 * HEAD], both[:, 2 * HEAD :]
        scaled = ins[0][...] * jnp.asarray(1.0 / math.sqrt(HEAD), bf16)
        grads = ins[6][...]
        masks = head_masks(tokens)
        select = jnp.concatenate([mask[0:1].astype(f32) for mask in masks] + [jnp.zeros((6, 2 * HEAD), f32)], axis=0)
        along = lax.dot_general(
            select,
            ins[5][...].astype(f32) * grads.astype(f32),
            NT,
            precision=lax.Precision.HIGHEST,
            preferred_element_type=f32,
        )
        query, grad = both_heads(scaled), both_heads(grads)
        scores = lax.dot_general(keys, query, NT, preferred_element_type=f32)
        top = jnp.concatenate([ins[7][0, head : head + 1, :] for head in range(2)], axis=1)
        probs = jnp.exp(scores - top)
        prob_grad = lax.dot_general(values, grad, NT, preferred_element_type=f32)
        pulled = jnp.concatenate([along[head : head + 1, :] for head in range(2)], axis=1)
        score_grad = (probs * (prob_grad - pulled)).astype(bf16)
        key_grad = jnp.dot(score_grad, query, preferred_element_type=f32)
        value_grad = jnp.dot(probs.astype(bf16), grad, preferred_element_type=f32)
        query_part = lax.dot_general(keys, score_grad, TN, preferred_element_type=f32)
        halves = [
            query_part[head * HEAD : (head + 1) * HEAD, head * tokens : (head + 1) * tokens] for head in range(2)
        ]
        query_grad = jnp.concatenate(halves, axis=0) * (1.0 / math.sqrt(HEAD))
        outs[0][...] = query_grad.T.astype(bf16)
        for chunk in range(4):
            rows = slice(chunk * tokens, (chunk + 1) * tokens)
            outs[1 + chunk][:, : 2 * HEAD] = key_grad[rows].astype(bf16)
            outs[1 + chunk][:, 2 * HEAD :] = value_grad[rows].astype(bf16)

    pair_spec = pl.BlockSpec((tokens, 2 * HEAD), lambda i, s: (0, i))
    part = ((tokens, 2 * width), bf16, pl.BlockSpec((tokens, 4 * HEAD), lambda i, s: (0, i)))
    return run(
        body,
        pairs,
        [(queries, pair_spec)]
        + key_specs(chunks)
        + [
            (kept, pl.BlockSpec((tokens, 2 * HEAD), lambda i, s: (0, MIXTURE // (2 * HEAD) + i))),
            (mixture_grad, pair_spec),
            (tops, pl.BlockSpec((1, 8, tokens), lambda i, s: (i, 0, 0))),
        ],
        [(queries.shape, bf16, pair_spec)] + [part] * 4,
        deps=deps,
        cost=18,
    )


ACTIVE, SECOND, MIXTURE, NORMED, KEPT = 0, 4 * TILE, 5 * TILE, 6 * TILE, 7 * TILE


def columns(tile, count=1):
    return pl.ds(tile * TILE, count * TILE)


def feed_forward(normed, mixture, packs, stream, vec, bias, next_vec, deps=()):
    tokens, width = mixture.shape
    hidden_width = bias.shape[1]
    half = 2 * TILE

    def body(place, flow, ins, weights, outs, scratch):
        (mixture_ref, stream_ref, vec_ref, next_ref, bias_ref, kept, w_out, w_expand, w_reduce) = scratch[:9]
        (middle, slope, result, following, ordered) = scratch[9:]
        flow.start("first", ins[0], mixture_ref)
        flow.start("first", ins[2], vec_ref)
        flow.pack("out", packs[0], weights[0], w_out, 3 * TILE, TILE)
        flow.start("out", ins[1], stream_ref)
        flow.start("out", ins[4], bias_ref)
        for number in range(2):
            flow.pack(f"expand{number}", packs[1], weights[1], w_expand, number * half, half)
        flow.start("normed", ins[5], kept.at[:, pl.ds(NORMED, TILE)])
        flow.start("next", ins[3], next_ref)
        for number in range(2):
            flow.pack(f"reduce{number}", packs[2], weights[2], w_reduce, number * half, half)

        flow.wait("first")
        kept[:, MIXTURE:NORMED] = mixture_ref[...]
        ordered[...] = columns_in_order(place, mixture_ref)
        flow.wait("out")
        branch = jnp.dot(ordered[...], w_out[...], preferred_element_type=f32)
        middle[...] = stream_ref[...].astype(f32) + (branch + vec_ref[2:3, :])
        flow.start("middle", middle, outs[0])
        kept[:, SECOND:MIXTURE] = modulated(middle[...], vec_ref, 3).astype(bf16)
        ordered[...] = columns_in_order(place, kept, BLOCK, SECOND)
        for tile in range(4):
            if tile % 2 == 0:
                flow.wait(f"expand{tile // 2}")
            at = columns(tile)
            hidden = jnp.dot(ordered[...], w_expand[:, at], preferred_element_type=f32) + bias_ref[:, at]
            square = hidden * hidden
            bent = jnp.tanh(ROOT * hidden * (1.0 + CUBIC * square))
            share = 0.5 * (1.0 + bent)
            kept[:, at] = (hidden * share).astype(bf16)
            steep = share + (0.5 * ROOT) * hidden * (1.0 - bent * bent) * (1.0 + (3.0 * CUBIC) * square)
            slope[:, at] = steep.astype(bf16)
            if tile == 1:
                flow.start("slope", slope.at[:, columns(0, 2)], outs[2].at[:, columns(0, 2)])
        flow.start("slope", slope.at[:, columns(2, 2)], outs[2].at[:, columns(2, 2)])
        flow.wait("normed")
        flow.start("kept", kept, outs[1])
        for tile in range(4):
            if tile % 2 == 0:
                flow.wait(f"reduce{tile // 2}")
            a = columns_in_order(place, kept, 4 * BLOCK, tile * BLOCK)
            product = jnp.dot(a, w_reduce[:, columns(tile)], preferred_element_type=f32)
            result[...] = product if tile == 0 else result[...] + product
        result[...] = middle[...] + (result[...] + vec_ref[5:6, :])
        flow.start("result", result, outs[3])
        flow.wait("next")
        if next_vec is None:
            following[...] = result[...].astype(bf16)
        else:
            following[...] = modulated(result[...], next_ref, 0).astype(bf16)
        flow.start("following", following, outs[4])
        flow.drain()

    wide_shape = (tokens, hidden_width)
    rows = SMALL * BLOCK
    return run_flow(
        body,
        [mixture, stream, vec, vec if next_vec is None else next_vec, bias, normed],
        packs,
        [(mixture.shape, f32), ((tokens, KEPT), bf16), (wide_shape, bf16), (mixture.shape, f32), (mixture.shape, bf16)],
        [
            (mixture.shape, bf16),
            (stream.shape, stream.dtype),
            (vec.shape, f32),
            (vec.shape, f32),
            (bias.shape, f32),
            ((tokens, KEPT), bf16),
            ((rows, TILE), bf16),
            ((rows, hidden_width), bf16),
            ((rows, hidden_width), bf16),
            (mixture.shape, f32),
            (wide_shape, bf16),
            (mixture.shape, f32),
            (mixture.shape, bf16),
            (mixture.shape, bf16),
        ],
        6 + 5 * len(packs[0]) + 6,
        deps,
        12,
    )


def feed_forward_back(grad, grad_low, slope, middle, packs, vec, deps=()):
    tokens, width = grad.shape
    hidden_width = slope.shape[1]
    low, low_block = grad_low
    half = 2 * TILE

    def body(place, flow, ins, weights, outs, scratch):
        (grad_ref, low_ref, slope_ref, middle_ref, vec_ref, w_out, w_expand, w_reduce) = scratch[:8]
        (hidden, bias, middle_grad, middle_low, sums, mixture, total, ordered) = scratch[8:]
        flow.start("low", ins[1].at[:, columns(low_block)], low_ref)
        flow.pack("reduce0", packs[2], weights[2], w_reduce, 0, half)
        flow.start("slope", ins[2], slope_ref)
        flow.pack("reduce1", packs[2], weights[2], w_reduce, half, half)
        for number in range(2):
            flow.pack(f"expand{number}", packs[1], weights[1], w_expand, number * half, half)
        flow.start("norm", ins[3], middle_ref)
        flow.start("norm", ins[4], vec_ref)
        flow.start("norm", ins[0], grad_ref)
        flow.pack("out", packs[0], weights[0], w_out, 3 * TILE, TILE)

        flow.wait("low")
        for tile in range(4):
            if tile % 2 == 0:
                flow.wait(f"reduce{tile // 2}")
            product = lax.dot_general(low_ref[...], w_reduce[:, columns(tile)], NT, preferred_element_type=f32)
            if tile == 0:
                flow.wait("slope")
            for part in range(SMALL):
                at = block_at(place, part, 4 * BLOCK, tile * BLOCK)
                piece = product[:, part * BLOCK : (part + 1) * BLOCK] * slope_ref[:, at].astype(f32)
                hidden[:, at] = piece.astype(bf16)
                bias[:, at] = jnp.sum(piece, axis=0, keepdims=True)
        flow.start("hidden", hidden.at[:, columns(0, 2)], outs[0])
        flow.start("hidden", hidden.at[:, columns(2, 2)], outs[1])
        flow.start("bias", bias, outs[3])
        for tile in range(4):
            if tile % 2 == 0:
                flow.wait(f"expand{tile // 2}")
            product = lax.dot_general(
                hidden[:, columns(tile)], w_expand[:, columns(tile)], NT, preferred_element_type=f32
            )
            total[...] = product if tile == 0 else total[...] + product
        for part in range(SMALL):
            ordered[:, block_at(place, part)] = total[:, part * BLOCK : (part + 1) * BLOCK]
        flow.wait("norm")
        back, gain_grad, shift_grad, scale_grad = modulated_back(middle_ref[...], vec_ref, 3, ordered[...])
        upstream = grad_ref[...].astype(f32)
        middle_grad[...] = upstream + back
        middle_low[...] = middle_grad[...].astype(bf16)
        flow.start("middle", middle_low, outs[2])
        flow.start("middle", middle_grad, outs[4])
        flow.wait("out")
        product = lax.dot_general(middle_low[...], w_out[...], NT, preferred_element_type=f32).astype(bf16)
        for part in range(SMALL):
            mixture[:, block_at(place, part)] = product[:, part * BLOCK : (part + 1) * BLOCK]
        flow.start("mixture", mixture, outs[6])
        sums[0:1, :] = gain_grad
        sums[1:2, :] = shift_grad
        sums[2:3, :] = scale_grad
        sums[3:4, :] = jnp.sum(middle_grad[...], axis=0, keepdims=True)
        sums[4:5, :] = jnp.sum(upstream, axis=0, keepdims=True)
        sums[5:8, :] = jnp.zeros((3, width), f32)
        flow.start("sums", sums, outs[5])
        flow.drain()

    rows = SMALL * BLOCK
    return run_flow(
        body,
        [grad, low, slope, middle, vec],
        packs,
        [
            ((tokens, half), bf16),
            ((tokens, half), bf16),
            (grad.shape, bf16),
            ((1, hidden_width), f32),
            (grad.shape, f32),
            ((8, width), f32),
            (grad.shape, bf16),
        ],
        [
            (grad.shape, grad.dtype),
            (grad.shape, bf16),
            (slope.shape, bf16),
            (middle.shape, f32),
            (vec.shape, f32),
            ((rows, TILE), bf16),
            ((rows, hidden_width), bf16),
            ((rows, hidden_width), bf16),
            (slope.shape, bf16),
            ((1, hidden_width), f32),
            (grad.shape, f32),
            (grad.shape, bf16),
            ((8, width), f32),
            (grad.shape, bf16),
            (grad.shape, f32),
            (grad.shape, f32),
        ],
        5 + 5 * len(packs[0]) + 7,
        deps,
        12,
    )


def first_back(query_grad, key_parts, pack, stream, middle_grad, vec, deps=()):
    tokens, width = stream.shape
    shape = key_parts[0].shape

    def body(place, flow, ins, weights, outs, scratch):
        (lower, near_ref, leave_ref, far_ref, stream_ref, middle_ref, vec_ref, w_in) = scratch[:8]
        (key_ref, grad_ref, sums, total, ordered) = scratch[8:]
        flow.start("query", ins[0], lower.at[:, columns(0)])
        flow.pack("w0", pack, weights[0], w_in, 0, TILE)
        for source, target in zip(ins[1:4], (near_ref, leave_ref, far_ref)):
            flow.start("keys", source, target)
        flow.pack("w1", pack, weights[0], w_in, TILE, 2 * TILE)
        for source, target in zip(ins[4:7], (stream_ref, middle_ref, vec_ref)):
            flow.start("norm", source, target)
        flow.wait("query")
        flow.wait("w0")
        total[...] = lax.dot_general(lower[:, columns(0)], w_in[:, columns(0)], NT, preferred_element_type=f32)
        flow.wait("keys")
        key_ref[...] = (
            near_ref[...].astype(f32) + leave_ref[...].astype(f32) + far_ref[...].astype(f32)
        ).astype(bf16)
        flow.start("key", key_ref, outs[3])
        flow.wait("w1")
        total[...] += lax.dot_general(key_ref[...], w_in[:, columns(1, 2)], NT, preferred_element_type=f32)
        for part in range(SMALL):
            ordered[:, block_at(place, part)] = total[:, part * BLOCK : (part + 1) * BLOCK]
        flow.wait("norm")
        back, gain_grad, shift_grad, scale_grad = modulated_back(
            stream_ref[...].astype(f32), vec_ref, 0, ordered[...]
        )
        grad_ref[...] = middle_ref[...] + back
        lower[:, columns(1)] = grad_ref[...].astype(bf16)
        flow.start("lower", lower, outs[1])
        flow.start("grad", grad_ref, outs[0])
        sums[0:1, :] = gain_grad
        sums[1:2, :] = shift_grad
        sums[2:3, :] = scale_grad
        sums[3:8, :] = jnp.zeros((5, width), f32)
        flow.start("sums", sums, outs[2])
        flow.drain()

    rows = SMALL * BLOCK
    return run_flow(
        body,
        [query_grad, *key_parts, stream, middle_grad, vec],
        [pack],
        [(stream.shape, f32), ((tokens, 2 * TILE), bf16), ((8, width), f32), (shape, bf16)],
        [
            ((tokens, 2 * TILE), bf16),
            (shape, bf16),
            (shape, bf16),
            (shape, bf16),
            (stream.shape, stream.dtype),
            (stream.shape, f32),
            (vec.shape, f32),
            ((rows, 3 * TILE), bf16),
            (shape, bf16),
            (stream.shape, f32),
            ((8, width), f32),
            (stream.shape, f32),
            (stream.shape, f32),
        ],
        7 + 2 * len(pack) + 4,
        deps,
        6,
    )


ORDERS = ((6, 2, 4, 0), (6, 4, 2, 0))


class Group:
    def __init__(self, arrays, left_of, right_of):
        self.arrays, self.left_of, self.right_of = arrays, left_of, right_of

    def left(self, place, refs, tile):
        array, stride, offset = self.left_of[tile]
        return jnp.concatenate(
            [refs[array][:, block_at(place, mask, stride, offset)] for mask in ORDERS[tile // 2]], axis=1
        )

    def product(self, place, refs, tile):
        array, start = self.right_of[tile]
        return lax.dot_general(
            self.left(place, refs, tile), refs[array][:, start : start + TILE], TN, preferred_element_type=f32
        )


def reduce_group(kept, lower, block):
    return Group(
        [(lower, block * TILE, TILE), (kept, ACTIVE, 4 * TILE)],
        [(1, 4 * BLOCK, u * BLOCK) for u in range(4)],
        [(0, 0)] * 4,
    )


def expand_group(kept, back):
    return Group(
        [(kept, SECOND, TILE), (back[0], 0, 2 * TILE), (back[1], 0, 2 * TILE)],
        [(0, BLOCK, 0)] * 4,
        [(1, 0), (1, TILE), (2, 0), (2, TILE)],
    )


def attention_group(kept, back, lower, key_grad):
    return Group(
        [
            (kept, NORMED, TILE),
            (lower, 0, TILE),
            (key_grad, 0, 2 * TILE),
            (kept, MIXTURE, TILE),
            (back[2], 0, TILE),
        ],
        [(0, BLOCK, 0)] * 3 + [(3, BLOCK, 0)],
        [(1, 0), (2, 0), (2, TILE), (4, 0)],
    )


def wide(value):
    return value.astype(f32)


class Reduction:
    def __init__(self, group, stacked=False):
        self.group, self.stacked = group, stacked

    def scatter(self, *tokens):
        piece = after(self.piece, *tokens) if tokens else self.piece
        self.share = lax.psum_scatter(piece, "seq", scatter_dimension=0, tiled=True)


def advance(seconds=(), thirds=(), fourths=(), joint=(), deps=(), later=False):
    arrays, outputs, scratch, loads, works = [], [], [], [], []
    half = 2 * TILE
    quarter, eighth = (2 * BLOCK, half), (BLOCK, half)

    def bring(array, shape, source, target=lambda ref: ref, key=None):
        number = len(loads)
        slot = len(scratch) if shape is not None else len(scratch) - 1
        if shape is not None:
            scratch.append((shape, array.dtype))
        loads.append((len(arrays), slot, source, target, number if key is None else key))
        arrays.append(array)
        return slot, number

    def make(shape):
        outputs.append((shape, bf16))
        scratch.append((shape, bf16))
        return len(outputs) - 1, len(scratch) - 1

    for one in seconds:
        group, slots, keys = one.group, [], []
        for pair, first, width in group.arrays:
            tokens = pair[0].shape[0]
            for side, array in enumerate(pair):
                slot, key = bring(
                    array,
                    (2 * tokens, width) if side == 0 else None,
                    lambda ref, first=first, width=width: ref.at[:, pl.ds(first, width)],
                    lambda ref, side=side, tokens=tokens: ref.at[pl.ds(side * tokens, tokens), :],
                )
                keys.append(key)
            slots.append(slot)
        made = [make(quarter), make(quarter), make((2,) + quarter)]

        def product(place, flow, held, outs, group=group, slots=slots, keys=keys, made=made):
            refs = [held[slot] for slot in slots]
            waited = 0
            stay = made[2]
            for tile in range(4):
                needed = 2 * (max(group.left_of[tile][0], group.right_of[tile][0]) + 1)
                while waited < needed:
                    flow.wait(keys[waited])
                    waited += 1
                total = group.product(place, refs, tile)
                leave = made[tile // 2]
                held[leave[1]][:, columns(tile % 2)] = total[: 2 * BLOCK].astype(bf16)
                held[stay[1]][tile // 2, :, columns(tile % 2)] = total[2 * BLOCK :].astype(bf16)
                if tile % 2:
                    flow.start("out", held[leave[1]], outs[leave[0]])
                    flow.start("out", held[stay[1]].at[tile // 2], outs[stay[0]].at[tile // 2])

        works.append(product)
    for one in thirds:
        loaded = [
            bring(one.staying, (2,) + quarter, lambda ref: ref),
            bring(one.from_x, quarter, lambda ref: ref),
            bring(one.from_y, quarter, lambda ref: ref),
        ]
        made = [make(eighth), make(eighth), make((2,) + eighth)]

        def add(place, flow, held, outs, loaded=loaded, made=made):
            flow.wait(loaded[0][1])
            for number in range(2):
                flow.wait(loaded[1 + number][1])
                total = (wide(held[loaded[0][0]][number]) + wide(held[loaded[1 + number][0]][...])).astype(bf16)
                held[made[number][1]][...] = total[:BLOCK]
                held[made[2][1]][number] = total[BLOCK:]
                flow.start("out", held[made[number][1]], outs[made[number][0]])
                flow.start("out", held[made[2][1]].at[number], outs[made[2][0]].at[number])

        works.append(add)
    sums = [[one] for one in fourths] + ([list(joint)] if joint else [])
    for members in sums:
        alone = len(members) == 1
        stacked = alone and members[0].stacked
        loaded = [
            [
                bring(one.kept, (2,) + eighth, lambda ref: ref),
                bring(one.second_y, eighth, lambda ref: ref),
                bring(one.second_x, eighth, lambda ref: ref),
            ]
            for one in members
        ]
        made = make((4 * BLOCK, TILE) if stacked else (len(members) * BLOCK, 4 * TILE))

        def finish(place, flow, held, outs, loaded=loaded, made=made, stacked=stacked, alone=alone):
            result, share = held[made[1]], BLOCK // 4
            for number, (kept, *arrived) in enumerate(loaded):
                flow.wait(kept[1])
                for side in range(2):
                    flow.wait(arrived[side][1])
                    total = (wide(held[kept[0]][side]) + wide(held[arrived[side][0]][...])).astype(bf16)
                    if stacked:
                        for tile in range(2):
                            at = (2 * side + tile) * BLOCK
                            result[at : at + BLOCK, :] = total[:, tile * TILE : (tile + 1) * TILE]
                    elif alone:
                        result[:, columns(2 * side, 2)] = total
                    else:
                        for plane in range(4):
                            start = (plane * len(loaded) + number) * share
                            result[start : start + share, columns(2 * side, 2)] = total[
                                plane * share : (plane + 1) * share
                            ]
            flow.start("out", result, outs[made[0]])

        works.append(finish)

    def body(place, flow, ins, _, outs, held):
        for number, slot, source, target, key in loads:
            flow.start(key, source(ins[number]), target(held[slot]))
        for work in works:
            work(place, flow, held, outs)
        flow.drain()

    results = list(run_flow(body, arrays, [], outputs, scratch, len(loads) + 2 * len(outputs) + 2, deps, 7 if seconds else 4))
    token = results[-1] if joint and len(works) == 1 else results[0]
    for one in seconds:
        along_x, along_y, one.staying = results[:3]
        results = results[3:]
        one.from_x, one.from_y = swap(along_x, 2), swap(along_y, 4)
    for one in thirds:
        along_y, along_x, one.kept = results[:3]
        results = results[3:]
        one.second_y, one.second_x = swap(along_y, 4), swap(along_x, 2)
    for one in fourths:
        one.piece = results[0]
        results = results[1:]
        if not later:
            one.scatter()
    if joint:
        both = lax.psum_scatter(results[0], "seq", scatter_dimension=0, tiled=True)
        share = BLOCK // 4
        for number, one in enumerate(joint):
            one.share = both[number * share : (number + 1) * share]
    return token


HALF = BLOCK // 2
EXTRA = 32


def raw_inputs(kind, layer, arrays):
    if kind == "attention":
        return [
            (arrays[0], pl.BlockSpec((1,) + arrays[0].shape[1:], lambda i, s: (layer, 0, 0))),
            (arrays[1], pl.BlockSpec((1,) + arrays[1].shape[1:], lambda i, s: (layer, 0, 0))),
        ]
    if kind == "expand":
        return [(arrays[0], pl.BlockSpec((1, BLOCK, TILE), lambda i, s: (layer, 0, i)))]
    return [(arrays[0], pl.BlockSpec((1, BLOCK, TILE), lambda i, s: (layer, i, 0)))]


def raw_tile(kind, ins, targets):
    if kind != "attention":
        for target in targets:
            target[:BLOCK, :] = ins[0][0]
        return
    pairs = TILE // (2 * BLOCK)
    for tile in range(4):

        @pl.when(pl.program_id(0) == tile)
        def _(tile=tile):
            for target in targets:
                if tile == 0:
                    target[:BLOCK, :] = ins[0][0, :, :TILE]
                elif tile == 3:
                    target[:BLOCK, :] = ins[1][0]
                else:
                    for pair in range(pairs):
                        start = (pairs * (tile - 1) + pair) * BLOCK
                        at = pair * 2 * BLOCK
                        target[:BLOCK, at : at + BLOCK] = ins[0][0, :, TILE + start : TILE + start + BLOCK]
                        target[:BLOCK, at + BLOCK : at + 2 * BLOCK] = ins[0][
                            0, :, 2 * TILE + start : 2 * TILE + start + BLOCK
                        ]


def column_spec(rows, row_block=0):
    return pl.BlockSpec((rows, TILE), lambda i, s: (row_block, i))


def first_pack(raw, time_table, members, noise_buckets):
    layers = time_table.shape[0]
    buckets = jnp.broadcast_to(noise_buckets.astype(bf16), (layers, BLOCK))
    chunks = [(2 + 1 + index, layer, 0) for index in range(6) for layer in range(layers)]
    bias_chunks = members[6].shape[1] // BLOCK
    chunks += [(2 + 1 + 6, layer, part) for layer in range(layers) for part in range(bias_chunks)]
    chunks.append((2 + 1 + 7, 0, 0))
    per_tile = TILE // BLOCK

    def body(place, ins, outs, _):
        raw_tile("attention", ins[:2], outs)
        for tile in range(4):

            @pl.when(pl.program_id(0) == tile)
            def _(tile=tile):
                start = (tile % 2) * 16
                outs[0][BLOCK : BLOCK + 16, :] = ins[2][tile // 2, start : start + 16, :]
                for slot in range(per_tile):
                    index = tile * per_tile + slot
                    at = slot * BLOCK
                    row = jnp.zeros((1, BLOCK), bf16)
                    if index < len(chunks):
                        array, layer, part = chunks[index]
                        row = ins[array][layer : layer + 1, part * BLOCK : (part + 1) * BLOCK]
                    outs[0][BLOCK + 16 :, at : at + BLOCK] = jnp.broadcast_to(row.astype(f32), (16, BLOCK)).astype(bf16)

    return run(
        body,
        4,
        raw_inputs("attention", 0, raw)
        + [(time_table, None)]
        + [(member, None) for member in members]
        + [(buckets, None)],
        [((BLOCK + EXTRA, 4 * TILE), bf16, column_spec(BLOCK + EXTRA))],
    )[0]


def other_packs(kinds, raws, deps=()):
    inputs, counts = [], []
    for (kind, layer), raw in zip(kinds, raws):
        inputs += raw_inputs(kind, layer, raw)
        counts.append(len(raw))

    def body(place, ins, outs, _):
        at = 0
        for position, ((kind, _), taken) in enumerate(zip(kinds, counts)):
            raw_tile(kind, ins[at : at + taken], [outs[0].at[position * BLOCK : (position + 1) * BLOCK]])
            at += taken

    rows = len(kinds) * BLOCK
    return run(body, 4, inputs, [((rows, 4 * TILE), bf16, column_spec(rows))], deps=deps)[0]


def own_rows(rest, position, rows, deps=()):
    def body(place, ins, outs, _):
        outs[0][...] = ins[0][...]
        outs[1][...] = ins[0][...]

    out = ((rows, 4 * TILE), bf16, column_spec(BLOCK))
    return run(body, 4, [(rest, column_spec(BLOCK, position))], [out, out], deps=deps)


def diagonal_rows(x, y, buffers, deps=()):
    def body(place, ins, outs, _):
        outs[0][...] = ins[1][...]
        outs[1][...] = ins[0][...]

    rows, block = (buffers[0].shape[0], BLOCK // HALF) if buffers else (HALF, 0)

    def spec(at):
        return pl.BlockSpec((HALF, 4 * TILE), lambda i, s: (at, 0))

    out = ((rows, 4 * TILE), bf16, spec(block))
    return run(body, 1, [(x, spec(1)), (y, spec(0))], [out, out], deps=deps, aliases=buffers)


def first_step(rest, x, y, deps=()):
    half = EXTRA // 2

    def body(place, ins, outs, _):
        from_x, from_y, own = ins
        for out, source, at in ((outs[0], from_y, 0), (outs[1], from_x, 1)):
            out[:BLOCK, :] = own[...]
            out[BLOCK : BLOCK + HALF, :] = source[at * HALF : (at + 1) * HALF, :]
            out[BLOCK + HALF :, :] = source[BLOCK + at * half : BLOCK + (at + 1) * half, :]

    rows = BLOCK + HALF + half
    out = ((rows, 4 * TILE), bf16, column_spec(rows))
    whole = column_spec(x.shape[0])
    return run(body, 4, [(x, whole), (y, whole), (rest, column_spec(BLOCK))], [out, out], deps=deps)


class Gather:
    def __init__(self, kinds, raws, time_table, members, noise_buckets):
        self.count = len(kinds)
        self.first = first_pack(raws[0], time_table, members, noise_buckets)
        self.xs, self.ys = [swap(self.first, 2)], [swap(self.first, 4)]
        self.core_first = swap(self.first, 1)
        self.kinds, self.raws = kinds, raws
        self.core_xs, self.core_ys = [], []

    def others(self, deps):
        self.rest = other_packs(self.kinds[1:], self.raws[1:], deps)
        self.ready = tuple(own_rows(self.rest, 1, BLOCK + HALF))
        return self.ready[0]

    def prepare(self, deps=()):
        step = len(self.xs)
        self.ready = ()
        if step < self.count:
            self.ready = tuple(own_rows(self.rest, step - 1, BLOCK + HALF, deps))
            return self.ready[0]
        return deps[0]

    def step(self, deps=(), token=None):
        step = len(self.xs)
        if step == 2:
            deps = (self.core_rest,) + tuple(deps)
        if step > 1:
            deps = (self.core_xs[-1], self.core_ys[-1]) + tuple(deps)
            on_x, on_y = diagonal_rows(self.xs[-1], self.ys[-1], self.ready, deps)
        else:
            on_x, on_y = first_step(self.rest, self.xs[-1], self.ys[-1], deps)
            self.core_rest = swap(after(self.rest, on_x), 1)
        self.cross(on_x if token is None else token)
        self.xs.append(swap(on_x, 2))
        self.ys.append(swap(on_y, 4))
        return on_x

    def cross(self, token):
        self.core_xs.append(swap(after(self.xs[-1], token), 1))
        self.core_ys.append(swap(after(self.ys[-1], token), 1))

    def pack(self, k):
        row = 2 if k + 1 < self.count else 0
        own = [(self.first, 0, BLOCK), (self.core_first, 0, BLOCK)] if k == 0 else [(self.rest, k - 1, BLOCK), (self.core_rest, k - 1, BLOCK)]
        sides = (self.xs, self.core_xs, self.ys, self.core_ys)
        return (
            own
            + [(side[k], 0, BLOCK) for side in sides]
            + [(sides[i][k + 1], row, HALF) for i in (0, 2, 1, 3)]
        )

    def extras(self):
        whole = [(self.first, BLOCK, EXTRA), (self.core_first, BLOCK, EXTRA)]
        whole += [(side[0], BLOCK, EXTRA) for side in (self.xs, self.core_xs, self.ys, self.core_ys)]
        at, rows = BLOCK + HALF, EXTRA // 2
        parts = [
            [(self.xs[1], at, rows), (self.ys[1], at, rows)],
            [(self.core_xs[1], at, rows), (self.core_ys[1], at, rows)],
        ]
        return [[piece] for piece in whole] + parts


def vectors_of(extras, members, layers, table_rows, width):
    share = members[6].shape[1]
    bias_at, bucket_at = 6 * layers * BLOCK, 6 * layers * BLOCK + layers * share
    pieces = [piece for parts in extras for piece in parts]
    tables, rows_at, at = [], [], 0
    for parts in extras:
        tables.append(at)
        rows_at.append((at + len(parts) - 1, 0 if len(parts) == 2 else EXTRA // 2))
        at += len(parts)

    def body(place, ins, outs, _):
        me = place[0]
        row = [ins[at][start : start + 16, :].astype(f32)[0:1, :] for at, start in rows_at]
        mine = (me // 2) * 2 + place[1] // 2 == me
        bucket = jnp.where(mine, row[0][:, bucket_at : bucket_at + 1], row[1][:, bucket_at : bucket_at + 1])
        for layer in range(layers):
            scaling = jnp.ones((1, width), f32)
            for part in range(SMALL):
                owner = me ^ part
                for member in range(6):
                    start = (member * layers + layer) * BLOCK
                    outs[2 * layer][member : member + 1, block_at(place, part)] = row[part][:, start : start + BLOCK]
                start = bias_at + layer * share
                outs[2 * layer + 1][:, pl.ds(pl.multiple_of(owner * share, BLOCK), share)] = row[part][
                    :, start : start + share
                ]
                for half in range(2):
                    block = ins[tables[part]][0:16, (2 * layer + half) * TILE : (2 * layer + half + 1) * TILE].astype(f32)
                    place_of = lax.broadcasted_iota(jnp.int32, block.shape, 0) + (owner * table_rows + half * 16)
                    hit = place_of.astype(f32) == bucket
                    scaling += jnp.sum(jnp.where(hit, block, 0.0), axis=0, keepdims=True)
            outs[2 * layer][6:7, :] = scaling
            outs[2 * layer][7:8, :] = jnp.zeros((1, width), f32)
        for part in range(SMALL):
            outs[2 * layers][pl.ds(me ^ part, 1), :] = row[part][:, bucket_at : bucket_at + BLOCK]

    result = run(
        body,
        1,
        [
            (array, pl.BlockSpec((rows, 4 * TILE), lambda i, s, r=start // rows: (r, 0)))
            for array, start, rows in pieces
        ],
        [
            item
            for _ in range(layers)
            for item in (((8, width), f32, None), ((1, SMALL * share), f32, None))
        ]
        + [((SMALL, BLOCK), f32, None)],
    )
    pairs = [(result[2 * layer], result[2 * layer + 1]) for layer in range(layers)]
    return pairs, result[2 * layers][:, 0].astype(jnp.int32)


def small_and_changes(sums):
    columns = []
    for early, late, hidden_sum in sums:
        for member in (early[0], early[1], late[3], late[0], late[1], late[4], hidden_sum[0]):
            columns.append(member.reshape(SMALL * 4, -1))
    small = jnp.concatenate(columns, axis=1)
    changes = jnp.concatenate([early[2] + late[2] for early, late, _ in sums])
    return small.reshape((2, 2, 2, 2, 2, -1)), changes[None]


def cross(small, changes, axis, mine, move, add, *tokens):
    leaving = lax.dynamic_index_in_dim(small, 1 - mine, axis, keepdims=False)
    staying = lax.dynamic_index_in_dim(small, mine, axis, keepdims=False)
    moved = move(jnp.concatenate([leaving.reshape(-1), changes.reshape(-1)]))
    if tokens:
        moved = after(moved, *tokens)
    small = staying + moved[: leaving.size].reshape(leaving.shape)
    arrived = moved[leaving.size :].reshape(changes.shape)
    return small, changes + arrived if add else jnp.concatenate([changes, arrived], axis=0)


def relay(array, back):
    moves = layout_moves(back)
    moved = lax.ppermute(array, ("dp", "seq"), [(a, b) for a, b in moves if a != b])
    core, plane = lax.axis_index("dp") % 2, lax.axis_index("seq")
    return moved, lambda moved: jnp.where(plane == 3 * core, array, moved)


def fast_device(
    inputs,
    noise_buckets,
    first_gain,
    first_shift,
    attention_in,
    attention_out,
    attention_bias,
    second_gain,
    second_shift,
    expand_weight,
    expand_bias,
    reduce_weight,
    reduce_bias,
    time_table,
    cotangent,
):
    layers, width = first_gain.shape[0], inputs.shape[-1]
    count, planes = lax.axis_size("dp"), lax.axis_size("seq")
    me, plane = lax.axis_index("dp"), lax.axis_index("seq")
    sequence = (me // 2) * 2 + plane // 2

    kinds = [(kind, layer) for layer in range(layers) for kind in ("attention", "expand", "reduce")]
    raw_of = {"attention": (attention_in, attention_out), "expand": (expand_weight,), "reduce": (reduce_weight,)}
    members = (first_gain, first_shift, attention_bias, second_gain, second_shift, reduce_bias, expand_bias)
    gather = Gather(kinds, [raw_of[kind] for kind, _ in kinds], time_table, members, noise_buckets)
    moved, finish = relay(inputs[0], False)
    moved = finish(moved)
    token = gather.others((gather.first,))
    token = gather.step((moved, token))
    grad_low, finish = relay(after(cotangent[0], token), False)
    grad_low = finish(grad_low)
    gather.step((grad_low,))
    vectors, buckets = vectors_of(gather.extras(), members, layers, time_table.shape[1], width)

    saved = []
    stream = moved
    normed = first_norm(stream, vectors[0][0])
    for layer in range(layers):
        vec, bias = vectors[layer]
        attention_pack = gather.pack(3 * layer)
        own_keys = project(normed, attention_pack, 1, 2, (token,) if layer else ())
        chunks = spread_keys(own_keys)
        queries = project(normed, attention_pack, 0, 1, (own_keys,))
        token = gather.step((gather.prepare((queries,)), queries), queries)
        if layer == 0:
            token = gather.prepare((token,))
        mixture, tops = attend_fast(queries, chunks, (token,))
        if layer == 0:
            token = gather.step((mixture,), mixture)
            token = gather.prepare((token,))
        else:
            gather.cross(mixture)
            token = mixture
        packs = (attention_pack, gather.pack(3 * layer + 1), gather.pack(3 * layer + 2))
        next_vec = vectors[layer + 1][0] if layer + 1 < layers else None
        middle, own_kept, slope, result, following = feed_forward(
            normed, mixture, packs, stream, vec, bias, next_vec, (token,)
        )
        if layer == 0:
            token = gather.step((following,), following)
        saved.append([stream, own_kept, queries, chunks, tops, middle, slope, packs])
        stream, normed = result, following

    grad = grad_low
    lower, block = (grad_low, swap(after(grad_low, following), 1)), 0
    sums = [None] * layers
    shares = {}
    for entry in reversed(saved):
        entry[1] = (entry[1], swap(after(entry[1], following), 1))
    above = None
    for layer in reversed(range(layers)):
        vec, bias = vectors[layer]
        stream, kept, queries, chunks, tops, middle, slope, packs = saved[layer]
        of_reduce = Reduction(reduce_group(kept, lower, block), True)
        deps = ()
        if above is not None:
            upper_reduce, upper_expand, of_attention = above
            deps = (advance([of_attention], deps=(token,)),)
        *own_back, expand_bias_grad, middle_grad, late_sums, mixture_grad = feed_forward_back(
            grad, (lower[0], block), slope, middle, packs, vec, deps
        )
        if above is None:
            back = [(own, swap(own, 1)) for own in own_back]
            token = advance([of_reduce], deps=(own_back[0], saved[0][1][1]))
            deps = (token,) + tuple(other for _, other in back)
        else:
            deps = (upper_expand.second_x, upper_expand.second_y)
        query_grad, near, near_leave, far, far_leave = attend_fast_back(
            queries, chunks, kept[0], mixture_grad, tops, deps
        )
        far_leave, near_leave = swap(far_leave, 1), swap(near_leave, 1)
        token = query_grad
        if above is None:
            of_expand = Reduction(expand_group(kept, back))
            token = advance([of_expand], deps=(token,))
            token = advance(thirds=[of_reduce], deps=(token,))
        else:
            token = advance(thirds=[of_attention], deps=(token, upper_reduce.share, moved_result))
            token = advance([of_reduce], deps=(token,))
        far, near_leave = after(far, token, near_leave), after(near_leave, token)
        far = (wide(far) + wide(far_leave)).astype(bf16)
        far = (far, swap_seq(far, 1))
        token = far[0]
        if above is not None:
            back = [(own, swap(after(own, token), 1)) for own in own_back[:2]]
            of_expand = Reduction(expand_group(kept, back))
            deps = (back[0][1], back[1][1], of_attention.second_x, of_attention.second_y)
            token = advance([of_expand], deps=(token,) + deps)
        deps = (token, of_expand.from_x, of_expand.from_y) if above is None else (token,)
        grad, own_lower, early_sums, key_grad = first_back(
            query_grad, (near, near_leave, far[1]), packs[0], stream, middle_grad, vec, deps
        )
        lower, block = (own_lower, swap(own_lower, 1)), 1
        key_grad = (key_grad, swap(key_grad, 1))
        if above is None:
            token = advance(thirds=[of_expand], fourths=[of_reduce], deps=(own_lower,))
            moved_result, finish = relay(after(result, token), True)
            outputs = finish(lax.optimization_barrier(moved_result)).astype(bf16)
        else:
            back.append((own_back[2], swap(after(own_back[2], own_lower), 1)))
            token = own_lower
            shares[("attention", layer + 1)] = of_attention
            shares[("expand", layer + 1)] = upper_expand
            upper_attention = of_attention
        of_attention = Reduction(attention_group(kept, back, lower, key_grad))
        shares[("reduce", layer)] = of_reduce
        above = (of_reduce, of_expand, of_attention)
        sums[layer] = (early_sums, late_sums, expand_bias_grad)

    of_reduce, of_expand, of_last = above
    token = advance(thirds=[of_reduce], joint=(upper_expand, upper_attention), deps=(token,))
    token = advance([of_last], deps=(token,))
    token = advance(fourths=[of_reduce], deps=(token,))
    token = advance(thirds=[of_expand], deps=(token,))
    token = advance(thirds=[of_last], deps=(token, upper_expand.share))
    token = advance(fourths=[of_expand], deps=(token,))
    small, changes = small_and_changes(sums)
    small, changes = after(small, token), after(changes, token)
    small, changes = cross(small, changes, 4, plane % 2, lambda a: swap_seq(a, 1), True)
    small, changes = cross(small, changes, 3, plane // 2, lambda a: swap_seq(a, 2), False)
    token = advance(fourths=[of_last], deps=(token, small, changes))
    input_grad, finish = relay(after(own_lower[:, TILE:], token), True)
    input_grad = finish(input_grad).astype(f32)
    shares[("attention", 0)] = of_last
    shares[("expand", 0)] = of_expand
    shares = {name: reduction.share.astype(f32) for name, reduction in shares.items()}

    small, changes = after(small, token), after(changes, token)
    small, changes = cross(small, changes, 2, me % 2, lambda a: swap(a, 1), True)
    small, changes = cross(small, changes, 1, (me // 2) % 2, lambda a: swap(a, 2), False)
    small, changes = cross(small, changes, 0, me // 4, lambda a: swap(a, 4), False)
    row = small.reshape(-1)
    small_out, start = [[] for _ in range(7)], 0
    for layer in range(layers):
        for member in range(7):
            size = (width if member < 6 else 4 * width) // (count * planes)
            small_out[member].append(row[start : start + size])
            start += size
    small_out = [jnp.stack(member) for member in small_out]
    entries = jnp.arange(count)
    owners = 2 * ((me // 2) ^ (entries // 2)) + ((plane // 2) ^ (entries % 2))
    source_buckets = jnp.sum(jnp.where(owners[:, None] == entries[None, :], buckets[None, :], 0), axis=1)
    table_grad = chosen_rows(changes, source_buckets, layers, width)

    ins, outs, expands, reduces = [], [], [], []
    for layer in range(layers):
        share = shares[("attention", layer)]
        pairs = share[:, width : 3 * width].reshape(share.shape[0], width // BLOCK, 2, BLOCK)
        ins.append(
            jnp.concatenate(
                [share[:, :width], pairs[:, :, 0].reshape(-1, width), pairs[:, :, 1].reshape(-1, width)], axis=1
            )
        )
        outs.append(share[:, 3 * width :])
        expands.append(shares[("expand", layer)])
        reduces.append(shares[("reduce", layer)])
    return (
        outputs[None],
        input_grad[None],
        small_out[0],
        small_out[1],
        jnp.stack(ins),
        jnp.stack(outs),
        small_out[2],
        small_out[3],
        small_out[4],
        jnp.stack(expands),
        small_out[6],
        jnp.stack(reduces),
        small_out[5],
        table_grad,
    )


def on_device(
    inputs,
    noise_buckets,
    first_gain,
    first_shift,
    attention_in,
    attention_out,
    attention_bias,
    second_gain,
    second_shift,
    expand_weight,
    expand_bias,
    reduce_weight,
    reduce_bias,
    time_table,
    cotangent,
):
    layers = first_gain.shape[0]
    count, planes = lax.axis_size("dp"), lax.axis_size("seq")
    me, plane = lax.axis_index("dp"), lax.axis_index("seq")
    model_width = inputs.shape[-1]
    table_rows = time_table.shape[1]

    stream = lax.ppermute(inputs[0], ("dp", "seq"), layout_moves(False)).astype(f32)

    sequence = (me // 2) * 2 + plane // 2
    packs = []
    for layer in range(layers):
        rows = [
            time_table[layer],
            pack_small(
                [
                    member[layer]
                    for member in (
                        first_gain,
                        first_shift,
                        attention_bias,
                        second_gain,
                        second_shift,
                        reduce_bias,
                        expand_bias,
                    )
                ],
                WIDE,
            ),
            jnp.broadcast_to(noise_buckets.astype(bf16)[:, None], (1, model_width)),
        ]
        packs.append(jnp.concatenate(rows, axis=0))

    def unpack(pack):
        stacked, sources, _ = gather_small(pack, ("dp",))
        slot = me ^ jnp.arange(count) if count == SMALL else jnp.arange(count)
        per_pack = stacked.shape[1]
        flat = stacked.reshape(count * per_pack, model_width)

        def place(index):
            return (me ^ index) if count == SMALL else index

        buckets = jnp.stack(
            [lax.dynamic_index_in_dim(flat, place(index) * per_pack + per_pack - 1, 0, False)[0] for index in range(count)]
        ).astype(jnp.int32)
        bucket = lax.dynamic_index_in_dim(buckets, sequence, 0, False)
        row = place(bucket // table_rows) * per_pack + bucket % table_rows
        scaling = lax.dynamic_slice_in_dim(flat, row, 1, 0).astype(f32)
        vectors = jnp.stack(
            [
                lax.dynamic_slice_in_dim(
                    flat, place(index) * per_pack + table_rows, per_pack - 1 - table_rows, 0
                ).reshape(-1)
                for index in range(count)
            ]
        ).astype(f32)
        share = model_width // count
        members = [vectors[:, i * share : (i + 1) * share].reshape(1, -1) for i in range(6)]
        members.append(vectors[:, 6 * share : 6 * share + expand_bias.shape[1]].reshape(1, -1))
        return tuple(members) + (scaling,), buckets

    keys_at = model_width
    shards = []
    for layer in range(layers):
        shards += [
            attention_in[layer][:, keys_at:],
            attention_in[layer][:, :keys_at],
            attention_out[layer],
            expand_weight[layer],
            reduce_weight[layer],
        ]
    gathered = []
    for position, shard in enumerate(shards):
        if count == SMALL and position >= 2:
            shard = after(shard, gathered[position - 2][2], gathered[position - 2][4])
        gathered.append(gather_rows(shard, position % 2))

    all_vectors, buckets = [], None
    for layer in range(layers):
        vectors, buckets = unpack(packs[layer])
        all_vectors.append(vectors)

    saved, all_weights = [], []
    for layer in range(layers):
        w_keys, w_query, w_out, w_expand, w_reduce = gathered[5 * layer : 5 * layer + 5]
        weights = (w_query, w_keys, w_out, w_expand, w_reduce)
        all_weights.append(weights)
        stream, kept = layer_forward(stream, weights, all_vectors[layer])
        saved.append(kept)
    back_moves = layout_moves(True)
    outputs = lax.ppermute(stream.astype(bf16), ("dp", "seq"), back_moves)[None]

    grad_flow = lax.ppermute(cotangent[0], ("dp", "seq"), layout_moves(False)).astype(f32)
    dense, small, modulation = [None] * layers, [None] * layers, [None] * layers
    for layer in reversed(range(layers)):
        grad_flow, dense[layer], small[layer], modulation[layer] = layer_backward(
            saved[layer], all_weights[layer], all_vectors[layer], grad_flow
        )
    input_grad = lax.ppermute(grad_flow, ("dp", "seq"), back_moves)[None]

    devices = count * planes
    packed = jnp.concatenate(
        [member.reshape(devices, -1) for layer in range(layers) for member in small[layer]], axis=1
    )
    row = scatter_small(packed)
    small_out, start = [[] for _ in range(7)], 0
    for layer in range(layers):
        for member in range(7):
            width = small[layer][member].size // devices
            small_out[member].append(row[start : start + width])
            start += width
    small_out = [jnp.stack(member) for member in small_out]

    changes, from_dp, from_seq = gather_small(jnp.concatenate(modulation), ("dp", "seq"))
    table_grad = table_rows_of(changes, from_dp, from_seq, buckets, layers, model_width)

    dense_out = [jnp.stack([dense[layer][member] for layer in range(layers)]) for member in range(4)]
    return (
        outputs,
        input_grad,
        small_out[0],
        small_out[1],
        dense_out[0],
        dense_out[1],
        small_out[2],
        small_out[3],
        small_out[4],
        dense_out[2],
        small_out[6],
        dense_out[3],
        small_out[5],
        table_grad,
    )


def solution(mesh):
    eight_way = mesh.shape["dp"] == SMALL and mesh.shape["seq"] == 4
    return jax.shard_map(
        fast_device if eight_way else on_device,
        mesh=mesh,
        in_specs=(
            P("dp", "seq", None),
            P("dp"),
            P(None, "dp"),
            P(None, "dp"),
            P(None, "dp", None),
            P(None, "dp", None),
            P(None, "dp"),
            P(None, "dp"),
            P(None, "dp"),
            P(None, "dp", None),
            P(None, "dp"),
            P(None, "dp", None),
            P(None, "dp"),
            P(None, "dp", None),
            P("dp", "seq", None),
        ),
        out_specs=(
            P("dp", "seq", None),
            P("dp", "seq", None),
            P(None, ("dp", "seq")),
            P(None, ("dp", "seq")),
            P(None, ("dp", "seq"), None),
            P(None, ("dp", "seq"), None),
            P(None, ("dp", "seq")),
            P(None, ("dp", "seq")),
            P(None, ("dp", "seq")),
            P(None, ("dp", "seq"), None),
            P(None, ("dp", "seq")),
            P(None, ("dp", "seq"), None),
            P(None, ("dp", "seq")),
            P(None, ("dp", "seq"), None),
        ),
        check_vma=False,
    )
```
